32 devices in a mesh: groups: 2 (over x), seq: 8 (over z, y), head: 2 (over core).
Axes of the slice: x: 2, y: 2, z: 4, core: 2. Of those that a mesh axis runs over, the one named last changes fastest.
Arguments:
- queries: bfloat16 [512, 4096], P(('groups', 'seq'), 'head'), parts along dimension 0, may hold values from -24 to 24
- vision: bfloat16 [4096, 7680], P(('groups', 'seq')), parts along dimension 0, may hold values from -6 to 6
- key_matrix: bfloat16 [7680, 512], P('seq', 'head'), may hold values from -0.0625 to 0.0625
- value_matrix: bfloat16 [7680, 512], P('seq', 'head'), may hold values from -0.0625 to 0.0625
- out_weight: bfloat16 [4096, 8192], P('head', 'seq'), may hold values from -0.09375 to 0.09375
- residual: bfloat16 [512, 8192], P(('groups', 'head'), 'seq'), parts along dimension 0, may hold values from -4 to 4
- query_norm_gain: float32 [128], replicated, may hold values from 1 to 12
- key_norm_gain: float32 [128], replicated, may hold values from 1 to 12
- attn_gate: float32 [1], replicated, may hold values from 0.5 to 2
Outputs:
- mixed: bfloat16 [512, 8192], P(('groups', 'head'), 'seq'), parts along dimension 0
The draws below stay inside these ranges and needn't reach their ends.
There are 2 independent parts, one for each index of `groups`. The reference program is written for one: setup_inputs(seed, part) draws one part's arguments, and reference() takes and returns one part's arrays. A program takes and returns all parts, laid end to end along the dimension named above; an argument that names none is the same for every part. Nothing has to cross between parts.
All inputs are finite; a program needn't handle non-finite values.
Results may differ from the reference program's by a relative error of at most 0.015.
The reference program's roundings to bfloat16 on the way count: a program that leaves them out, or rounds other values in their place, can miss the bound.
Values may be sent and summed in bfloat16 or wider, within the bound.
No kernel may reach another device: no remote copies, remote signals or barrier semaphores. Data moves between devices by JAX's collectives and lax.ppermute only.
A program may use at most 64 MiB of HBM per device.

```python
import math
import jax
import jax.numpy as jnp
from jax import lax

D = 8192
VISION_WIDTH = 7680
HEAD_SIZE = 128
QUERY_HEADS = 32
KEY_VALUE_HEADS = 4
TEXT_TOKENS = 256
VISION_TOKENS = 2048


def draw_queries(key, part):
    base = jax.random.normal(key, (TEXT_TOKENS, QUERY_HEADS * HEAD_SIZE), jnp.float32)
    return jnp.clip(base, -6.0, 6.0).astype(jnp.bfloat16)


def gain_values(key, salt):
    base = jnp.exp(jax.random.uniform(jax.random.fold_in(key, salt), (HEAD_SIZE,), jnp.float32, 0.0, math.log(3.0)))
    return base


def draw_query_norm_gain(key, part):
    return gain_values(key, 21)


def draw_key_norm_gain(key, part):
    return gain_values(key, 37)


def steps_of(stream_key, dims, cuts, low, largest):
    level, own = 1.0, jax.random.fold_in(stream_key, 6)
    for dim, blocks in cuts:
        draws = jnp.exp(jax.random.uniform(jax.random.fold_in(own, dim), (blocks,), jnp.float32, low / len(cuts), largest / len(cuts)))
        level = level * jnp.repeat(draws, dims[dim] // blocks).reshape([-1 if axis == dim else 1 for axis in range(len(dims))])
    return level


def noise(rng, extent, deviation, most, shards=(), dtype=jnp.bfloat16):
    loudness = steps_of(rng, extent, shards, -0.22, 0.18) if shards else 1.0
    result = jax.random.normal(rng, extent, jnp.float32) * deviation * loudness
    return jnp.minimum(jnp.maximum(result, -most), most).astype(dtype)


def setup_inputs(seed: int = 0, part: int = 0) -> dict:
    key_list = jax.random.split(jax.random.key(seed), 10)
    own_keys = jax.random.split(jax.random.fold_in(key_list[9], part), 10)
    return {
        "queries": draw_queries(jax.random.fold_in(jax.random.fold_in(key_list[9], part), 71), part),
        "vision": noise(own_keys[1], (VISION_TOKENS, VISION_WIDTH), 1.0, 6.0, ((0, 8),)),
        "key_matrix": noise(key_list[2], (VISION_WIDTH, KEY_VALUE_HEADS * HEAD_SIZE), VISION_WIDTH ** -0.5, 0.0625, ((0, 8), (1, 2))),
        "value_matrix": noise(key_list[3], (VISION_WIDTH, KEY_VALUE_HEADS * HEAD_SIZE), VISION_WIDTH ** -0.5, 0.0625, ((0, 8), (1, 2))),
        "out_weight": noise(key_list[4], (QUERY_HEADS * HEAD_SIZE, D), (QUERY_HEADS * HEAD_SIZE) ** -0.5, 0.09375, ((0, 2), (1, 8))),
        "residual": noise(own_keys[5], (TEXT_TOKENS, D), 0.3, 4.0, ((0, 2), (1, 8))),
        "query_norm_gain": draw_query_norm_gain(jax.random.fold_in(key_list[9], 71), part),
        "key_norm_gain": draw_key_norm_gain(jax.random.fold_in(key_list[9], 71), part),
        "attn_gate": jnp.clip(jax.random.uniform(key_list[8], (1,), jnp.float32, 0.5, 2.0), 0.5, 2.0),
    }


epsilon = 1e-05

def apply_norm(value_heads, gain):
    return value_heads * lax.rsqrt(lax.optimization_barrier(jnp.mean(value_heads * value_heads, axis=-1, keepdims=True)) + epsilon) * gain

def reference(queries, vision, key_matrix, value_matrix, out_weight, residual, query_norm_gain, key_norm_gain, attn_gate):
    expanded_keys = jnp.dot(vision, key_matrix, preferred_element_type=jnp.float32)
    expanded_values = jnp.dot(vision, value_matrix, preferred_element_type=jnp.float32)
    key_heads = apply_norm(expanded_keys.reshape(VISION_TOKENS, KEY_VALUE_HEADS, HEAD_SIZE), key_norm_gain).astype(jnp.bfloat16)
    value_heads = expanded_values.reshape(VISION_TOKENS, KEY_VALUE_HEADS, HEAD_SIZE).astype(jnp.bfloat16)
    heads_per_group = QUERY_HEADS // KEY_VALUE_HEADS
    norm_result = apply_norm(queries.astype(jnp.float32).reshape(TEXT_TOKENS, KEY_VALUE_HEADS, heads_per_group, HEAD_SIZE), query_norm_gain).astype(jnp.bfloat16)
    rows_per_block = 128 if TEXT_TOKENS % 128 == 0 else TEXT_TOKENS
    blocked_queries = norm_result.reshape(TEXT_TOKENS // rows_per_block, rows_per_block, KEY_VALUE_HEADS, heads_per_group, HEAD_SIZE)
    keys_wide = key_heads.astype(jnp.float32)
    values_wide = value_heads.astype(jnp.float32)

    def attend_block(query_block):
        scores = jnp.einsum('tgqd,rgd->tgqr', query_block.astype(jnp.float32), keys_wide) * HEAD_SIZE ** (-0.5)
        maxima = lax.optimization_barrier(jnp.max(scores, axis=-1, keepdims=True))
        weights = jnp.exp(scores - maxima)
        denominator = lax.optimization_barrier(jnp.sum(weights, axis=-1))
        rounded = lax.optimization_barrier(weights.astype(jnp.bfloat16))
        numerator = jnp.einsum('tgqr,rgd->tgqd', rounded.astype(jnp.float32), values_wide)
        return (numerator / denominator[..., None]).astype(jnp.bfloat16)
    attended = lax.map(attend_block, blocked_queries).reshape(TEXT_TOKENS, QUERY_HEADS * HEAD_SIZE)
    projected = jnp.dot(attended, out_weight, preferred_element_type=jnp.float32)
    return (residual.astype(jnp.float32) + jnp.tanh(attn_gate[0]) * projected).astype(jnp.bfloat16)
```

```python
import functools

import jax
import jax.numpy as jnp
from jax import lax
from jax.sharding import PartitionSpec as P

HEAD_SIZE = 128
epsilon = 1e-05
AXES = ("groups", "seq", "head")


def body(
    sizes,
    queries,
    vision,
    key_matrix,
    value_matrix,
    out_weight,
    residual,
    query_norm_gain,
    key_norm_gain,
    attn_gate,
):
    groups, seq, cores = sizes
    pairs = seq // 2
    group = lax.axis_index("groups")
    place = lax.axis_index("seq")
    core = lax.axis_index("head")
    side = place % 2
    f32, bf16 = jnp.float32, jnp.bfloat16

    def plane_shift(array, by_group, by_side):
        perm = []
        for g in range(groups):
            for s in range(seq):
                for c in range(cores):
                    to_g = (g + by_group) % groups
                    to_s = s // 2 * 2 + (s + by_side) % 2
                    perm.append(
                        ((g * seq + s) * cores + c, (to_g * seq + to_s) * cores + c)
                    )
        return lax.ppermute(array, AXES, perm)

    def core_swap(array):
        return lax.ppermute(array, "head", [(c, (c + 1) % cores) for c in range(cores)])

    lines = [[2 * z + y for z in range(pairs)] for y in range(2)]

    def gather_pairs(array):
        return lax.all_gather(array, "seq", axis=0, tiled=True, axis_index_groups=lines)

    offsets = [(g, y) for g in range(groups) for y in range(2)]

    slab = key_matrix.shape[0]
    part = slab // groups

    def prepare(matrix):
        mine = lax.dynamic_slice_in_dim(matrix, group * part, part, axis=0)
        half = mine.shape[1] // 2
        return jnp.where(side == 0, mine, jnp.roll(mine, half, axis=1))

    key_weight = gather_pairs(prepare(key_matrix))
    value_weight = gather_pairs(prepare(value_matrix))

    rows_q = queries.shape[0]
    half_q = queries.shape[1] // 2
    q_own = lax.dynamic_slice_in_dim(queries, side * half_q, half_q, axis=1)
    q_send = lax.dynamic_slice_in_dim(queries, (1 - side) * half_q, half_q, axis=1)
    q_recv = plane_shift(q_send, 0, 1)
    q_pair = jnp.where(
        side == 0,
        jnp.concatenate([q_own, q_recv], axis=0),
        jnp.concatenate([q_recv, q_own], axis=0),
    ).astype(f32)
    heads = half_q // HEAD_SIZE
    q_heads = q_pair.reshape(2 * rows_q, heads, HEAD_SIZE).transpose(1, 0, 2)
    normed = (
        q_heads
        * lax.rsqrt(jnp.mean(q_heads * q_heads, axis=-1, keepdims=True) + epsilon)
        * query_norm_gain
    ).astype(bf16)
    normed = normed.reshape(heads * 2 * rows_q, HEAD_SIZE)

    rows = vision.shape[0]
    half = rows // cores
    classes = (
        vision.reshape(rows, pairs, 2, groups, part)
        .transpose(3, 2, 0, 1, 4)
        .reshape(groups, 2, cores, half, pairs * part)
    )

    def take(by_group, by_side, which_core):
        return lax.dynamic_slice(
            classes,
            ((group + by_group) % groups, (side + by_side) % 2, which_core, 0, 0),
            (1, 1, 1, half, pairs * part),
        ).reshape(half, pairs * part)

    received = [plane_shift(take(g, y, core), g, y) for g, y in offsets[1:]]
    firsts = jnp.concatenate([take(0, 0, core)] + received, axis=0)
    seconds = jnp.concatenate(
        [take(0, 0, 1 - core), core_swap(jnp.concatenate(received, axis=0))], axis=0
    )

    def project(weight, dtype):
        first = jnp.dot(firsts, weight, preferred_element_type=f32)
        second = jnp.dot(seconds, weight, preferred_element_type=f32)
        both = jnp.stack(
            [
                first.reshape(groups, 2, half, 2, HEAD_SIZE),
                second.reshape(groups, 2, half, 2, HEAD_SIZE),
            ],
            axis=2,
        )
        total = None
        for g, y in offsets:
            piece = jnp.concatenate(
                [both[(-g) % groups, y, :, :, y, :], both[(-g) % groups, 1 - y, :, :, y, :]],
                axis=0,
            ).reshape(2 * rows, HEAD_SIZE)
            if (g, y) != (0, 0):
                piece = plane_shift(piece.astype(dtype), g, y).astype(f32)
            total = piece if total is None else total + piece
        return total

    keys = project(key_weight, f32)
    keys = (
        keys * lax.rsqrt(jnp.mean(keys * keys, axis=-1, keepdims=True) + epsilon) * key_norm_gain
    ).astype(bf16)
    keys = gather_pairs(keys)
    values = gather_pairs(project(value_weight, bf16).astype(bf16))

    scores = jnp.dot(normed, keys.T, preferred_element_type=f32) * HEAD_SIZE ** (-0.5)
    weights = jnp.exp(scores - jnp.max(scores, axis=-1, keepdims=True))
    denominator = jnp.sum(weights, axis=-1, keepdims=True)
    numerator = jnp.dot(weights.astype(bf16), values, preferred_element_type=f32)
    attended = (numerator / denominator).astype(bf16)
    attended = (
        attended.reshape(heads, 2 * rows_q, HEAD_SIZE)
        .transpose(1, 0, 2)
        .reshape(2 * rows_q, heads * HEAD_SIZE)
    )
    attended = gather_pairs(attended)
    other = plane_shift(attended, 0, 1)
    depth = heads * HEAD_SIZE
    weight_own = lax.dynamic_slice_in_dim(out_weight, side * depth, depth, axis=0)
    weight_other = lax.dynamic_slice_in_dim(out_weight, (1 - side) * depth, depth, axis=0)
    projected = jnp.dot(attended, weight_own, preferred_element_type=f32) + jnp.dot(
        other, weight_other, preferred_element_type=f32
    )
    out_rows = residual.shape[0]
    send = lax.dynamic_slice_in_dim(projected, (1 - core) * out_rows, out_rows, axis=0)
    mine = lax.dynamic_slice_in_dim(projected, core * out_rows, out_rows, axis=0)
    mine = mine + core_swap(send.astype(bf16)).astype(f32)
    return (residual.astype(f32) + jnp.tanh(attn_gate[0]) * mine).astype(bf16)


def solution(mesh):
    in_specs = (
        P(("groups", "seq"), "head"),
        P(("groups", "seq"), None),
        P("seq", "head"),
        P("seq", "head"),
        P("head", "seq"),
        P(("groups", "head"), "seq"),
        P(),
        P(),
        P(),
    )
    out_specs = P(("groups", "head"), "seq")
    sizes = tuple(mesh.shape[axis] for axis in AXES)
    return jax.shard_map(
        functools.partial(body, sizes),
        mesh=mesh,
        in_specs=in_specs,
        out_specs=out_specs,
        check_vma=False,
    )
```

```python
import functools

import jax
import jax.numpy as jnp
from jax import lax
from jax.experimental import pallas as pl
from jax.experimental.pallas import tpu as pltpu
from jax.sharding import PartitionSpec as P

HEAD_SIZE = 128
epsilon = 1e-05
AXES = ("groups", "seq", "head")
VMEM_BYTES = 48 * 1024 * 1024
f32, bf16 = jnp.float32, jnp.bfloat16


def pack_kernel(groups, pairs, part, index_ref, near_ref, far_ref, *outs):
    sends, own_far = outs[:-1], outs[-1]
    for g in range(groups):
        for y in range(2):
            starts = [((2 * z + y) * groups + g) * part for z in range(pairs)]

            def columns(ref):
                return jnp.concatenate([ref[:, s : s + part] for s in starts], axis=1)

            for k, send in enumerate(sends):

                @pl.when(index_ref[k] == g * 2 + y)
                def _():
                    send[...] = columns(near_ref)

            @pl.when(index_ref[0] == g * 2 + y)
            def _():
                own_far[...] = columns(far_ref)


def pack(vision, index, core, groups, pairs, part):
    rows, width = vision.shape
    half = rows // 2
    block = 32
    steps = half // block
    count = groups * 2
    depth = pairs * part
    scalars = jnp.concatenate([index, jnp.stack([core])]).astype(jnp.int32)
    return pl.pallas_call(
        functools.partial(pack_kernel, groups, pairs, part),
        grid_spec=pltpu.PrefetchScalarGridSpec(
            num_scalar_prefetch=1,
            grid=(steps,),
            in_specs=[
                pl.BlockSpec((block, width), lambda i, s: (s[count] * steps + i, 0)),
                pl.BlockSpec((block, width), lambda i, s: ((1 - s[count]) * steps + i, 0)),
            ],
            out_specs=[pl.BlockSpec((block, depth), lambda i, s: (i, 0))] * (count + 1),
        ),
        out_shape=[jax.ShapeDtypeStruct((half, depth), vision.dtype)] * (count + 1),
        compiler_params=pltpu.CompilerParams(vmem_limit_bytes=VMEM_BYTES),
        name="pack",
    )(scalars, vision, vision)


def project_kernel(groups, *refs):
    count = groups * 2
    near, own_far, far, weight = refs[:count], refs[count], refs[count + 1], refs[count + 2]
    outs = refs[count + 3 :]
    half = own_far.shape[0]
    firsts = jnp.concatenate([ref[...] for ref in near], axis=0)
    seconds = jnp.concatenate([own_far[...], far[...]], axis=0)
    w = weight[...]
    for part, lhs in enumerate((firsts, seconds)):
        result = jnp.dot(lhs, w, preferred_element_type=f32)
        for source in range(count):
            by_group, by_side = source // 2, source % 2
            for side in range(2):
                out = outs[(-by_group) % groups * 2 + side]
                start = (0 if by_side == side else 2 * half) + part * half
                out[start : start + half, :] = result[
                    source * half : (source + 1) * half, side * HEAD_SIZE : (side + 1) * HEAD_SIZE
                ].astype(out.dtype)


def project(near, own_far, far, weight, dtype):
    count = len(near)
    half = own_far.shape[0]
    shapes = [
        jax.ShapeDtypeStruct((4 * half, HEAD_SIZE), f32 if k == 0 else dtype) for k in range(count)
    ]
    return pl.pallas_call(
        functools.partial(project_kernel, count // 2),
        out_shape=shapes,
        compiler_params=pltpu.CompilerParams(vmem_limit_bytes=VMEM_BYTES),
        name="project",
    )(*near, own_far, far, weight)


def attend_kernel(q_ref, k_ref, v_ref, out_ref):
    text = out_ref.shape[0]
    heads = q_ref.shape[0] // text
    keys, values = k_ref[...], v_ref[...]
    for h in range(heads):
        scores = (
            lax.dot_general(
                q_ref[h * text : (h + 1) * text, :],
                keys,
                (((1,), (1,)), ((), ())),
                preferred_element_type=f32,
            )
            * HEAD_SIZE ** (-0.5)
        )
        weights = jnp.exp(scores - jnp.max(scores, axis=-1, keepdims=True))
        denominator = jnp.sum(weights, axis=-1, keepdims=True)
        numerator = jnp.dot(weights.astype(bf16), values, preferred_element_type=f32)
        out_ref[:, h * HEAD_SIZE : (h + 1) * HEAD_SIZE] = (numerator / denominator).astype(bf16)


def attend(normed, keys, values, text):
    heads = normed.shape[0] // text
    return pl.pallas_call(
        attend_kernel,
        out_shape=jax.ShapeDtypeStruct((text, heads * HEAD_SIZE), bf16),
        compiler_params=pltpu.CompilerParams(vmem_limit_bytes=VMEM_BYTES),
        name="attend",
    )(normed, keys, values)


def norm(array, gain):
    mean = jnp.mean(array * array, axis=-1, keepdims=True)
    return (array * lax.rsqrt(mean + epsilon) * gain).astype(bf16)


def body(
    sizes,
    queries,
    vision,
    key_matrix,
    value_matrix,
    out_weight,
    residual,
    query_norm_gain,
    key_norm_gain,
    attn_gate,
):
    groups, seq, cores = sizes
    pairs = seq // 2
    group = lax.axis_index("groups")
    side = lax.axis_index("seq") % 2
    core = lax.axis_index("head")

    def plane_shift(array, by_group, by_side):
        perm = []
        for g in range(groups):
            for s in range(seq):
                for c in range(cores):
                    to_g = (g + by_group) % groups
                    to_s = s // 2 * 2 + (s + by_side) % 2
                    perm.append(
                        ((g * seq + s) * cores + c, (to_g * seq + to_s) * cores + c)
                    )
        return lax.ppermute(array, AXES, perm)

    def core_swap(array):
        return lax.ppermute(array, "head", [(c, (c + 1) % cores) for c in range(cores)])

    lines = [[2 * z + y for z in range(pairs)] for y in range(2)]

    def gather_pairs(array):
        return lax.all_gather(array, "seq", axis=0, tiled=True, axis_index_groups=lines)

    offsets = [(g, y) for g in range(groups) for y in range(2)]

    part = key_matrix.shape[0] // groups

    def prepare(matrix):
        mine = lax.dynamic_slice_in_dim(matrix, group * part, part, axis=0)
        half = mine.shape[1] // 2
        return jnp.where(side == 0, mine, jnp.roll(mine, half, axis=1))

    index = jnp.stack([(group + g) % groups * 2 + (side + y) % 2 for g, y in offsets])
    packed = pack(vision, index, core, groups, pairs, part)
    received = [plane_shift(packed[k], g, y) for k, (g, y) in enumerate(offsets) if k]
    near = [packed[0]] + received
    own_far = packed[-1]

    key_send, _ = lax.optimization_barrier((prepare(key_matrix), packed[1]))
    key_weight = gather_pairs(key_send)
    joined, _ = lax.optimization_barrier((jnp.concatenate(received, axis=0), key_weight))
    far = core_swap(joined)

    rows_q = queries.shape[0]
    half_q = queries.shape[1] // 2
    heads = half_q // HEAD_SIZE
    q_own = lax.dynamic_slice_in_dim(queries, side * half_q, half_q, axis=1)
    q_send = lax.dynamic_slice_in_dim(queries, (1 - side) * half_q, half_q, axis=1)
    q_recv = plane_shift(q_send, 0, 1)
    q_pair = jnp.where(
        side == 0,
        jnp.concatenate([q_own, q_recv], axis=0),
        jnp.concatenate([q_recv, q_own], axis=0),
    )
    q_heads = jnp.concatenate(
        [q_pair[:, h * HEAD_SIZE : (h + 1) * HEAD_SIZE] for h in range(heads)], axis=0
    )
    normed = norm(q_heads.astype(f32), query_norm_gain)

    def scatter(pieces):
        total = pieces[0]
        for k, (g, y) in enumerate(offsets):
            if k:
                total = total + plane_shift(pieces[k], g, y).astype(f32)
        return total

    key_pieces = project(near, own_far, far, key_weight, f32)
    value_send, key_pieces = lax.optimization_barrier((prepare(value_matrix), key_pieces))
    key_total = scatter(key_pieces)
    value_weight = gather_pairs(value_send)
    value_pieces = project(near, own_far, far, value_weight, bf16)
    keys, value_pieces = lax.optimization_barrier((norm(key_total, key_norm_gain), value_pieces))
    value_total = scatter(value_pieces)
    keys = gather_pairs(keys)
    value_rows, keys = lax.optimization_barrier((value_total.astype(bf16), keys))
    values = gather_pairs(value_rows)

    attended = gather_pairs(attend(normed, keys, values, 2 * rows_q))
    other = plane_shift(attended, 0, 1)
    depth = heads * HEAD_SIZE
    weight_own = lax.dynamic_slice_in_dim(out_weight, side * depth, depth, axis=0)
    weight_other = lax.dynamic_slice_in_dim(out_weight, (1 - side) * depth, depth, axis=0)
    projected = jnp.dot(attended, weight_own, preferred_element_type=f32) + jnp.dot(
        other, weight_other, preferred_element_type=f32
    )
    out_rows = residual.shape[0]
    send = lax.dynamic_slice_in_dim(projected, (1 - core) * out_rows, out_rows, axis=0)
    mine = lax.dynamic_slice_in_dim(projected, core * out_rows, out_rows, axis=0)
    mine = mine + core_swap(send.astype(bf16)).astype(f32)
    return (residual.astype(f32) + jnp.tanh(attn_gate[0]) * mine).astype(bf16)


def solution(mesh):
    in_specs = (
        P(("groups", "seq"), "head"),
        P(("groups", "seq"), None),
        P("seq", "head"),
        P("seq", "head"),
        P("head", "seq"),
        P(("groups", "head"), "seq"),
        P(),
        P(),
        P(),
    )
    out_specs = P(("groups", "head"), "seq")
    sizes = tuple(mesh.shape[axis] for axis in AXES)
    return jax.shard_map(
        functools.partial(body, sizes),
        mesh=mesh,
        in_specs=in_specs,
        out_specs=out_specs,
        check_vma=False,
    )
```

```python
import functools

import jax
import jax.numpy as jnp
from jax import lax
from jax.experimental import pallas as pl
from jax.experimental.pallas import tpu as pltpu
from jax.sharding import PartitionSpec as P

HEAD_SIZE = 128
epsilon = 1e-05
AXES = ("groups", "seq", "head")
VMEM_BYTES = 48 * 1024 * 1024
f32, bf16 = jnp.float32, jnp.bfloat16


def pack_kernel(groups, pairs, part, count, index_ref, rows_ref, *outs):
    for g in range(groups):
        for y in range(2):
            starts = [((2 * z + y) * groups + g) * part for z in range(pairs)]
            for k, out in enumerate(outs):

                @pl.when(index_ref[k] == g * 2 + y)
                def _():
                    out[...] = jnp.concatenate(
                        [rows_ref[:, s : s + part] for s in starts], axis=1
                    )


def pack(vision, index, core, groups, pairs, part, name):
    rows, width = vision.shape
    half = rows // 2
    block = 32
    steps = half // block
    count = len(index)
    depth = pairs * part
    scalars = jnp.stack([*index, core]).astype(jnp.int32)
    return pl.pallas_call(
        functools.partial(pack_kernel, groups, pairs, part, count),
        grid_spec=pltpu.PrefetchScalarGridSpec(
            num_scalar_prefetch=1,
            grid=(steps,),
            in_specs=[pl.BlockSpec((block, width), lambda i, s: (s[count] * steps + i, 0))],
            out_specs=[pl.BlockSpec((block, depth), lambda i, s: (i, 0))] * count,
        ),
        out_shape=[jax.ShapeDtypeStruct((half, depth), vision.dtype)] * count,
        compiler_params=pltpu.CompilerParams(vmem_limit_bytes=VMEM_BYTES),
        name=name,
    )(scalars, vision)


def project_kernel(groups, pairs, shifts, scalars, *refs):
    count = groups * 2
    near, far, slabs = refs[:count], refs[count : 2 * count], refs[2 * count : -count - 1]
    outs, placed = refs[-count - 1 : -1], refs[-1]
    half = near[0].shape[0]
    side, place = scalars[0], scalars[1]
    for shift, slab in zip(shifts, slabs):
        if isinstance(shift, tuple):
            continue
        placed[lax.rem(place + pairs - shift, pairs)] = slab[...]
    for shift, slab in zip(shifts, slabs):
        if isinstance(shift, tuple):

            @pl.when(place >= pairs // 2)
            def _():
                placed[lax.rem(place + pairs - shift[0], pairs)] = slab[...]

    w = jnp.concatenate([placed[z] for z in range(pairs)], axis=0)
    swapped = jnp.concatenate([w[:, HEAD_SIZE:], w[:, :HEAD_SIZE]], axis=1)
    w = jnp.where(side == 0, w, swapped)
    for part, pieces in enumerate((near, far)):
        lhs = jnp.concatenate([ref[...] for ref in pieces], axis=0)
        result = jnp.dot(lhs, w, preferred_element_type=f32)
        for source in range(count):
            by_group, by_side = source // 2, source % 2
            for to in range(2):
                out = outs[(-by_group) % groups * 2 + to]
                start = (0 if by_side == to else 2 * half) + part * half
                out[start : start + half, :] = result[
                    source * half : (source + 1) * half, to * HEAD_SIZE : (to + 1) * HEAD_SIZE
                ].astype(out.dtype)


def project(near, far, shifts, slabs, side, place, pairs, dtype, name):
    count = len(near)
    half = near[0].shape[0]
    vmem = pl.BlockSpec(memory_space=pltpu.VMEM)
    return pl.pallas_call(
        functools.partial(project_kernel, count // 2, pairs, shifts),
        in_specs=[pl.BlockSpec(memory_space=pltpu.SMEM)] + [vmem] * (2 * count + len(slabs)),
        out_specs=[vmem] * count,
        out_shape=[
            jax.ShapeDtypeStruct((4 * half, HEAD_SIZE), dtype if k else f32) for k in range(count)
        ],
        scratch_shapes=[pltpu.VMEM((pairs,) + slabs[0].shape, bf16)],
        compiler_params=pltpu.CompilerParams(vmem_limit_bytes=VMEM_BYTES),
        name=name,
    )(jnp.stack([side, place]).astype(jnp.int32), *near, *far, *slabs)


def score_kernel(heads, q_ref, *refs):
    keys, weights_ref, denominator_ref = refs[:-2], refs[-2], refs[-1]
    block = keys[0].shape[0]
    text = q_ref.shape[0] // heads
    for h in range(heads):
        rows = slice(h * text, (h + 1) * text)
        scores = [
            lax.dot_general(
                q_ref[rows, :], k[...], (((1,), (1,)), ((), ())), preferred_element_type=f32
            )
            * HEAD_SIZE ** (-0.5)
            for k in keys
        ]
        top = functools.reduce(
            jnp.maximum, [jnp.max(s, axis=-1, keepdims=True) for s in scores]
        )
        total = jnp.zeros_like(top)
        for n, s in enumerate(scores):
            weights = jnp.exp(s - top)
            total = total + jnp.sum(weights, axis=-1, keepdims=True)
            weights_ref[rows, n * block : (n + 1) * block] = weights.astype(bf16)
        denominator_ref[rows, :] = jnp.broadcast_to(total, (text, HEAD_SIZE))


def score(normed, keys, heads):
    rows = normed.shape[0]
    return pl.pallas_call(
        functools.partial(score_kernel, heads),
        out_shape=[
            jax.ShapeDtypeStruct((rows, len(keys) * keys[0].shape[0]), bf16),
            jax.ShapeDtypeStruct((rows, HEAD_SIZE), f32),
        ],
        compiler_params=pltpu.CompilerParams(vmem_limit_bytes=VMEM_BYTES),
        name="score",
    )(normed, *keys)


def mix_kernel(weights_ref, denominator_ref, *refs):
    values, out_ref = refs[:-1], refs[-1]
    text = out_ref.shape[0]
    v = jnp.concatenate([ref[...] for ref in values], axis=0)
    numerator = jnp.dot(weights_ref[...], v, preferred_element_type=f32)
    attended = (numerator / denominator_ref[...]).astype(bf16)
    for h in range(out_ref.shape[1] // HEAD_SIZE):
        out_ref[:, h * HEAD_SIZE : (h + 1) * HEAD_SIZE] = attended[h * text : (h + 1) * text, :]


def mix(weights, denominator, values, heads):
    rows = weights.shape[0]
    return pl.pallas_call(
        mix_kernel,
        out_shape=jax.ShapeDtypeStruct((rows // heads, heads * HEAD_SIZE), bf16),
        compiler_params=pltpu.CompilerParams(vmem_limit_bytes=VMEM_BYTES),
        name="mix",
    )(weights, denominator, *values)


def after(array, *others):
    return lax.optimization_barrier((array, others))[0]


def norm(array, gain):
    mean = jnp.mean(array * array, axis=-1, keepdims=True)
    return (array * lax.rsqrt(mean + epsilon) * gain).astype(bf16)


def body(
    sizes,
    queries,
    vision,
    key_matrix,
    value_matrix,
    out_weight,
    residual,
    query_norm_gain,
    key_norm_gain,
    attn_gate,
):
    groups, seq, cores = sizes
    pairs = seq // 2
    group = lax.axis_index("groups")
    side = lax.axis_index("seq") % 2
    place = lax.axis_index("seq") // 2
    core = lax.axis_index("head")

    def permute(array, target):
        perm = []
        for g in range(groups):
            for z in range(pairs):
                for y in range(2):
                    for c in range(cores):
                        to = target(g, z, y, c)
                        if to is not None:
                            tg, tz, ty, tc = to
                            perm.append(
                                (
                                    (g * seq + z * 2 + y) * cores + c,
                                    (tg % groups * seq + tz % pairs * 2 + ty % 2) * cores
                                    + tc % cores,
                                )
                            )
        return lax.ppermute(array, AXES, perm)

    def plane_shift(array, by_group, by_side):
        return permute(array, lambda g, z, y, c: (g + by_group, z, y + by_side, c))

    def line_shift(array, by):
        return permute(array, lambda g, z, y, c: (g, z + by, y, c))

    def core_swap(array):
        return permute(array, lambda g, z, y, c: (g, z, y, c + 1))

    middle = pairs // 2 if pairs % 2 == 0 and pairs > 2 else 0

    def line_near(array):
        return {k: line_shift(array, k) for k in range(1, pairs) if k != middle}

    def line_far(pieces):
        if not middle:
            return []
        up = permute(
            pieces[middle - 1],
            lambda g, z, y, c: (g, z + 1, y, c) if middle <= z + 1 < pairs else None,
        )
        down = permute(
            pieces[middle + 1],
            lambda g, z, y, c: (g, z - 1, y, c) if 0 <= z - 1 < middle else None,
        )
        return [up, down]

    near_shifts = [k for k in range(1, pairs) if k != middle]
    shifts = [0] + near_shifts + ([middle, (middle,)] if middle else [])

    def line_slabs(own, pieces, far):
        return [own] + [pieces[k] for k in near_shifts] + far[::-1]

    lines = [[2 * z + y for z in range(pairs)] for y in range(2)]

    def gather_pairs(array):
        return lax.all_gather(array, "seq", axis=0, tiled=True, axis_index_groups=lines)

    def all_pairs(array):
        return [array] + [line_shift(array, k) for k in range(1, pairs)]

    offsets = [(g, y) for g in range(groups) for y in range(2)]

    part = key_matrix.shape[0] // groups

    def own_part(matrix):
        return lax.dynamic_slice_in_dim(matrix, group * part, part, axis=0)

    key_own = own_part(key_matrix)
    key_near = line_near(key_own)

    index = [(group + g) % groups * 2 + (side + y) % 2 for g, y in offsets]
    vision = after(vision, key_own)
    sends = pack(vision, index[1:], core, groups, pairs, part, "pack_sends")
    received = [plane_shift(send, g, y) for send, (g, y) in zip(sends, offsets[1:])]
    vision = after(vision, *sends)
    near = pack(vision, index[:1], core, groups, pairs, part, "pack_near")
    near = [*near, *received]
    far = pack(vision, index[:1], 1 - core, groups, pairs, part, "pack_far")

    rows_q = queries.shape[0]
    half_q = queries.shape[1] // 2
    heads = half_q // HEAD_SIZE
    queries = after(queries, far[0])
    q_own = lax.dynamic_slice_in_dim(queries, side * half_q, half_q, axis=1)
    q_send = lax.dynamic_slice_in_dim(queries, (1 - side) * half_q, half_q, axis=1)

    key_far = line_far(key_near)
    received = [after(piece, *key_near.values()) for piece in received]
    far = [*far] + [core_swap(piece) for piece in received]
    value_own = after(own_part(value_matrix), *key_far)
    value_near = line_near(value_own)

    def scatter(pieces):
        return [plane_shift(piece, g, y) for piece, (g, y) in zip(pieces[1:], offsets[1:])]

    def sum_up(own, pieces):
        return functools.reduce(lambda a, b: a + b.astype(f32), pieces, own)

    key_slabs = line_slabs(key_own, key_near, key_far)
    key_pieces = project(near, far, shifts, key_slabs, side, place, pairs, f32, "project_keys")
    key_parts = scatter(key_pieces)
    value_near = {k: after(v, *key_pieces) for k, v in value_near.items()}
    value_far = line_far(value_near)
    q_recv = plane_shift(after(q_send, *key_parts), 0, 1)
    keys = norm(sum_up(key_pieces[0], key_parts), key_norm_gain)
    all_keys = all_pairs(keys)
    value_far = [after(v, keys) for v in value_far]
    value_slabs = line_slabs(value_own, value_near, value_far)
    value_pieces = project(
        near, far, shifts, value_slabs, side, place, pairs, bf16, "project_values"
    )
    value_parts = scatter(value_pieces)
    q_recv = after(q_recv, *value_pieces)
    q_pair = jnp.where(
        side == 0,
        jnp.concatenate([q_own, q_recv], axis=0),
        jnp.concatenate([q_recv, q_own], axis=0),
    )
    q_heads = jnp.concatenate(
        [q_pair[:, h * HEAD_SIZE : (h + 1) * HEAD_SIZE] for h in range(heads)], axis=0
    )
    normed = norm(q_heads.astype(f32), query_norm_gain)
    values = sum_up(value_pieces[0], value_parts).astype(bf16)
    all_values = all_pairs(values)
    all_keys = [after(k, values) for k in all_keys]
    weights, denominator = score(normed, all_keys, heads)
    attended = gather_pairs(mix(weights, denominator, all_values, heads))
    other = plane_shift(attended, 0, 1)
    depth = heads * HEAD_SIZE
    weight_own = lax.dynamic_slice_in_dim(out_weight, side * depth, depth, axis=0)
    weight_other = lax.dynamic_slice_in_dim(out_weight, (1 - side) * depth, depth, axis=0)
    projected = jnp.dot(attended, weight_own, preferred_element_type=f32) + jnp.dot(
        other, weight_other, preferred_element_type=f32
    )
    out_rows = residual.shape[0]
    send = lax.dynamic_slice_in_dim(projected, (1 - core) * out_rows, out_rows, axis=0)
    mine = lax.dynamic_slice_in_dim(projected, core * out_rows, out_rows, axis=0)
    mine = mine + core_swap(send.astype(bf16)).astype(f32)
    return (residual.astype(f32) + jnp.tanh(attn_gate[0]) * mine).astype(bf16)


def solution(mesh):
    in_specs = (
        P(("groups", "seq"), "head"),
        P(("groups", "seq"), None),
        P("seq", "head"),
        P("seq", "head"),
        P("head", "seq"),
        P(("groups", "head"), "seq"),
        P(),
        P(),
        P(),
    )
    out_specs = P(("groups", "head"), "seq")
    sizes = tuple(mesh.shape[axis] for axis in AXES)
    return jax.shard_map(
        functools.partial(body, sizes),
        mesh=mesh,
        in_specs=in_specs,
        out_specs=out_specs,
        check_vma=False,
    )
```

```python
import functools

import jax
import jax.numpy as jnp
from jax import lax
from jax.experimental import pallas as pl
from jax.experimental.pallas import tpu as pltpu
from jax.sharding import PartitionSpec as P

HEAD_SIZE = 128
epsilon = 1e-05
AXES = ("groups", "seq", "head")
VMEM_BYTES = 48 * 1024 * 1024
f32, bf16 = jnp.float32, jnp.bfloat16


def pack_kernel(groups, pairs, part, count, index_ref, rows_ref, *outs):
    for g in range(groups):
        for y in range(2):
            starts = [((2 * z + y) * groups + g) * part for z in range(pairs)]
            for k, out in enumerate(outs):

                @pl.when(index_ref[k] == g * 2 + y)
                def _():
                    out[...] = jnp.concatenate(
                        [rows_ref[:, s : s + part] for s in starts], axis=1
                    )


def pack(vision, index, core, groups, pairs, part, name):
    rows, width = vision.shape
    half = rows // 2
    block = 32
    steps = half // block
    count = len(index)
    depth = pairs * part
    scalars = jnp.stack([*index, core]).astype(jnp.int32)
    return pl.pallas_call(
        functools.partial(pack_kernel, groups, pairs, part, count),
        grid_spec=pltpu.PrefetchScalarGridSpec(
            num_scalar_prefetch=1,
            grid=(steps,),
            in_specs=[pl.BlockSpec((block, width), lambda i, s: (s[count] * steps + i, 0))],
            out_specs=[pl.BlockSpec((block, depth), lambda i, s: (i, 0))] * count,
        ),
        out_shape=[jax.ShapeDtypeStruct((half, depth), vision.dtype)] * count,
        compiler_params=pltpu.CompilerParams(vmem_limit_bytes=VMEM_BYTES),
        name=name,
    )(scalars, vision)


def project_kernel(groups, pairs, shifts, scalars, *refs):
    count = groups * 2
    near, far, slabs = refs[:count], refs[count : 2 * count], refs[2 * count : -2 * count - 1]
    outs, placed = refs[-2 * count - 1 : -1], refs[-1]
    half = near[0].shape[0]
    side, place = scalars[0], scalars[1]
    for shift, slab in zip(shifts, slabs):
        if isinstance(shift, tuple):
            continue
        placed[lax.rem(place + pairs - shift, pairs)] = slab[...]
    for shift, slab in zip(shifts, slabs):
        if isinstance(shift, tuple):

            @pl.when(place >= pairs // 2)
            def _():
                placed[lax.rem(place + pairs - shift[0], pairs)] = slab[...]

    w = jnp.concatenate([placed[z] for z in range(pairs)], axis=0)
    for part, pieces in enumerate((near, far)):
        lhs = jnp.concatenate([ref[...] for ref in pieces], axis=0)
        result = jnp.dot(lhs, w, preferred_element_type=f32)
        columns = [result[:, n * HEAD_SIZE : (n + 1) * HEAD_SIZE] for n in range(4)]
        for matrix in range(2):
            first, second = columns[2 * matrix : 2 * matrix + 2]
            heads = jnp.where(side == 0, first, second), jnp.where(side == 0, second, first)
            for source in range(count):
                by_group, by_side = source // 2, source % 2
                for to in range(2):
                    out = outs[matrix * count + (-by_group) % groups * 2 + to]
                    start = (0 if by_side == to else 2 * half) + part * half
                    out[start : start + half, :] = heads[to][
                        source * half : (source + 1) * half, :
                    ].astype(out.dtype)


def project(near, far, shifts, slabs, side, place, pairs):
    count = len(near)
    half = near[0].shape[0]
    vmem = pl.BlockSpec(memory_space=pltpu.VMEM)
    return pl.pallas_call(
        functools.partial(project_kernel, count // 2, pairs, shifts),
        in_specs=[pl.BlockSpec(memory_space=pltpu.SMEM)] + [vmem] * (2 * count + len(slabs)),
        out_specs=[vmem] * (2 * count),
        out_shape=[
            jax.ShapeDtypeStruct((4 * half, HEAD_SIZE), bf16 if k > count else f32)
            for k in range(2 * count)
        ],
        scratch_shapes=[pltpu.VMEM((pairs,) + slabs[0].shape, bf16)],
        compiler_params=pltpu.CompilerParams(vmem_limit_bytes=VMEM_BYTES),
        name="project",
    )(jnp.stack([side, place]).astype(jnp.int32), *near, *far, *slabs)


def score_kernel(heads, q_ref, *refs):
    keys, weights_ref, denominator_ref = refs[:-2], refs[-2], refs[-1]
    block = keys[0].shape[0]
    text = q_ref.shape[0] // heads
    for h in range(heads):
        rows = slice(h * text, (h + 1) * text)
        scores = [
            lax.dot_general(
                q_ref[rows, :], k[...], (((1,), (1,)), ((), ())), preferred_element_type=f32
            )
            * HEAD_SIZE ** (-0.5)
            for k in keys
        ]
        top = functools.reduce(
            jnp.maximum, [jnp.max(s, axis=-1, keepdims=True) for s in scores]
        )
        total = jnp.zeros_like(top)
        for n, s in enumerate(scores):
            weights = jnp.exp(s - top)
            total = total + jnp.sum(weights, axis=-1, keepdims=True)
            weights_ref[rows, n * block : (n + 1) * block] = weights.astype(bf16)
        denominator_ref[rows, :] = jnp.broadcast_to(total, (text, HEAD_SIZE))


def score(normed, keys, heads):
    rows = normed.shape[0]
    return pl.pallas_call(
        functools.partial(score_kernel, heads),
        out_shape=[
            jax.ShapeDtypeStruct((rows, len(keys) * keys[0].shape[0]), bf16),
            jax.ShapeDtypeStruct((rows, HEAD_SIZE), f32),
        ],
        compiler_params=pltpu.CompilerParams(vmem_limit_bytes=VMEM_BYTES),
        name="score",
    )(normed, *keys)


def mix_kernel(weights_ref, denominator_ref, *refs):
    values, out_ref = refs[:-1], refs[-1]
    text = out_ref.shape[0]
    v = jnp.concatenate([ref[...] for ref in values], axis=0)
    numerator = jnp.dot(weights_ref[...], v, preferred_element_type=f32)
    attended = (numerator / denominator_ref[...]).astype(bf16)
    for h in range(out_ref.shape[1] // HEAD_SIZE):
        out_ref[:, h * HEAD_SIZE : (h + 1) * HEAD_SIZE] = attended[h * text : (h + 1) * text, :]


def mix(weights, denominator, values, heads):
    rows = weights.shape[0]
    return pl.pallas_call(
        mix_kernel,
        out_shape=jax.ShapeDtypeStruct((rows // heads, heads * HEAD_SIZE), bf16),
        compiler_params=pltpu.CompilerParams(vmem_limit_bytes=VMEM_BYTES),
        name="mix",
    )(weights, denominator, *values)


def output_kernel(pairs, last, scalars, *refs):
    pieces, weight, placed = refs[:pairs], refs[pairs], refs[-1]
    place, core = scalars[1], scalars[2]
    for k, piece in enumerate(pieces):
        placed[lax.rem(place + pairs - k, pairs)] = piece[...]
    lhs = jnp.concatenate([placed[z] for z in range(pairs)], axis=0)
    product = jnp.dot(lhs, weight[...], preferred_element_type=f32)
    if not last:
        refs[pairs + 1][...] = product
        return
    total, mine, send = refs[pairs + 1 : pairs + 4]
    product = product + total[...]
    half = mine.shape[0]
    upper, lower = product[:half], product[half:]
    mine[...] = jnp.where(core == 0, upper, lower)
    send[...] = jnp.where(core == 0, lower, upper).astype(bf16)


def output(pieces, out_weight, side, place, core, total, name):
    pairs = len(pieces)
    text, depth = pieces[0].shape
    width = out_weight.shape[1]
    rows = pairs * text
    whole = lambda *shape: pl.BlockSpec(shape, lambda i, s: (0, 0))
    last = total is not None
    shapes = [(rows // 2, width, f32), (rows // 2, width, bf16)] if last else [(rows, width, f32)]
    return pl.pallas_call(
        functools.partial(output_kernel, pairs, last),
        grid_spec=pltpu.PrefetchScalarGridSpec(
            num_scalar_prefetch=1,
            grid=(1,),
            in_specs=[whole(text, depth)] * pairs
            + [pl.BlockSpec((depth, width), lambda i, s: (s[0], 0))]
            + ([whole(rows, width)] if last else []),
            out_specs=[whole(*shape[:2]) for shape in shapes],
            scratch_shapes=[pltpu.VMEM((pairs, text, depth), bf16)],
        ),
        out_shape=[jax.ShapeDtypeStruct(shape[:2], shape[2]) for shape in shapes],
        compiler_params=pltpu.CompilerParams(vmem_limit_bytes=VMEM_BYTES),
        name=name,
    )(
        jnp.stack([side, place, core]).astype(jnp.int32),
        *pieces,
        out_weight,
        *([total] if last else []),
    )


def after(array, *others):
    return lax.optimization_barrier((array, others))[0]


def norm(array, gain):
    mean = jnp.mean(array * array, axis=-1, keepdims=True)
    return (array * lax.rsqrt(mean + epsilon) * gain).astype(bf16)


def body(
    sizes,
    queries,
    vision,
    key_matrix,
    value_matrix,
    out_weight,
    residual,
    query_norm_gain,
    key_norm_gain,
    attn_gate,
):
    groups, seq, cores = sizes
    pairs = seq // 2
    group = lax.axis_index("groups")
    side = lax.axis_index("seq") % 2
    place = lax.axis_index("seq") // 2
    core = lax.axis_index("head")

    def permute(array, target):
        perm = []
        for g in range(groups):
            for z in range(pairs):
                for y in range(2):
                    for c in range(cores):
                        to = target(g, z, y, c)
                        if to is not None:
                            tg, tz, ty, tc = to
                            perm.append(
                                (
                                    (g * seq + z * 2 + y) * cores + c,
                                    (tg % groups * seq + tz % pairs * 2 + ty % 2) * cores
                                    + tc % cores,
                                )
                            )
        return lax.ppermute(array, AXES, perm)

    def plane_shift(array, by_group, by_side):
        return permute(array, lambda g, z, y, c: (g + by_group, z, y + by_side, c))

    def line_shift(array, by):
        return permute(array, lambda g, z, y, c: (g, z + by, y, c))

    def core_swap(array):
        return permute(array, lambda g, z, y, c: (g, z, y, c + 1))

    middle = pairs // 2 if pairs % 2 == 0 and pairs > 2 else 0

    def line_near(array):
        return {k: line_shift(array, k) for k in range(1, pairs) if k != middle}

    def line_far(pieces):
        if not middle:
            return []
        up = permute(
            pieces[middle - 1],
            lambda g, z, y, c: (g, z + 1, y, c) if middle <= z + 1 < pairs else None,
        )
        down = permute(
            pieces[middle + 1],
            lambda g, z, y, c: (g, z - 1, y, c) if 0 <= z - 1 < middle else None,
        )
        return [up, down]

    near_shifts = [k for k in range(1, pairs) if k != middle]
    shifts = [0] + near_shifts + ([middle, (middle,)] if middle else [])

    def line_slabs(own, pieces, far):
        return [own] + [pieces[k] for k in near_shifts] + far[::-1]

    def all_pairs(array):
        return [array] + [line_shift(array, k) for k in range(1, pairs)]

    offsets = [(g, y) for g in range(groups) for y in range(2)]

    part = key_matrix.shape[0] // groups

    def own_part(matrix):
        return lax.dynamic_slice_in_dim(matrix, group * part, part, axis=0)

    slab = jnp.concatenate([own_part(key_matrix), own_part(value_matrix)], axis=1)
    slab_near = line_near(slab)

    index = [(group + g) % groups * 2 + (side + y) % 2 for g, y in offsets]
    vision = after(vision, slab)
    sends = pack(vision, index[1:], core, groups, pairs, part, "pack_sends")
    received = [plane_shift(send, g, y) for send, (g, y) in zip(sends, offsets[1:])]
    vision = after(vision, *sends)
    near = pack(vision, index[:1], core, groups, pairs, part, "pack_near")
    far = pack(vision, index[:1], 1 - core, groups, pairs, part, "pack_far")

    rows_q = queries.shape[0]
    half_q = queries.shape[1] // 2
    heads = half_q // HEAD_SIZE
    queries = after(queries, far[0])
    q_own = lax.dynamic_slice_in_dim(queries, side * half_q, half_q, axis=1)
    q_send = lax.dynamic_slice_in_dim(queries, (1 - side) * half_q, half_q, axis=1)

    received = [after(piece, near[0], far[0]) for piece in received]
    near = [*near, *received]
    slab_far = line_far({k: after(s, near[0], far[0]) for k, s in slab_near.items()})
    far = [*far] + [core_swap(piece) for piece in received]

    def scatter(pieces):
        return [plane_shift(piece, g, y) for piece, (g, y) in zip(pieces[1:], offsets[1:])]

    def sum_up(own, pieces):
        return functools.reduce(lambda a, b: a + b.astype(f32), pieces, own)

    q_recv = plane_shift(after(q_send, *received), 0, 1)
    far[-1] = after(far[-1], q_recv)
    slabs = line_slabs(slab, slab_near, slab_far)
    pieces = project(near, far, shifts, slabs, side, place, pairs)
    key_pieces, value_pieces = pieces[: len(offsets)], pieces[len(offsets) :]
    key_parts = scatter(key_pieces)
    value_parts = scatter(value_pieces)
    keys = norm(sum_up(key_pieces[0], key_parts), key_norm_gain)
    all_keys = all_pairs(keys)
    q_recv = after(q_recv, *pieces)
    q_pair = jnp.where(
        side == 0,
        jnp.concatenate([q_own, q_recv], axis=0),
        jnp.concatenate([q_recv, q_own], axis=0),
    )
    q_heads = jnp.concatenate(
        [q_pair[:, h * HEAD_SIZE : (h + 1) * HEAD_SIZE] for h in range(heads)], axis=0
    )
    normed = norm(q_heads.astype(f32), query_norm_gain)
    values = sum_up(value_pieces[0], value_parts).astype(bf16)
    all_values = all_pairs(values)
    all_keys = [after(k, values) for k in all_keys]
    weights, denominator = score(normed, all_keys, heads)
    attended = mix(weights, denominator, all_values, heads)
    others = [plane_shift(attended, 0, 1)]
    own_pieces = [attended]
    order = sorted(range(1, pairs), key=lambda k: min(k, pairs - k))
    arrived = {k: line_shift(attended, k) for k in order}
    for last, k in zip(order, order[1:]):
        arrived[k] = after(arrived[k], arrived[last])
    passed = {k: plane_shift(arrived[k], 0, 1) for k in order}
    own_pieces += [arrived[k] for k in range(1, pairs)]
    others += [passed[k] for k in range(1, pairs)]
    (total,) = output(own_pieces, out_weight, side, place, core, None, "output_own")
    mine, send = output(others, out_weight, 1 - side, place, core, total, "output_other")
    mine = mine + core_swap(send).astype(f32)
    return (residual.astype(f32) + jnp.tanh(attn_gate[0]) * mine).astype(bf16)


def solution(mesh):
    in_specs = (
        P(("groups", "seq"), "head"),
        P(("groups", "seq"), None),
        P("seq", "head"),
        P("seq", "head"),
        P("head", "seq"),
        P(("groups", "head"), "seq"),
        P(),
        P(),
        P(),
    )
    out_specs = P(("groups", "head"), "seq")
    sizes = tuple(mesh.shape[axis] for axis in AXES)
    return jax.shard_map(
        functools.partial(body, sizes),
        mesh=mesh,
        in_specs=in_specs,
        out_specs=out_specs,
        check_vma=False,
    )
```

```python
import functools

import jax
import jax.numpy as jnp
from jax import lax
from jax.experimental import pallas as pl
from jax.experimental.pallas import tpu as pltpu
from jax.sharding import PartitionSpec as P

HEAD_SIZE = 128
epsilon = 1e-05
AXES = ("groups", "seq", "head")
VMEM_BYTES = 48 * 1024 * 1024
f32, bf16 = jnp.float32, jnp.bfloat16


def pack_kernel(groups, pairs, part, count, index_ref, rows_ref, *outs):
    for g in range(groups):
        for y in range(2):
            starts = [((2 * z + y) * groups + g) * part for z in range(pairs)]
            for k, out in enumerate(outs):

                @pl.when(index_ref[k] == g * 2 + y)
                def _():
                    out[...] = jnp.concatenate(
                        [rows_ref[:, s : s + part] for s in starts], axis=1
                    )


def pack(vision, index, core, groups, pairs, part, name):
    rows, width = vision.shape
    half = rows // 2
    block = 32
    steps = half // block
    count = len(index)
    depth = pairs * part
    scalars = jnp.stack([*index, core]).astype(jnp.int32)
    return pl.pallas_call(
        functools.partial(pack_kernel, groups, pairs, part, count),
        grid_spec=pltpu.PrefetchScalarGridSpec(
            num_scalar_prefetch=1,
            grid=(steps,),
            in_specs=[pl.BlockSpec((block, width), lambda i, s: (s[count] * steps + i, 0))],
            out_specs=[pl.BlockSpec((block, depth), lambda i, s: (i, 0))] * count,
        ),
        out_shape=[jax.ShapeDtypeStruct((half, depth), vision.dtype)] * count,
        compiler_params=pltpu.CompilerParams(vmem_limit_bytes=VMEM_BYTES),
        name=name,
    )(scalars, vision)


def project_kernel(groups, pairs, shifts, matrix, scalars, *refs):
    count = groups * 2
    near, far, slabs = refs[:count], refs[count : 2 * count], refs[2 * count : -count - 1]
    outs, placed = refs[-count - 1 : -1], refs[-1]
    width = 2 * HEAD_SIZE
    columns = slice(matrix * width, (matrix + 1) * width)
    half = near[0].shape[0]
    side, place = scalars[0], scalars[1]
    for shift, slab in zip(shifts, slabs):
        if isinstance(shift, tuple):
            continue
        placed[lax.rem(place + pairs - shift, pairs)] = slab[:, columns]
    for shift, slab in zip(shifts, slabs):
        if isinstance(shift, tuple):

            @pl.when(place >= pairs // 2)
            def _():
                placed[lax.rem(place + pairs - shift[0], pairs)] = slab[:, columns]

    w = jnp.concatenate([placed[z] for z in range(pairs)], axis=0)
    for part, pieces in enumerate((near, far)):
        lhs = jnp.concatenate([ref[...] for ref in pieces], axis=0)
        result = jnp.dot(lhs, w, preferred_element_type=f32)
        first, second = result[:, :HEAD_SIZE], result[:, HEAD_SIZE:]
        heads = jnp.where(side == 0, first, second), jnp.where(side == 0, second, first)
        for source in range(count):
            by_group, by_side = source // 2, source % 2
            for to in range(2):
                out = outs[(-by_group) % groups * 2 + to]
                start = (0 if by_side == to else 2 * half) + part * half
                out[start : start + half, :] = heads[to][
                    source * half : (source + 1) * half, :
                ].astype(out.dtype)


def project(near, far, shifts, slabs, side, place, pairs, matrix, dtype, name):
    count = len(near)
    half = near[0].shape[0]
    vmem = pl.BlockSpec(memory_space=pltpu.VMEM)
    return pl.pallas_call(
        functools.partial(project_kernel, count // 2, pairs, shifts, matrix),
        in_specs=[pl.BlockSpec(memory_space=pltpu.SMEM)] + [vmem] * (2 * count + len(slabs)),
        out_specs=[vmem] * count,
        out_shape=[
            jax.ShapeDtypeStruct((4 * half, HEAD_SIZE), dtype if k else f32) for k in range(count)
        ],
        scratch_shapes=[pltpu.VMEM((pairs, slabs[0].shape[0], 2 * HEAD_SIZE), bf16)],
        compiler_params=pltpu.CompilerParams(vmem_limit_bytes=VMEM_BYTES),
        name=name,
    )(jnp.stack([side, place]).astype(jnp.int32), *near, *far, *slabs)


def score_kernel(heads, q_ref, *refs):
    keys, weights_ref, denominator_ref = refs[:-2], refs[-2], refs[-1]
    block = keys[0].shape[0]
    text = q_ref.shape[0] // heads
    for h in range(heads):
        rows = slice(h * text, (h + 1) * text)
        scores = [
            lax.dot_general(
                q_ref[rows, :], k[...], (((1,), (1,)), ((), ())), preferred_element_type=f32
            )
            * HEAD_SIZE ** (-0.5)
            for k in keys
        ]
        top = functools.reduce(
            jnp.maximum, [jnp.max(s, axis=-1, keepdims=True) for s in scores]
        )
        total = jnp.zeros_like(top)
        for n, s in enumerate(scores):
            weights = jnp.exp(s - top)
            total = total + jnp.sum(weights, axis=-1, keepdims=True)
            weights_ref[rows, n * block : (n + 1) * block] = weights.astype(bf16)
        denominator_ref[rows, :] = jnp.broadcast_to(total, (text, HEAD_SIZE))


def score(normed, keys, heads):
    rows = normed.shape[0]
    return pl.pallas_call(
        functools.partial(score_kernel, heads),
        out_shape=[
            jax.ShapeDtypeStruct((rows, len(keys) * keys[0].shape[0]), bf16),
            jax.ShapeDtypeStruct((rows, HEAD_SIZE), f32),
        ],
        compiler_params=pltpu.CompilerParams(vmem_limit_bytes=VMEM_BYTES),
        name="score",
    )(normed, *keys)


def mix_kernel(weights_ref, denominator_ref, *refs):
    values, out_ref = refs[:-1], refs[-1]
    text = out_ref.shape[0]
    v = jnp.concatenate([ref[...] for ref in values], axis=0)
    numerator = jnp.dot(weights_ref[...], v, preferred_element_type=f32)
    attended = (numerator / denominator_ref[...]).astype(bf16)
    for h in range(out_ref.shape[1] // HEAD_SIZE):
        out_ref[:, h * HEAD_SIZE : (h + 1) * HEAD_SIZE] = attended[h * text : (h + 1) * text, :]


def mix(weights, denominator, values, heads):
    rows = weights.shape[0]
    return pl.pallas_call(
        mix_kernel,
        out_shape=jax.ShapeDtypeStruct((rows // heads, heads * HEAD_SIZE), bf16),
        compiler_params=pltpu.CompilerParams(vmem_limit_bytes=VMEM_BYTES),
        name="mix",
    )(weights, denominator, *values)


def output_kernel(pairs, last, scalars, *refs):
    pieces, weight, placed = refs[:pairs], refs[pairs], refs[-1]
    place, core = scalars[1], scalars[2]
    for k, piece in enumerate(pieces):
        placed[lax.rem(place + pairs - k, pairs)] = piece[...]
    lhs = jnp.concatenate([placed[z] for z in range(pairs)], axis=0)
    product = jnp.dot(lhs, weight[...], preferred_element_type=f32)
    if not last:
        refs[pairs + 1][...] = product
        return
    total, mine, send = refs[pairs + 1 : pairs + 4]
    product = product + total[...]
    half = mine.shape[0]
    upper, lower = product[:half], product[half:]
    mine[...] = jnp.where(core == 0, upper, lower)
    send[...] = jnp.where(core == 0, lower, upper).astype(bf16)


def output(pieces, out_weight, side, place, core, total, name):
    pairs = len(pieces)
    text, depth = pieces[0].shape
    width = out_weight.shape[1]
    rows = pairs * text
    whole = lambda *shape: pl.BlockSpec(shape, lambda i, s: (0, 0))
    last = total is not None
    shapes = [(rows // 2, width, f32), (rows // 2, width, bf16)] if last else [(rows, width, f32)]
    return pl.pallas_call(
        functools.partial(output_kernel, pairs, last),
        grid_spec=pltpu.PrefetchScalarGridSpec(
            num_scalar_prefetch=1,
            grid=(1,),
            in_specs=[whole(text, depth)] * pairs
            + [pl.BlockSpec((depth, width), lambda i, s: (s[0], 0))]
            + ([whole(rows, width)] if last else []),
            out_specs=[whole(*shape[:2]) for shape in shapes],
            scratch_shapes=[pltpu.VMEM((pairs, text, depth), bf16)],
        ),
        out_shape=[jax.ShapeDtypeStruct(shape[:2], shape[2]) for shape in shapes],
        compiler_params=pltpu.CompilerParams(vmem_limit_bytes=VMEM_BYTES),
        name=name,
    )(
        jnp.stack([side, place, core]).astype(jnp.int32),
        *pieces,
        out_weight,
        *([total] if last else []),
    )


def after(array, *others):
    return lax.optimization_barrier((array, others))[0]


def norm(array, gain):
    mean = jnp.mean(array * array, axis=-1, keepdims=True)
    return (array * lax.rsqrt(mean + epsilon) * gain).astype(bf16)


def body(
    sizes,
    queries,
    vision,
    key_matrix,
    value_matrix,
    out_weight,
    residual,
    query_norm_gain,
    key_norm_gain,
    attn_gate,
):
    groups, seq, cores = sizes
    pairs = seq // 2
    group = lax.axis_index("groups")
    side = lax.axis_index("seq") % 2
    place = lax.axis_index("seq") // 2
    core = lax.axis_index("head")

    def permute(array, target):
        perm = []
        for g in range(groups):
            for z in range(pairs):
                for y in range(2):
                    for c in range(cores):
                        to = target(g, z, y, c)
                        if to is not None:
                            tg, tz, ty, tc = to
                            perm.append(
                                (
                                    (g * seq + z * 2 + y) * cores + c,
                                    (tg % groups * seq + tz % pairs * 2 + ty % 2) * cores
                                    + tc % cores,
                                )
                            )
        return lax.ppermute(array, AXES, perm)

    def plane_shift(array, by_group, by_side):
        return permute(array, lambda g, z, y, c: (g + by_group, z, y + by_side, c))

    def line_shift(array, by):
        return permute(array, lambda g, z, y, c: (g, z + by, y, c))

    def core_swap(array):
        return permute(array, lambda g, z, y, c: (g, z, y, c + 1))

    middle = pairs // 2 if pairs % 2 == 0 and pairs > 2 else 0

    def line_near(array):
        return {k: line_shift(array, k) for k in range(1, pairs) if k != middle}

    def line_far(pieces):
        if not middle:
            return []
        up = permute(
            pieces[middle - 1],
            lambda g, z, y, c: (g, z + 1, y, c) if middle <= z + 1 < pairs else None,
        )
        down = permute(
            pieces[middle + 1],
            lambda g, z, y, c: (g, z - 1, y, c) if 0 <= z - 1 < middle else None,
        )
        return [up, down]

    near_shifts = [k for k in range(1, pairs) if k != middle]
    shifts = [0] + near_shifts + ([middle, (middle,)] if middle else [])

    def line_slabs(own, pieces, far):
        return [own] + [pieces[k] for k in near_shifts] + far[::-1]

    def all_pairs(array):
        return [array] + [line_shift(array, k) for k in range(1, pairs)]

    offsets = [(g, y) for g in range(groups) for y in range(2)]

    part = key_matrix.shape[0] // groups

    def own_part(matrix):
        return lax.dynamic_slice_in_dim(matrix, group * part, part, axis=0)

    slab = jnp.concatenate([own_part(key_matrix), own_part(value_matrix)], axis=1)
    slab_near = line_near(slab)

    index = [(group + g) % groups * 2 + (side + y) % 2 for g, y in offsets]
    vision = after(vision, slab)
    sends = pack(vision, index[1:], core, groups, pairs, part, "pack_sends")
    received = [plane_shift(send, g, y) for send, (g, y) in zip(sends, offsets[1:])]
    vision = after(vision, *sends)
    near = pack(vision, index[:1], core, groups, pairs, part, "pack_near")
    far = pack(vision, index[:1], 1 - core, groups, pairs, part, "pack_far")

    rows_q = queries.shape[0]
    half_q = queries.shape[1] // 2
    heads = half_q // HEAD_SIZE
    queries = after(queries, far[0])
    q_own = lax.dynamic_slice_in_dim(queries, side * half_q, half_q, axis=1)
    q_send = lax.dynamic_slice_in_dim(queries, (1 - side) * half_q, half_q, axis=1)

    received = [after(piece, near[0], far[0]) for piece in received]
    near = [*near, *received]
    slab_far = line_far({k: after(s, near[0], far[0]) for k, s in slab_near.items()})
    far = [*far] + [core_swap(piece) for piece in received]

    def scatter(pieces):
        return [plane_shift(piece, g, y) for piece, (g, y) in zip(pieces[1:], offsets[1:])]

    def sum_up(own, pieces):
        return functools.reduce(lambda a, b: a + b.astype(f32), pieces, own)

    slabs = line_slabs(slab, slab_near, slab_far)
    key_pieces = project(near, far, shifts, slabs, side, place, pairs, 0, f32, "project_keys")
    key_parts = scatter(key_pieces)
    slabs[0] = after(slabs[0], *key_pieces)
    value_pieces = project(near, far, shifts, slabs, side, place, pairs, 1, bf16, "project_values")
    value_parts = scatter(value_pieces)
    keys = norm(sum_up(key_pieces[0], key_parts), key_norm_gain)
    all_keys = all_pairs(keys)
    q_recv = plane_shift(after(q_send, all_keys[1]), 0, 1)
    q_pair = jnp.where(
        side == 0,
        jnp.concatenate([q_own, q_recv], axis=0),
        jnp.concatenate([q_recv, q_own], axis=0),
    )
    q_heads = jnp.concatenate(
        [q_pair[:, h * HEAD_SIZE : (h + 1) * HEAD_SIZE] for h in range(heads)], axis=0
    )
    normed = norm(q_heads.astype(f32), query_norm_gain)
    value_parts = [after(v, all_keys[1]) for v in value_parts]
    values = sum_up(value_pieces[0], value_parts).astype(bf16)
    all_values = all_pairs(values)
    all_keys = [after(k, values) for k in all_keys]
    weights, denominator = score(normed, all_keys, heads)
    attended = mix(weights, denominator, all_values, heads)
    others = [plane_shift(attended, 0, 1)]
    own_pieces = [attended]
    order = sorted(range(1, pairs), key=lambda k: min(k, pairs - k))
    arrived = {k: line_shift(attended, k) for k in order}
    for last, k in zip(order, order[1:]):
        arrived[k] = after(arrived[k], arrived[last])
    passed = {k: plane_shift(arrived[k], 0, 1) for k in order}
    own_pieces += [arrived[k] for k in range(1, pairs)]
    others += [passed[k] for k in range(1, pairs)]
    (total,) = output(own_pieces, out_weight, side, place, core, None, "output_own")
    mine, send = output(others, out_weight, 1 - side, place, core, total, "output_other")
    mine = mine + core_swap(send).astype(f32)
    return (residual.astype(f32) + jnp.tanh(attn_gate[0]) * mine).astype(bf16)


def solution(mesh):
    in_specs = (
        P(("groups", "seq"), "head"),
        P(("groups", "seq"), None),
        P("seq", "head"),
        P("seq", "head"),
        P("head", "seq"),
        P(("groups", "head"), "seq"),
        P(),
        P(),
        P(),
    )
    out_specs = P(("groups", "head"), "seq")
    sizes = tuple(mesh.shape[axis] for axis in AXES)
    return jax.shard_map(
        functools.partial(body, sizes),
        mesh=mesh,
        in_specs=in_specs,
        out_specs=out_specs,
        check_vma=False,
    )
```

```python
import functools

import jax
import jax.numpy as jnp
from jax import lax
from jax.experimental import pallas as pl
from jax.experimental.pallas import tpu as pltpu
from jax.sharding import PartitionSpec as P

HEAD_SIZE = 128
epsilon = 1e-05
AXES = ("groups", "seq", "head")
VMEM_BYTES = 20 * 1024 * 1024
f32, bf16 = jnp.float32, jnp.bfloat16


def pack_kernel(groups, pairs, part, count, index_ref, rows_ref, *outs):
    for g in range(groups):
        for y in range(2):
            starts = [((2 * z + y) * groups + g) * part for z in range(pairs)]
            for k, out in enumerate(outs):

                @pl.when(index_ref[k] == g * 2 + y)
                def _():
                    out[...] = jnp.concatenate(
                        [rows_ref[:, s : s + part] for s in starts], axis=1
                    )


def pack(vision, index, core, groups, pairs, part, name):
    rows, width = vision.shape
    half = rows // 2
    block = 32
    steps = half // block
    count = len(index)
    depth = pairs * part
    scalars = jnp.stack([*index, core]).astype(jnp.int32)
    return pl.pallas_call(
        functools.partial(pack_kernel, groups, pairs, part, count),
        grid_spec=pltpu.PrefetchScalarGridSpec(
            num_scalar_prefetch=1,
            grid=(steps,),
            in_specs=[pl.BlockSpec((block, width), lambda i, s: (s[count] * steps + i, 0))],
            out_specs=[pl.BlockSpec((block, depth), lambda i, s: (i, 0))] * count,
        ),
        out_shape=[jax.ShapeDtypeStruct((half, depth), vision.dtype)] * count,
        compiler_params=pltpu.CompilerParams(vmem_limit_bytes=VMEM_BYTES),
        name=name,
    )(scalars, vision)


def project_kernel(groups, pairs, shifts, matrix, scalars, *refs):
    count = groups * 2
    near, far, slabs = refs[:count], refs[count : 2 * count], refs[2 * count : -count - 1]
    outs, placed = refs[-count - 1 : -1], refs[-1]
    width = 2 * HEAD_SIZE
    columns = slice(matrix * width, (matrix + 1) * width)
    half = near[0].shape[0]
    side, place = scalars[0], scalars[1]
    for shift, slab in zip(shifts, slabs):
        if isinstance(shift, tuple):
            continue
        placed[lax.rem(place + pairs - shift, pairs)] = slab[:, columns]
    for shift, slab in zip(shifts, slabs):
        if isinstance(shift, tuple):

            @pl.when(place >= pairs // 2)
            def _():
                placed[lax.rem(place + pairs - shift[0], pairs)] = slab[:, columns]

    w = jnp.concatenate([placed[z] for z in range(pairs)], axis=0)
    for part, pieces in enumerate((near, far)):
        lhs = jnp.concatenate([ref[...] for ref in pieces], axis=0)
        result = jnp.dot(lhs, w, preferred_element_type=f32)
        first, second = result[:, :HEAD_SIZE], result[:, HEAD_SIZE:]
        heads = jnp.where(side == 0, first, second), jnp.where(side == 0, second, first)
        for source in range(count):
            by_group, by_side = source // 2, source % 2
            for to in range(2):
                out = outs[(-by_group) % groups * 2 + to]
                start = (0 if by_side == to else 2 * half) + part * half
                out[start : start + half, :] = heads[to][
                    source * half : (source + 1) * half, :
                ].astype(out.dtype)


def project(near, far, shifts, slabs, side, place, pairs, matrix, dtype, name):
    count = len(near)
    half = near[0].shape[0]
    vmem = pl.BlockSpec(memory_space=pltpu.VMEM)
    return pl.pallas_call(
        functools.partial(project_kernel, count // 2, pairs, shifts, matrix),
        in_specs=[pl.BlockSpec(memory_space=pltpu.SMEM)] + [vmem] * (2 * count + len(slabs)),
        out_specs=[vmem] * count,
        out_shape=[
            jax.ShapeDtypeStruct((4 * half, HEAD_SIZE), dtype if k else f32) for k in range(count)
        ],
        scratch_shapes=[pltpu.VMEM((pairs, slabs[0].shape[0], 2 * HEAD_SIZE), bf16)],
        compiler_params=pltpu.CompilerParams(vmem_limit_bytes=VMEM_BYTES),
        name=name,
    )(jnp.stack([side, place]).astype(jnp.int32), *near, *far, *slabs)


def score_kernel(heads, q_ref, *refs):
    keys, weights_ref, denominator_ref = refs[:-2], refs[-2], refs[-1]
    block = keys[0].shape[0]
    text = q_ref.shape[0] // heads
    for h in range(heads):
        rows = slice(h * text, (h + 1) * text)
        scores = [
            lax.dot_general(
                q_ref[rows, :], k[...], (((1,), (1,)), ((), ())), preferred_element_type=f32
            )
            * HEAD_SIZE ** (-0.5)
            for k in keys
        ]
        top = functools.reduce(
            jnp.maximum, [jnp.max(s, axis=-1, keepdims=True) for s in scores]
        )
        total = jnp.zeros_like(top)
        for n, s in enumerate(scores):
            weights = jnp.exp(s - top)
            total = total + jnp.sum(weights, axis=-1, keepdims=True)
            weights_ref[rows, n * block : (n + 1) * block] = weights.astype(bf16)
        denominator_ref[rows, :] = jnp.broadcast_to(total, (text, HEAD_SIZE))


def score(normed, keys, heads):
    rows = normed.shape[0]
    return pl.pallas_call(
        functools.partial(score_kernel, heads),
        out_shape=[
            jax.ShapeDtypeStruct((rows, len(keys) * keys[0].shape[0]), bf16),
            jax.ShapeDtypeStruct((rows, HEAD_SIZE), f32),
        ],
        compiler_params=pltpu.CompilerParams(vmem_limit_bytes=VMEM_BYTES),
        name="score",
    )(normed, *keys)


def mix_kernel(weights_ref, denominator_ref, *refs):
    values, out_ref = refs[:-1], refs[-1]
    text = out_ref.shape[0]
    v = jnp.concatenate([ref[...] for ref in values], axis=0)
    numerator = jnp.dot(weights_ref[...], v, preferred_element_type=f32)
    attended = (numerator / denominator_ref[...]).astype(bf16)
    for h in range(out_ref.shape[1] // HEAD_SIZE):
        out_ref[:, h * HEAD_SIZE : (h + 1) * HEAD_SIZE] = attended[h * text : (h + 1) * text, :]


def mix(weights, denominator, values, heads):
    rows = weights.shape[0]
    return pl.pallas_call(
        mix_kernel,
        out_shape=jax.ShapeDtypeStruct((rows // heads, heads * HEAD_SIZE), bf16),
        compiler_params=pltpu.CompilerParams(vmem_limit_bytes=VMEM_BYTES),
        name="mix",
    )(weights, denominator, *values)


def own_kernel(scalars, *refs):
    pieces, weight, out = refs[:-2], refs[-2], refs[-1]
    depth = pieces[0].shape[1]
    rows = pl.ds(pl.multiple_of(scalars[0] * depth, depth), depth)
    lhs = jnp.concatenate([piece[...] for piece in pieces], axis=0)
    out[...] = jnp.dot(lhs, weight[rows, :], preferred_element_type=f32)


def own_output(pieces, out_weight, side, name):
    vmem = pl.BlockSpec(memory_space=pltpu.VMEM)
    rows = len(pieces) * pieces[0].shape[0]
    return pl.pallas_call(
        own_kernel,
        in_specs=[pl.BlockSpec(memory_space=pltpu.SMEM)] + [vmem] * (len(pieces) + 1),
        out_specs=vmem,
        out_shape=jax.ShapeDtypeStruct((rows, out_weight.shape[1]), f32),
        compiler_params=pltpu.CompilerParams(vmem_limit_bytes=VMEM_BYTES),
        name=name,
    )(jnp.stack([side]).astype(jnp.int32), *pieces, out_weight)


def other_kernel(shifts, scalars, *refs):
    pairs = len(shifts)
    pieces, weight, totals = refs[:pairs], refs[pairs], refs[pairs + 1 : -4]
    mine, send, placed, summed = refs[-4:]
    side, place, core = scalars[0], scalars[1], scalars[2]
    text, depth = pieces[0].shape
    for k, piece in enumerate(pieces):
        placed[lax.rem(place + pairs - k, pairs)] = piece[...]
    parts = [(ref, r) for ref in totals for r in range(0, ref.shape[0], text)]
    for k, (ref, r) in zip(shifts, parts):
        summed[lax.rem(place + pairs - k, pairs)] = ref[r : r + text, :]
    rows = pl.ds(pl.multiple_of(side * depth, depth), depth)
    half = pairs // 2
    for out, which in ((send, 1 - core), (mine, core)):
        base = which * half
        lhs = jnp.concatenate([placed[base + n] for n in range(half)], axis=0)
        own = jnp.concatenate([summed[base + n] for n in range(half)], axis=0)
        product = jnp.dot(lhs, weight[rows, :], preferred_element_type=f32)
        out[...] = (product + own).astype(out.dtype)


def other_output(pieces, out_weight, totals, shifts, side, place, core):
    vmem = pl.BlockSpec(memory_space=pltpu.VMEM)
    pairs = len(pieces)
    text, depth = pieces[0].shape
    width = out_weight.shape[1]
    rows = pairs * text // 2
    return pl.pallas_call(
        functools.partial(other_kernel, shifts),
        in_specs=[pl.BlockSpec(memory_space=pltpu.SMEM)] + [vmem] * (pairs + 1 + len(totals)),
        out_specs=[vmem] * 2,
        out_shape=[
            jax.ShapeDtypeStruct((rows, width), f32),
            jax.ShapeDtypeStruct((rows, width), bf16),
        ],
        scratch_shapes=[
            pltpu.VMEM((pairs, text, depth), bf16),
            pltpu.VMEM((pairs, text, width), f32),
        ],
        compiler_params=pltpu.CompilerParams(vmem_limit_bytes=VMEM_BYTES),
        name="output_other",
    )(jnp.stack([side, place, core]).astype(jnp.int32), *pieces, out_weight, *totals)


def after(array, *others):
    return lax.optimization_barrier((array, others))[0]


def norm(array, gain):
    mean = jnp.mean(array * array, axis=-1, keepdims=True)
    return (array * lax.rsqrt(mean + epsilon) * gain).astype(bf16)


def body(
    sizes,
    queries,
    vision,
    key_matrix,
    value_matrix,
    out_weight,
    residual,
    query_norm_gain,
    key_norm_gain,
    attn_gate,
):
    groups, seq, cores = sizes
    pairs = seq // 2
    group = lax.axis_index("groups")
    side = lax.axis_index("seq") % 2
    place = lax.axis_index("seq") // 2
    core = lax.axis_index("head")

    def permute(array, target):
        perm = []
        for g in range(groups):
            for z in range(pairs):
                for y in range(2):
                    for c in range(cores):
                        to = target(g, z, y, c)
                        if to is not None:
                            tg, tz, ty, tc = to
                            perm.append(
                                (
                                    (g * seq + z * 2 + y) * cores + c,
                                    (tg % groups * seq + tz % pairs * 2 + ty % 2) * cores
                                    + tc % cores,
                                )
                            )
        return lax.ppermute(array, AXES, perm)

    def plane_shift(array, by_group, by_side):
        return permute(array, lambda g, z, y, c: (g + by_group, z, y + by_side, c))

    def line_shift(array, by):
        return permute(array, lambda g, z, y, c: (g, z + by, y, c))

    def core_swap(array):
        return permute(array, lambda g, z, y, c: (g, z, y, c + 1))

    middle = pairs // 2 if pairs % 2 == 0 and pairs > 2 else 0

    def line_near(array):
        return {k: line_shift(array, k) for k in range(1, pairs) if k != middle}

    def line_far(pieces):
        if not middle:
            return []
        up = permute(
            pieces[middle - 1],
            lambda g, z, y, c: (g, z + 1, y, c) if middle <= z + 1 < pairs else None,
        )
        down = permute(
            pieces[middle + 1],
            lambda g, z, y, c: (g, z - 1, y, c) if 0 <= z - 1 < middle else None,
        )
        return [up, down]

    near_shifts = [k for k in range(1, pairs) if k != middle]
    shifts = [0] + near_shifts + ([middle, (middle,)] if middle else [])

    def line_slabs(own, pieces, far):
        return [own] + [pieces[k] for k in near_shifts] + far[::-1]

    def all_pairs(array):
        return [array] + [line_shift(array, k) for k in range(1, pairs)]

    offsets = [(g, y) for g in range(groups) for y in range(2)]

    part = key_matrix.shape[0] // groups

    def own_part(matrix):
        return lax.dynamic_slice_in_dim(matrix, group * part, part, axis=0)

    slab = jnp.concatenate([own_part(key_matrix), own_part(value_matrix)], axis=1)
    slab_near = line_near(slab)

    index = [(group + g) % groups * 2 + (side + y) % 2 for g, y in offsets]
    sends = pack(vision, index[1:], core, groups, pairs, part, "pack_sends")
    received = [plane_shift(send, g, y) for send, (g, y) in zip(sends, offsets[1:])]
    vision = after(vision, *sends)
    near = pack(vision, index[:1], core, groups, pairs, part, "pack_near")
    far = pack(vision, index[:1], 1 - core, groups, pairs, part, "pack_far")

    rows_q = queries.shape[0]
    half_q = queries.shape[1] // 2
    heads = half_q // HEAD_SIZE
    queries = after(queries, far[0])
    q_own = lax.dynamic_slice_in_dim(queries, side * half_q, half_q, axis=1)
    q_send = lax.dynamic_slice_in_dim(queries, (1 - side) * half_q, half_q, axis=1)

    received = [after(piece, near[0], far[0]) for piece in received]
    near = [*near, *received]
    slab_far = line_far({k: after(s, near[0], far[0]) for k, s in slab_near.items()})
    far = [*far] + [core_swap(piece) for piece in received]

    def scatter(pieces):
        return [plane_shift(piece, g, y) for piece, (g, y) in zip(pieces[1:], offsets[1:])]

    def sum_up(own, pieces):
        return functools.reduce(lambda a, b: a + b.astype(f32), pieces, own)

    slabs = line_slabs(slab, slab_near, slab_far)
    key_pieces = project(near, far, shifts, slabs, side, place, pairs, 0, f32, "project_keys")
    key_parts = scatter(key_pieces)
    slabs[0] = after(slabs[0], *key_pieces)
    value_pieces = project(near, far, shifts, slabs, side, place, pairs, 1, bf16, "project_values")
    value_parts = scatter(value_pieces)
    keys = norm(sum_up(key_pieces[0], key_parts), key_norm_gain)
    all_keys = all_pairs(keys)
    q_recv = plane_shift(after(q_send, all_keys[1]), 0, 1)
    q_pair = jnp.where(
        side == 0,
        jnp.concatenate([q_own, q_recv], axis=0),
        jnp.concatenate([q_recv, q_own], axis=0),
    )
    q_heads = jnp.concatenate(
        [q_pair[:, h * HEAD_SIZE : (h + 1) * HEAD_SIZE] for h in range(heads)], axis=0
    )
    normed = norm(q_heads.astype(f32), query_norm_gain)
    value_parts = [after(v, all_keys[1]) for v in value_parts]
    values = sum_up(value_pieces[0], value_parts).astype(bf16)
    all_values = all_pairs(values)
    all_keys = [after(k, values) for k in all_keys]
    weights, denominator = score(normed, all_keys, heads)
    attended = mix(weights, denominator, all_values, heads)
    passed = {0: plane_shift(attended, 0, 1)}
    arrived = {k: line_shift(attended, k) for k in range(1, pairs)}
    for k in near_shifts:
        passed[k] = plane_shift(after(arrived[k], passed[0]), 0, 1)
    totals = [
        own_output([attended, *(arrived[k] for k in near_shifts)], out_weight, side, "output_near")
    ]
    order = [0, *near_shifts]
    if middle:
        opposite = after(arrived[middle], totals[0], passed[near_shifts[0]])
        passed[middle] = plane_shift(opposite, 0, 1)
        totals.append(own_output([opposite], out_weight, side, "output_far"))
        order.append(middle)
    others = [passed[k] for k in range(pairs)]
    mine, send = other_output(others, out_weight, totals, order, 1 - side, place, core)
    mine = mine + core_swap(send).astype(f32)
    return (residual.astype(f32) + jnp.tanh(attn_gate[0]) * mine).astype(bf16)


def solution(mesh):
    in_specs = (
        P(("groups", "seq"), "head"),
        P(("groups", "seq"), None),
        P("seq", "head"),
        P("seq", "head"),
        P("head", "seq"),
        P(("groups", "head"), "seq"),
        P(),
        P(),
        P(),
    )
    out_specs = P(("groups", "head"), "seq")
    sizes = tuple(mesh.shape[axis] for axis in AXES)
    return jax.shard_map(
        functools.partial(body, sizes),
        mesh=mesh,
        in_specs=in_specs,
        out_specs=out_specs,
        check_vma=False,
    )
```

```python
import functools

import jax
import jax.numpy as jnp
from jax import lax
from jax.experimental import pallas as pl
from jax.experimental.pallas import tpu as pltpu
from jax.sharding import PartitionSpec as P

HEAD_SIZE = 128
epsilon = 1e-05
AXES = ("groups", "seq", "head")
VMEM_BYTES = 20 * 1024 * 1024
f32, bf16 = jnp.float32, jnp.bfloat16


def pack_kernel(groups, pairs, part, count, index_ref, rows_ref, *outs):
    for g in range(groups):
        for y in range(2):
            starts = [((2 * z + y) * groups + g) * part for z in range(pairs)]
            for k, out in enumerate(outs):

                @pl.when(index_ref[k] == g * 2 + y)
                def _():
                    out[...] = jnp.concatenate(
                        [rows_ref[:, s : s + part] for s in starts], axis=1
                    )


def pack(vision, index, core, groups, pairs, part, name):
    rows, width = vision.shape
    half = rows // 2
    block = 32
    steps = half // block
    count = len(index)
    depth = pairs * part
    scalars = jnp.stack([*index, core]).astype(jnp.int32)
    return pl.pallas_call(
        functools.partial(pack_kernel, groups, pairs, part, count),
        grid_spec=pltpu.PrefetchScalarGridSpec(
            num_scalar_prefetch=1,
            grid=(steps,),
            in_specs=[pl.BlockSpec((block, width), lambda i, s: (s[count] * steps + i, 0))],
            out_specs=[pl.BlockSpec((block, depth), lambda i, s: (i, 0))] * count,
        ),
        out_shape=[jax.ShapeDtypeStruct((half, depth), vision.dtype)] * count,
        compiler_params=pltpu.CompilerParams(vmem_limit_bytes=VMEM_BYTES),
        name=name,
    )(scalars, vision)


def project_kernel(groups, pairs, shifts, matrix, scalars, *refs):
    count = groups * 2
    slabs, near, far = refs[: -3 * count - 1], refs[-3 * count - 1 : -2 * count - 1], refs[-2 * count - 1 : -count - 1]
    outs, placed = refs[-count - 1 : -1], refs[-1]
    width = 2 * HEAD_SIZE
    columns = slice(matrix * width, (matrix + 1) * width)
    half = near[0].shape[0]
    side, place = scalars[0], scalars[1]
    for shift, slab in zip(shifts, slabs):
        if isinstance(shift, tuple):
            continue
        placed[lax.rem(place + pairs - shift, pairs)] = slab[:, columns]
    for shift, slab in zip(shifts, slabs):
        if isinstance(shift, tuple):

            @pl.when(place >= pairs // 2)
            def _():
                placed[lax.rem(place + pairs - shift[0], pairs)] = slab[:, columns]

    w = jnp.concatenate([placed[z] for z in range(pairs)], axis=0)
    for part, pieces in enumerate((near, far)):
        lhs = jnp.concatenate([ref[...] for ref in pieces], axis=0)
        result = jnp.dot(lhs, w, preferred_element_type=f32)
        first, second = result[:, :HEAD_SIZE], result[:, HEAD_SIZE:]
        heads = jnp.where(side == 0, first, second), jnp.where(side == 0, second, first)
        for source in range(count):
            by_group, by_side = source // 2, source % 2
            for to in range(2):
                out = outs[(-by_group) % groups * 2 + to]
                start = (0 if by_side == to else 2 * half) + part * half
                out[start : start + half, :] = heads[to][
                    source * half : (source + 1) * half, :
                ].astype(out.dtype)


def project(near, far, shifts, slabs, side, place, pairs, matrix, dtype, name):
    count = len(near)
    half = near[0].shape[0]
    vmem = pl.BlockSpec(memory_space=pltpu.VMEM)
    return pl.pallas_call(
        functools.partial(project_kernel, count // 2, pairs, shifts, matrix),
        in_specs=[pl.BlockSpec(memory_space=pltpu.SMEM)] + [vmem] * (2 * count + len(slabs)),
        out_specs=[vmem] * count,
        out_shape=[
            jax.ShapeDtypeStruct((4 * half, HEAD_SIZE), dtype if k else f32) for k in range(count)
        ],
        scratch_shapes=[pltpu.VMEM((pairs, slabs[0].shape[0], 2 * HEAD_SIZE), bf16)],
        compiler_params=pltpu.CompilerParams(vmem_limit_bytes=VMEM_BYTES),
        name=name,
    )(jnp.stack([side, place]).astype(jnp.int32), *slabs, *near, *far)


def score_kernel(heads, q_ref, *refs):
    keys, weights_ref, denominator_ref = refs[:-2], refs[-2], refs[-1]
    block = keys[0].shape[0]
    text = q_ref.shape[0] // heads
    for h in range(heads):
        rows = slice(h * text, (h + 1) * text)
        scores = [
            lax.dot_general(
                q_ref[rows, :], k[...], (((1,), (1,)), ((), ())), preferred_element_type=f32
            )
            * HEAD_SIZE ** (-0.5)
            for k in keys
        ]
        top = functools.reduce(
            jnp.maximum, [jnp.max(s, axis=-1, keepdims=True) for s in scores]
        )
        total = jnp.zeros_like(top)
        for n, s in enumerate(scores):
            weights = jnp.exp(s - top)
            total = total + jnp.sum(weights, axis=-1, keepdims=True)
            weights_ref[rows, n * block : (n + 1) * block] = weights.astype(bf16)
        denominator_ref[rows, :] = jnp.broadcast_to(total, (text, HEAD_SIZE))


def score(normed, keys, heads):
    rows = normed.shape[0]
    return pl.pallas_call(
        functools.partial(score_kernel, heads),
        out_shape=[
            jax.ShapeDtypeStruct((rows, len(keys) * keys[0].shape[0]), bf16),
            jax.ShapeDtypeStruct((rows, HEAD_SIZE), f32),
        ],
        compiler_params=pltpu.CompilerParams(vmem_limit_bytes=VMEM_BYTES),
        name="score",
    )(normed, *keys)


def mix_kernel(weights_ref, denominator_ref, *refs):
    values, out_ref = refs[:-1], refs[-1]
    text = out_ref.shape[0]
    v = jnp.concatenate([ref[...] for ref in values], axis=0)
    numerator = jnp.dot(weights_ref[...], v, preferred_element_type=f32)
    attended = (numerator / denominator_ref[...]).astype(bf16)
    for h in range(out_ref.shape[1] // HEAD_SIZE):
        out_ref[:, h * HEAD_SIZE : (h + 1) * HEAD_SIZE] = attended[h * text : (h + 1) * text, :]


def mix(weights, denominator, values, heads):
    rows = weights.shape[0]
    return pl.pallas_call(
        mix_kernel,
        out_shape=jax.ShapeDtypeStruct((rows // heads, heads * HEAD_SIZE), bf16),
        compiler_params=pltpu.CompilerParams(vmem_limit_bytes=VMEM_BYTES),
        name="mix",
    )(weights, denominator, *values)


def own_kernel(scalars, *refs):
    pieces, weight, out = refs[:-2], refs[-2], refs[-1]
    depth = pieces[0].shape[1]
    rows = pl.ds(pl.multiple_of(scalars[0] * depth, depth), depth)
    lhs = jnp.concatenate([piece[...] for piece in pieces], axis=0)
    out[...] = jnp.dot(lhs, weight[rows, :], preferred_element_type=f32)


def own_output(pieces, out_weight, side, name):
    vmem = pl.BlockSpec(memory_space=pltpu.VMEM)
    rows = len(pieces) * pieces[0].shape[0]
    return pl.pallas_call(
        own_kernel,
        in_specs=[pl.BlockSpec(memory_space=pltpu.SMEM)] + [vmem] * (len(pieces) + 1),
        out_specs=vmem,
        out_shape=jax.ShapeDtypeStruct((rows, out_weight.shape[1]), f32),
        compiler_params=pltpu.CompilerParams(vmem_limit_bytes=VMEM_BYTES),
        name=name,
    )(jnp.stack([side]).astype(jnp.int32), *pieces, out_weight)


def other_kernel(shifts, scalars, *refs):
    pairs = len(shifts)
    pieces, weight, totals = refs[:pairs], refs[pairs], refs[pairs + 1 : -4]
    mine, send, placed, summed = refs[-4:]
    side, place, core = scalars[0], scalars[1], scalars[2]
    text, depth = pieces[0].shape
    for k, piece in enumerate(pieces):
        placed[lax.rem(place + pairs - k, pairs)] = piece[...]
    parts = [(ref, r) for ref in totals for r in range(0, ref.shape[0], text)]
    for k, (ref, r) in zip(shifts, parts):
        summed[lax.rem(place + pairs - k, pairs)] = ref[r : r + text, :]
    rows = pl.ds(pl.multiple_of(side * depth, depth), depth)
    half = pairs // 2
    for out, which in ((send, 1 - core), (mine, core)):
        base = which * half
        lhs = jnp.concatenate([placed[base + n] for n in range(half)], axis=0)
        own = jnp.concatenate([summed[base + n] for n in range(half)], axis=0)
        product = jnp.dot(lhs, weight[rows, :], preferred_element_type=f32)
        out[...] = (product + own).astype(out.dtype)


def other_output(pieces, out_weight, totals, shifts, side, place, core):
    vmem = pl.BlockSpec(memory_space=pltpu.VMEM)
    pairs = len(pieces)
    text, depth = pieces[0].shape
    width = out_weight.shape[1]
    rows = pairs * text // 2
    return pl.pallas_call(
        functools.partial(other_kernel, shifts),
        in_specs=[pl.BlockSpec(memory_space=pltpu.SMEM)] + [vmem] * (pairs + 1 + len(totals)),
        out_specs=[vmem] * 2,
        out_shape=[
            jax.ShapeDtypeStruct((rows, width), f32),
            jax.ShapeDtypeStruct((rows, width), bf16),
        ],
        scratch_shapes=[
            pltpu.VMEM((pairs, text, depth), bf16),
            pltpu.VMEM((pairs, text, width), f32),
        ],
        compiler_params=pltpu.CompilerParams(vmem_limit_bytes=VMEM_BYTES),
        name="output_other",
    )(jnp.stack([side, place, core]).astype(jnp.int32), *pieces, out_weight, *totals)


def after(array, *others):
    return lax.optimization_barrier((array, others))[0]


def norm(array, gain):
    mean = jnp.mean(array * array, axis=-1, keepdims=True)
    return (array * lax.rsqrt(mean + epsilon) * gain).astype(bf16)


def body(
    sizes,
    queries,
    vision,
    key_matrix,
    value_matrix,
    out_weight,
    residual,
    query_norm_gain,
    key_norm_gain,
    attn_gate,
):
    groups, seq, cores = sizes
    pairs = seq // 2
    group = lax.axis_index("groups")
    side = lax.axis_index("seq") % 2
    place = lax.axis_index("seq") // 2
    core = lax.axis_index("head")

    def permute(array, target):
        perm = []
        for g in range(groups):
            for z in range(pairs):
                for y in range(2):
                    for c in range(cores):
                        to = target(g, z, y, c)
                        if to is not None:
                            tg, tz, ty, tc = to
                            perm.append(
                                (
                                    (g * seq + z * 2 + y) * cores + c,
                                    (tg % groups * seq + tz % pairs * 2 + ty % 2) * cores
                                    + tc % cores,
                                )
                            )
        return lax.ppermute(array, AXES, perm)

    def plane_shift(array, by_group, by_side):
        return permute(array, lambda g, z, y, c: (g + by_group, z, y + by_side, c))

    def line_shift(array, by):
        return permute(array, lambda g, z, y, c: (g, z + by, y, c))

    def core_swap(array):
        return permute(array, lambda g, z, y, c: (g, z, y, c + 1))

    middle = pairs // 2 if pairs % 2 == 0 and pairs > 2 else 0

    def line_near(array):
        return {k: line_shift(array, k) for k in range(1, pairs) if k != middle}

    def line_far(pieces):
        if not middle:
            return []
        up = permute(
            pieces[middle - 1],
            lambda g, z, y, c: (g, z + 1, y, c) if middle <= z + 1 < pairs else None,
        )
        down = permute(
            pieces[middle + 1],
            lambda g, z, y, c: (g, z - 1, y, c) if 0 <= z - 1 < middle else None,
        )
        return [up, down]

    near_shifts = [k for k in range(1, pairs) if k != middle]
    shifts = [0] + near_shifts + ([middle, (middle,)] if middle else [])

    def line_slabs(own, pieces, far):
        return [own] + [pieces[k] for k in near_shifts] + far[::-1]

    def all_pairs(array):
        return [array] + [line_shift(array, k) for k in range(1, pairs)]

    offsets = [(g, y) for g in range(groups) for y in range(2)]

    part = key_matrix.shape[0] // groups

    def own_part(matrix):
        return lax.dynamic_slice_in_dim(matrix, group * part, part, axis=0)

    slab = jnp.concatenate([own_part(key_matrix), own_part(value_matrix)], axis=1)
    slab_near = line_near(slab)

    index = [(group + g) % groups * 2 + (side + y) % 2 for g, y in offsets]
    sends = pack(vision, index[1:], core, groups, pairs, part, "pack_sends")
    received = [plane_shift(send, g, y) for send, (g, y) in zip(sends, offsets[1:])]
    vision = after(vision, *sends)
    near = pack(vision, index[:1], core, groups, pairs, part, "pack_near")
    far = pack(vision, index[:1], 1 - core, groups, pairs, part, "pack_far")

    rows_q = queries.shape[0]
    half_q = queries.shape[1] // 2
    heads = half_q // HEAD_SIZE
    queries = after(queries, far[0])
    q_own = lax.dynamic_slice_in_dim(queries, side * half_q, half_q, axis=1)
    q_send = lax.dynamic_slice_in_dim(queries, (1 - side) * half_q, half_q, axis=1)

    received = [after(piece, near[0], far[0]) for piece in received]
    near = [*near, *received]
    slab_far = line_far({k: after(s, near[0], far[0]) for k, s in slab_near.items()})
    far = [*far] + [core_swap(piece) for piece in received]

    def scatter(pieces):
        return [plane_shift(piece, g, y) for piece, (g, y) in zip(pieces[1:], offsets[1:])]

    def sum_up(own, pieces):
        return functools.reduce(lambda a, b: a + b.astype(f32), pieces, own)

    slabs = line_slabs(slab, slab_near, slab_far)
    value_pieces = project(near, far, shifts, slabs, side, place, pairs, 1, bf16, "project_values")
    value_parts = scatter(value_pieces)
    slabs[0] = after(slabs[0], *value_pieces)
    key_pieces = project(near, far, shifts, slabs, side, place, pairs, 0, f32, "project_keys")
    key_parts = scatter(key_pieces)
    values = sum_up(value_pieces[0], value_parts).astype(bf16)
    all_values = all_pairs(values)
    key_parts = [after(k, all_values[1]) for k in key_parts]
    q_recv = plane_shift(after(q_send, all_values[1]), 0, 1)
    q_pair = jnp.where(
        side == 0,
        jnp.concatenate([q_own, q_recv], axis=0),
        jnp.concatenate([q_recv, q_own], axis=0),
    )
    q_heads = jnp.concatenate(
        [q_pair[:, h * HEAD_SIZE : (h + 1) * HEAD_SIZE] for h in range(heads)], axis=0
    )
    normed = norm(q_heads.astype(f32), query_norm_gain)
    keys = norm(sum_up(key_pieces[0], key_parts), key_norm_gain)
    all_keys = all_pairs(keys)
    weights, denominator = score(normed, all_keys, heads)
    attended = mix(weights, denominator, all_values, heads)
    passed = {0: plane_shift(attended, 0, 1)}
    arrived = {k: line_shift(attended, k) for k in range(1, pairs)}
    for k in near_shifts:
        passed[k] = plane_shift(after(arrived[k], passed[0]), 0, 1)
    totals = [
        own_output([attended, *(arrived[k] for k in near_shifts)], out_weight, side, "output_near")
    ]
    order = [0, *near_shifts]
    if middle:
        opposite = after(arrived[middle], totals[0], passed[near_shifts[0]])
        passed[middle] = plane_shift(opposite, 0, 1)
        totals.append(own_output([opposite], out_weight, side, "output_far"))
        order.append(middle)
    others = [passed[k] for k in range(pairs)]
    mine, send = other_output(others, out_weight, totals, order, 1 - side, place, core)
    mine = mine + core_swap(send).astype(f32)
    return (residual.astype(f32) + jnp.tanh(attn_gate[0]) * mine).astype(bf16)


def solution(mesh):
    in_specs = (
        P(("groups", "seq"), "head"),
        P(("groups", "seq"), None),
        P("seq", "head"),
        P("seq", "head"),
        P("head", "seq"),
        P(("groups", "head"), "seq"),
        P(),
        P(),
        P(),
    )
    out_specs = P(("groups", "head"), "seq")
    sizes = tuple(mesh.shape[axis] for axis in AXES)
    return jax.shard_map(
        functools.partial(body, sizes),
        mesh=mesh,
        in_specs=in_specs,
        out_specs=out_specs,
        check_vma=False,
    )
```

```python
import functools

import jax
import jax.numpy as jnp
from jax import lax
from jax.experimental import pallas as pl
from jax.experimental.pallas import tpu as pltpu
from jax.sharding import PartitionSpec as P

HEAD_SIZE = 128
epsilon = 1e-05
AXES = ("groups", "seq", "head")
VMEM_BYTES = 20 * 1024 * 1024
f32, bf16 = jnp.float32, jnp.bfloat16


def pack_kernel(groups, pairs, part, count, index_ref, rows_ref, *outs):
    for g in range(groups):
        for y in range(2):
            starts = [((2 * z + y) * groups + g) * part for z in range(pairs)]
            for k, out in enumerate(outs):

                @pl.when(index_ref[k] == g * 2 + y)
                def _():
                    out[...] = jnp.concatenate(
                        [rows_ref[:, s : s + part] for s in starts], axis=1
                    )


def pack(vision, index, core, groups, pairs, part, name):
    rows, width = vision.shape
    half = rows // 2
    block = 32
    steps = half // block
    count = len(index)
    depth = pairs * part
    scalars = jnp.stack([*index, core]).astype(jnp.int32)
    return pl.pallas_call(
        functools.partial(pack_kernel, groups, pairs, part, count),
        grid_spec=pltpu.PrefetchScalarGridSpec(
            num_scalar_prefetch=1,
            grid=(steps,),
            in_specs=[pl.BlockSpec((block, width), lambda i, s: (s[count] * steps + i, 0))],
            out_specs=[pl.BlockSpec((block, depth), lambda i, s: (i, 0))] * count,
        ),
        out_shape=[jax.ShapeDtypeStruct((half, depth), vision.dtype)] * count,
        compiler_params=pltpu.CompilerParams(vmem_limit_bytes=VMEM_BYTES),
        name=name,
    )(scalars, vision)


def project_kernel(groups, pairs, shifts, scalars, *refs):
    count = groups * 2
    near, far, slabs = refs[:count], refs[count : 2 * count], refs[2 * count : -2 * count - 1]
    outs, placed = refs[-2 * count - 1 : -1], refs[-1]
    half = near[0].shape[0]
    side, place = scalars[0], scalars[1]
    for shift, slab in zip(shifts, slabs):
        if isinstance(shift, tuple):
            continue
        placed[lax.rem(place + pairs - shift, pairs)] = slab[...]
    for shift, slab in zip(shifts, slabs):
        if isinstance(shift, tuple):

            @pl.when(place >= pairs // 2)
            def _():
                placed[lax.rem(place + pairs - shift[0], pairs)] = slab[...]

    w = jnp.concatenate([placed[z] for z in range(pairs)], axis=0)
    for part, pieces in enumerate((near, far)):
        lhs = jnp.concatenate([ref[...] for ref in pieces], axis=0)
        result = jnp.dot(lhs, w, preferred_element_type=f32)
        columns = [result[:, n * HEAD_SIZE : (n + 1) * HEAD_SIZE] for n in range(4)]
        for matrix in range(2):
            first, second = columns[2 * matrix : 2 * matrix + 2]
            heads = jnp.where(side == 0, first, second), jnp.where(side == 0, second, first)
            for source in range(count):
                by_group, by_side = source // 2, source % 2
                for to in range(2):
                    out = outs[matrix * count + (-by_group) % groups * 2 + to]
                    start = (0 if by_side == to else 2 * half) + part * half
                    out[start : start + half, :] = heads[to][
                        source * half : (source + 1) * half, :
                    ].astype(out.dtype)


def project(near, far, shifts, slabs, side, place, pairs):
    count = len(near)
    half = near[0].shape[0]
    vmem = pl.BlockSpec(memory_space=pltpu.VMEM)
    return pl.pallas_call(
        functools.partial(project_kernel, count // 2, pairs, shifts),
        in_specs=[pl.BlockSpec(memory_space=pltpu.SMEM)] + [vmem] * (2 * count + len(slabs)),
        out_specs=[vmem] * (2 * count),
        out_shape=[
            jax.ShapeDtypeStruct((4 * half, HEAD_SIZE), bf16 if k > count else f32)
            for k in range(2 * count)
        ],
        scratch_shapes=[pltpu.VMEM((pairs,) + slabs[0].shape, bf16)],
        compiler_params=pltpu.CompilerParams(vmem_limit_bytes=VMEM_BYTES),
        name="project",
    )(jnp.stack([side, place]).astype(jnp.int32), *near, *far, *slabs)


def score_kernel(heads, q_ref, *refs):
    keys, weights_ref, denominator_ref = refs[:-2], refs[-2], refs[-1]
    block = keys[0].shape[0]
    text = q_ref.shape[0] // heads
    for h in range(heads):
        rows = slice(h * text, (h + 1) * text)
        scores = [
            lax.dot_general(
                q_ref[rows, :], k[...], (((1,), (1,)), ((), ())), preferred_element_type=f32
            )
            * HEAD_SIZE ** (-0.5)
            for k in keys
        ]
        top = functools.reduce(
            jnp.maximum, [jnp.max(s, axis=-1, keepdims=True) for s in scores]
        )
        total = jnp.zeros_like(top)
        for n, s in enumerate(scores):
            weights = jnp.exp(s - top)
            total = total + jnp.sum(weights, axis=-1, keepdims=True)
            weights_ref[rows, n * block : (n + 1) * block] = weights.astype(bf16)
        denominator_ref[rows, :] = jnp.broadcast_to(total, (text, HEAD_SIZE))


def score(normed, keys, heads):
    rows = normed.shape[0]
    return pl.pallas_call(
        functools.partial(score_kernel, heads),
        out_shape=[
            jax.ShapeDtypeStruct((rows, len(keys) * keys[0].shape[0]), bf16),
            jax.ShapeDtypeStruct((rows, HEAD_SIZE), f32),
        ],
        compiler_params=pltpu.CompilerParams(vmem_limit_bytes=VMEM_BYTES),
        name="score",
    )(normed, *keys)


def mix_kernel(weights_ref, denominator_ref, *refs):
    values, out_ref = refs[:-1], refs[-1]
    text = out_ref.shape[0]
    v = jnp.concatenate([ref[...] for ref in values], axis=0)
    numerator = jnp.dot(weights_ref[...], v, preferred_element_type=f32)
    attended = (numerator / denominator_ref[...]).astype(bf16)
    for h in range(out_ref.shape[1] // HEAD_SIZE):
        out_ref[:, h * HEAD_SIZE : (h + 1) * HEAD_SIZE] = attended[h * text : (h + 1) * text, :]


def mix(weights, denominator, values, heads):
    rows = weights.shape[0]
    return pl.pallas_call(
        mix_kernel,
        out_shape=jax.ShapeDtypeStruct((rows // heads, heads * HEAD_SIZE), bf16),
        compiler_params=pltpu.CompilerParams(vmem_limit_bytes=VMEM_BYTES),
        name="mix",
    )(weights, denominator, *values)


def own_kernel(scalars, *refs):
    pieces, weight, out = refs[:-2], refs[-2], refs[-1]
    depth = pieces[0].shape[1]
    rows = pl.ds(pl.multiple_of(scalars[0] * depth, depth), depth)
    lhs = jnp.concatenate([piece[...] for piece in pieces], axis=0)
    out[...] = jnp.dot(lhs, weight[rows, :], preferred_element_type=f32)


def own_output(pieces, out_weight, side, name):
    vmem = pl.BlockSpec(memory_space=pltpu.VMEM)
    rows = len(pieces) * pieces[0].shape[0]
    return pl.pallas_call(
        own_kernel,
        in_specs=[pl.BlockSpec(memory_space=pltpu.SMEM)] + [vmem] * (len(pieces) + 1),
        out_specs=vmem,
        out_shape=jax.ShapeDtypeStruct((rows, out_weight.shape[1]), f32),
        compiler_params=pltpu.CompilerParams(vmem_limit_bytes=VMEM_BYTES),
        name=name,
    )(jnp.stack([side]).astype(jnp.int32), *pieces, out_weight)


def other_kernel(shifts, scalars, *refs):
    pairs = len(shifts)
    pieces, weight, totals = refs[:pairs], refs[pairs], refs[pairs + 1 : -4]
    mine, send, placed, summed = refs[-4:]
    side, place, core = scalars[0], scalars[1], scalars[2]
    text, depth = pieces[0].shape
    for k, piece in enumerate(pieces):
        placed[lax.rem(place + pairs - k, pairs)] = piece[...]
    parts = [(ref, r) for ref in totals for r in range(0, ref.shape[0], text)]
    for k, (ref, r) in zip(shifts, parts):
        summed[lax.rem(place + pairs - k, pairs)] = ref[r : r + text, :]
    rows = pl.ds(pl.multiple_of(side * depth, depth), depth)
    half = pairs // 2
    for out, which in ((send, 1 - core), (mine, core)):
        base = which * half
        lhs = jnp.concatenate([placed[base + n] for n in range(half)], axis=0)
        own = jnp.concatenate([summed[base + n] for n in range(half)], axis=0)
        product = jnp.dot(lhs, weight[rows, :], preferred_element_type=f32)
        out[...] = (product + own).astype(out.dtype)


def other_output(pieces, out_weight, totals, shifts, side, place, core):
    vmem = pl.BlockSpec(memory_space=pltpu.VMEM)
    pairs = len(pieces)
    text, depth = pieces[0].shape
    width = out_weight.shape[1]
    rows = pairs * text // 2
    return pl.pallas_call(
        functools.partial(other_kernel, shifts),
        in_specs=[pl.BlockSpec(memory_space=pltpu.SMEM)] + [vmem] * (pairs + 1 + len(totals)),
        out_specs=[vmem] * 2,
        out_shape=[
            jax.ShapeDtypeStruct((rows, width), f32),
            jax.ShapeDtypeStruct((rows, width), bf16),
        ],
        scratch_shapes=[
            pltpu.VMEM((pairs, text, depth), bf16),
            pltpu.VMEM((pairs, text, width), f32),
        ],
        compiler_params=pltpu.CompilerParams(vmem_limit_bytes=VMEM_BYTES),
        name="output_other",
    )(jnp.stack([side, place, core]).astype(jnp.int32), *pieces, out_weight, *totals)


def after(array, *others):
    return lax.optimization_barrier((array, others))[0]


def norm(array, gain):
    mean = jnp.mean(array * array, axis=-1, keepdims=True)
    return (array * lax.rsqrt(mean + epsilon) * gain).astype(bf16)


def body(
    sizes,
    queries,
    vision,
    key_matrix,
    value_matrix,
    out_weight,
    residual,
    query_norm_gain,
    key_norm_gain,
    attn_gate,
):
    groups, seq, cores = sizes
    pairs = seq // 2
    group = lax.axis_index("groups")
    side = lax.axis_index("seq") % 2
    place = lax.axis_index("seq") // 2
    core = lax.axis_index("head")

    def permute(array, target):
        perm = []
        for g in range(groups):
            for z in range(pairs):
                for y in range(2):
                    for c in range(cores):
                        to = target(g, z, y, c)
                        if to is not None:
                            tg, tz, ty, tc = to
                            perm.append(
                                (
                                    (g * seq + z * 2 + y) * cores + c,
                                    (tg % groups * seq + tz % pairs * 2 + ty % 2) * cores
                                    + tc % cores,
                                )
                            )
        return lax.ppermute(array, AXES, perm)

    def plane_shift(array, by_group, by_side):
        return permute(array, lambda g, z, y, c: (g + by_group, z, y + by_side, c))

    def line_shift(array, by):
        return permute(array, lambda g, z, y, c: (g, z + by, y, c))

    def core_swap(array):
        return permute(array, lambda g, z, y, c: (g, z, y, c + 1))

    middle = pairs // 2 if pairs % 2 == 0 and pairs > 2 else 0

    def line_near(array):
        return {k: line_shift(array, k) for k in range(1, pairs) if k != middle}

    def line_far(pieces):
        if not middle:
            return []
        up = permute(
            pieces[middle - 1],
            lambda g, z, y, c: (g, z + 1, y, c) if middle <= z + 1 < pairs else None,
        )
        down = permute(
            pieces[middle + 1],
            lambda g, z, y, c: (g, z - 1, y, c) if 0 <= z - 1 < middle else None,
        )
        return [up, down]

    near_shifts = [k for k in range(1, pairs) if k != middle]
    shifts = [0] + near_shifts + ([middle, (middle,)] if middle else [])

    def line_slabs(own, pieces, far):
        return [own] + [pieces[k] for k in near_shifts] + far[::-1]

    def all_pairs(array):
        return [array] + [line_shift(array, k) for k in range(1, pairs)]

    offsets = [(g, y) for g in range(groups) for y in range(2)]

    part = key_matrix.shape[0] // groups

    def own_part(matrix):
        return lax.dynamic_slice_in_dim(matrix, group * part, part, axis=0)

    slab = jnp.concatenate([own_part(key_matrix), own_part(value_matrix)], axis=1)
    slab_near = line_near(slab)

    index = [(group + g) % groups * 2 + (side + y) % 2 for g, y in offsets]
    sends = pack(vision, index[1:], core, groups, pairs, part, "pack_sends")
    received = [plane_shift(send, g, y) for send, (g, y) in zip(sends, offsets[1:])]
    vision = after(vision, *sends)
    near = pack(vision, index[:1], core, groups, pairs, part, "pack_near")
    far = pack(vision, index[:1], 1 - core, groups, pairs, part, "pack_far")

    rows_q = queries.shape[0]
    half_q = queries.shape[1] // 2
    heads = half_q // HEAD_SIZE
    queries = after(queries, far[0])
    q_own = lax.dynamic_slice_in_dim(queries, side * half_q, half_q, axis=1)
    q_send = lax.dynamic_slice_in_dim(queries, (1 - side) * half_q, half_q, axis=1)

    received = [after(piece, near[0], far[0]) for piece in received]
    near = [*near, *received]
    slab_far = line_far({k: after(s, near[0], far[0]) for k, s in slab_near.items()})
    far = [*far] + [core_swap(piece) for piece in received]

    def scatter(pieces):
        return [plane_shift(piece, g, y) for piece, (g, y) in zip(pieces[1:], offsets[1:])]

    def sum_up(own, pieces):
        return functools.reduce(lambda a, b: a + b.astype(f32), pieces, own)

    slabs = line_slabs(slab, slab_near, slab_far)
    pieces = project(near, far, shifts, slabs, side, place, pairs)
    key_pieces, value_pieces = pieces[: len(offsets)], pieces[len(offsets) :]
    value_parts = scatter(value_pieces)
    key_parts = scatter(key_pieces)
    values = sum_up(value_pieces[0], value_parts).astype(bf16)
    all_values = all_pairs(values)
    key_parts = [after(k, all_values[1]) for k in key_parts]
    q_recv = plane_shift(after(q_send, all_values[1]), 0, 1)
    q_pair = jnp.where(
        side == 0,
        jnp.concatenate([q_own, q_recv], axis=0),
        jnp.concatenate([q_recv, q_own], axis=0),
    )
    q_heads = jnp.concatenate(
        [q_pair[:, h * HEAD_SIZE : (h + 1) * HEAD_SIZE] for h in range(heads)], axis=0
    )
    normed = norm(q_heads.astype(f32), query_norm_gain)
    keys = norm(sum_up(key_pieces[0], key_parts), key_norm_gain)
    all_keys = all_pairs(keys)
    weights, denominator = score(normed, all_keys, heads)
    attended = mix(weights, denominator, all_values, heads)
    passed = {0: plane_shift(attended, 0, 1)}
    arrived = {k: line_shift(attended, k) for k in range(1, pairs)}
    for k in near_shifts:
        passed[k] = plane_shift(after(arrived[k], passed[0]), 0, 1)
    totals = [
        own_output([attended, *(arrived[k] for k in near_shifts)], out_weight, side, "output_near")
    ]
    order = [0, *near_shifts]
    if middle:
        opposite = after(arrived[middle], totals[0], passed[near_shifts[0]])
        passed[middle] = plane_shift(opposite, 0, 1)
        totals.append(own_output([opposite], out_weight, side, "output_far"))
        order.append(middle)
    others = [passed[k] for k in range(pairs)]
    mine, send = other_output(others, out_weight, totals, order, 1 - side, place, core)
    mine = mine + core_swap(send).astype(f32)
    return (residual.astype(f32) + jnp.tanh(attn_gate[0]) * mine).astype(bf16)


def solution(mesh):
    in_specs = (
        P(("groups", "seq"), "head"),
        P(("groups", "seq"), None),
        P("seq", "head"),
        P("seq", "head"),
        P("head", "seq"),
        P(("groups", "head"), "seq"),
        P(),
        P(),
        P(),
    )
    out_specs = P(("groups", "head"), "seq")
    sizes = tuple(mesh.shape[axis] for axis in AXES)
    return jax.shard_map(
        functools.partial(body, sizes),
        mesh=mesh,
        in_specs=in_specs,
        out_specs=out_specs,
        check_vma=False,
    )
```

```python
import functools

import jax
import jax.numpy as jnp
from jax import lax
from jax.experimental import pallas as pl
from jax.experimental.pallas import tpu as pltpu
from jax.sharding import PartitionSpec as P

HEAD_SIZE = 128
epsilon = 1e-05
AXES = ("groups", "seq", "head")
VMEM_BYTES = 20 * 1024 * 1024
f32, bf16 = jnp.float32, jnp.bfloat16


def pack_kernel(groups, pairs, part, count, index_ref, rows_ref, *outs):
    for g in range(groups):
        for y in range(2):
            starts = [((2 * z + y) * groups + g) * part for z in range(pairs)]
            for k, out in enumerate(outs):

                @pl.when(index_ref[k] == g * 2 + y)
                def _():
                    out[...] = jnp.concatenate(
                        [rows_ref[:, s : s + part] for s in starts], axis=1
                    )


def pack(vision, index, core, groups, pairs, part, name):
    rows, width = vision.shape
    half = rows // 2
    block = 32
    steps = half // block
    count = len(index)
    depth = pairs * part
    scalars = jnp.stack([*index, core]).astype(jnp.int32)
    return pl.pallas_call(
        functools.partial(pack_kernel, groups, pairs, part, count),
        grid_spec=pltpu.PrefetchScalarGridSpec(
            num_scalar_prefetch=1,
            grid=(steps,),
            in_specs=[pl.BlockSpec((block, width), lambda i, s: (s[count] * steps + i, 0))],
            out_specs=[pl.BlockSpec((block, depth), lambda i, s: (i, 0))] * count,
        ),
        out_shape=[jax.ShapeDtypeStruct((half, depth), vision.dtype)] * count,
        compiler_params=pltpu.CompilerParams(vmem_limit_bytes=VMEM_BYTES),
        name=name,
    )(scalars, vision)


def project_kernel(groups, pairs, shifts, scalars, *refs):
    count = groups * 2
    near, far, slabs = refs[:count], refs[count : 2 * count], refs[2 * count : -2 * count - 1]
    outs, placed = refs[-2 * count - 1 : -1], refs[-1]
    half = near[0].shape[0]
    side, place = scalars[0], scalars[1]
    for shift, slab in zip(shifts, slabs):
        if isinstance(shift, tuple):
            continue
        placed[lax.rem(place + pairs - shift, pairs)] = slab[...]
    for shift, slab in zip(shifts, slabs):
        if isinstance(shift, tuple):

            @pl.when(place >= pairs // 2)
            def _():
                placed[lax.rem(place + pairs - shift[0], pairs)] = slab[...]

    w = jnp.concatenate([placed[z] for z in range(pairs)], axis=0)
    for part, pieces in enumerate((near, far)):
        lhs = jnp.concatenate([ref[...] for ref in pieces], axis=0)
        result = jnp.dot(lhs, w, preferred_element_type=f32)
        columns = [result[:, n * HEAD_SIZE : (n + 1) * HEAD_SIZE] for n in range(4)]
        for matrix in range(2):
            first, second = columns[2 * matrix : 2 * matrix + 2]
            heads = jnp.where(side == 0, first, second), jnp.where(side == 0, second, first)
            for source in range(count):
                by_group, by_side = source // 2, source % 2
                for to in range(2):
                    out = outs[matrix * count + (-by_group) % groups * 2 + to]
                    start = (0 if by_side == to else 2 * half) + part * half
                    out[start : start + half, :] = heads[to][
                        source * half : (source + 1) * half, :
                    ].astype(out.dtype)


def project(near, far, shifts, slabs, side, place, pairs):
    count = len(near)
    half = near[0].shape[0]
    vmem = pl.BlockSpec(memory_space=pltpu.VMEM)
    return pl.pallas_call(
        functools.partial(project_kernel, count // 2, pairs, shifts),
        in_specs=[pl.BlockSpec(memory_space=pltpu.SMEM)] + [vmem] * (2 * count + len(slabs)),
        out_specs=[vmem] * (2 * count),
        out_shape=[
            jax.ShapeDtypeStruct((4 * half, HEAD_SIZE), bf16 if k > count else f32)
            for k in range(2 * count)
        ],
        scratch_shapes=[pltpu.VMEM((pairs,) + slabs[0].shape, bf16)],
        compiler_params=pltpu.CompilerParams(vmem_limit_bytes=VMEM_BYTES),
        name="project",
    )(jnp.stack([side, place]).astype(jnp.int32), *near, *far, *slabs)


def score_kernel(heads, q_ref, *refs):
    keys, weights_ref, denominator_ref = refs[:-2], refs[-2], refs[-1]
    block = keys[0].shape[0]
    text = q_ref.shape[0] // heads
    for h in range(heads):
        rows = slice(h * text, (h + 1) * text)
        scores = [
            lax.dot_general(
                q_ref[rows, :], k[...], (((1,), (1,)), ((), ())), preferred_element_type=f32
            )
            * HEAD_SIZE ** (-0.5)
            for k in keys
        ]
        top = functools.reduce(
            jnp.maximum, [jnp.max(s, axis=-1, keepdims=True) for s in scores]
        )
        total = jnp.zeros_like(top)
        for n, s in enumerate(scores):
            weights = jnp.exp(s - top)
            total = total + jnp.sum(weights, axis=-1, keepdims=True)
            weights_ref[rows, n * block : (n + 1) * block] = weights.astype(bf16)
        denominator_ref[rows, :] = jnp.broadcast_to(total, (text, HEAD_SIZE))


def score(normed, keys, heads):
    rows = normed.shape[0]
    return pl.pallas_call(
        functools.partial(score_kernel, heads),
        out_shape=[
            jax.ShapeDtypeStruct((rows, len(keys) * keys[0].shape[0]), bf16),
            jax.ShapeDtypeStruct((rows, HEAD_SIZE), f32),
        ],
        compiler_params=pltpu.CompilerParams(vmem_limit_bytes=VMEM_BYTES),
        name="score",
    )(normed, *keys)


def mix_kernel(weights_ref, denominator_ref, *refs):
    values, out_ref = refs[:-1], refs[-1]
    text = out_ref.shape[0]
    v = jnp.concatenate([ref[...] for ref in values], axis=0)
    numerator = jnp.dot(weights_ref[...], v, preferred_element_type=f32)
    attended = (numerator / denominator_ref[...]).astype(bf16)
    for h in range(out_ref.shape[1] // HEAD_SIZE):
        out_ref[:, h * HEAD_SIZE : (h + 1) * HEAD_SIZE] = attended[h * text : (h + 1) * text, :]


def mix(weights, denominator, values, heads):
    rows = weights.shape[0]
    return pl.pallas_call(
        mix_kernel,
        out_shape=jax.ShapeDtypeStruct((rows // heads, heads * HEAD_SIZE), bf16),
        compiler_params=pltpu.CompilerParams(vmem_limit_bytes=VMEM_BYTES),
        name="mix",
    )(weights, denominator, *values)


def own_kernel(scalars, *refs):
    pieces, weight, out = refs[:-2], refs[-2], refs[-1]
    depth = pieces[0].shape[1]
    rows = pl.ds(pl.multiple_of(scalars[0] * depth, depth), depth)
    lhs = jnp.concatenate([piece[...] for piece in pieces], axis=0)
    out[...] = jnp.dot(lhs, weight[rows, :], preferred_element_type=f32)


def own_output(pieces, out_weight, side, name):
    vmem = pl.BlockSpec(memory_space=pltpu.VMEM)
    rows = len(pieces) * pieces[0].shape[0]
    return pl.pallas_call(
        own_kernel,
        in_specs=[pl.BlockSpec(memory_space=pltpu.SMEM)] + [vmem] * (len(pieces) + 1),
        out_specs=vmem,
        out_shape=jax.ShapeDtypeStruct((rows, out_weight.shape[1]), f32),
        compiler_params=pltpu.CompilerParams(vmem_limit_bytes=VMEM_BYTES),
        name=name,
    )(jnp.stack([side]).astype(jnp.int32), *pieces, out_weight)


def other_kernel(shifts, scalars, *refs):
    pairs = len(shifts)
    pieces, weight, totals = refs[:pairs], refs[pairs], refs[pairs + 1 : -4]
    mine, send, placed, summed = refs[-4:]
    side, place, core = scalars[0], scalars[1], scalars[2]
    text, depth = pieces[0].shape
    for k, piece in enumerate(pieces):
        placed[lax.rem(place + pairs - k, pairs)] = piece[...]
    parts = [(ref, r) for ref in totals for r in range(0, ref.shape[0], text)]
    for k, (ref, r) in zip(shifts, parts):
        summed[lax.rem(place + pairs - k, pairs)] = ref[r : r + text, :]
    rows = pl.ds(pl.multiple_of(side * depth, depth), depth)
    half = pairs // 2
    for out, which in ((send, 1 - core), (mine, core)):
        base = which * half
        lhs = jnp.concatenate([placed[base + n] for n in range(half)], axis=0)
        own = jnp.concatenate([summed[base + n] for n in range(half)], axis=0)
        product = jnp.dot(lhs, weight[rows, :], preferred_element_type=f32)
        out[...] = (product + own).astype(out.dtype)


def other_output(pieces, out_weight, totals, shifts, side, place, core):
    vmem = pl.BlockSpec(memory_space=pltpu.VMEM)
    pairs = len(pieces)
    text, depth = pieces[0].shape
    width = out_weight.shape[1]
    rows = pairs * text // 2
    return pl.pallas_call(
        functools.partial(other_kernel, shifts),
        in_specs=[pl.BlockSpec(memory_space=pltpu.SMEM)] + [vmem] * (pairs + 1 + len(totals)),
        out_specs=[vmem] * 2,
        out_shape=[
            jax.ShapeDtypeStruct((rows, width), f32),
            jax.ShapeDtypeStruct((rows, width), bf16),
        ],
        scratch_shapes=[
            pltpu.VMEM((pairs, text, depth), bf16),
            pltpu.VMEM((pairs, text, width), f32),
        ],
        compiler_params=pltpu.CompilerParams(vmem_limit_bytes=VMEM_BYTES),
        name="output_other",
    )(jnp.stack([side, place, core]).astype(jnp.int32), *pieces, out_weight, *totals)


def after(array, *others):
    return lax.optimization_barrier((array, others))[0]


def norm(array, gain):
    mean = jnp.mean(array * array, axis=-1, keepdims=True)
    return (array * lax.rsqrt(mean + epsilon) * gain).astype(bf16)


def body(
    sizes,
    queries,
    vision,
    key_matrix,
    value_matrix,
    out_weight,
    residual,
    query_norm_gain,
    key_norm_gain,
    attn_gate,
):
    groups, seq, cores = sizes
    pairs = seq // 2
    group = lax.axis_index("groups")
    side = lax.axis_index("seq") % 2
    place = lax.axis_index("seq") // 2
    core = lax.axis_index("head")

    def permute(array, target):
        perm = []
        for g in range(groups):
            for z in range(pairs):
                for y in range(2):
                    for c in range(cores):
                        to = target(g, z, y, c)
                        if to is not None:
                            tg, tz, ty, tc = to
                            perm.append(
                                (
                                    (g * seq + z * 2 + y) * cores + c,
                                    (tg % groups * seq + tz % pairs * 2 + ty % 2) * cores
                                    + tc % cores,
                                )
                            )
        return lax.ppermute(array, AXES, perm)

    def plane_shift(array, by_group, by_side):
        return permute(array, lambda g, z, y, c: (g + by_group, z, y + by_side, c))

    def line_shift(array, by):
        return permute(array, lambda g, z, y, c: (g, z + by, y, c))

    def core_swap(array):
        return permute(array, lambda g, z, y, c: (g, z, y, c + 1))

    middle = pairs // 2 if pairs % 2 == 0 and pairs > 2 else 0

    def line_near(array):
        return {k: line_shift(array, k) for k in range(1, pairs) if k != middle}

    def line_far(pieces):
        if not middle:
            return []
        up = permute(
            pieces[middle - 1],
            lambda g, z, y, c: (g, z + 1, y, c) if middle <= z + 1 < pairs else None,
        )
        down = permute(
            pieces[middle + 1],
            lambda g, z, y, c: (g, z - 1, y, c) if 0 <= z - 1 < middle else None,
        )
        return [up, down]

    near_shifts = [k for k in range(1, pairs) if k != middle]
    shifts = [0] + near_shifts + ([middle, (middle,)] if middle else [])

    def line_slabs(own, pieces, far):
        return [own] + [pieces[k] for k in near_shifts] + far[::-1]

    def all_pairs(array):
        return [array] + [line_shift(array, k) for k in range(1, pairs)]

    offsets = [(g, y) for g in range(groups) for y in range(2)]

    part = key_matrix.shape[0] // groups

    def own_part(matrix):
        return lax.dynamic_slice_in_dim(matrix, group * part, part, axis=0)

    slab = jnp.concatenate([own_part(key_matrix), own_part(value_matrix)], axis=1)
    slab_near = line_near(slab)

    index = [(group + g) % groups * 2 + (side + y) % 2 for g, y in offsets]
    sends = pack(vision, index[1:], core, groups, pairs, part, "pack_sends")
    received = [plane_shift(send, g, y) for send, (g, y) in zip(sends, offsets[1:])]
    vision = after(vision, *sends)
    near = pack(vision, index[:1], core, groups, pairs, part, "pack_near")
    far = pack(vision, index[:1], 1 - core, groups, pairs, part, "pack_far")

    rows_q = queries.shape[0]
    half_q = queries.shape[1] // 2
    heads = half_q // HEAD_SIZE
    queries = after(queries, far[0])
    q_own = lax.dynamic_slice_in_dim(queries, side * half_q, half_q, axis=1)
    q_send = lax.dynamic_slice_in_dim(queries, (1 - side) * half_q, half_q, axis=1)

    received = [after(piece, near[0], far[0]) for piece in received]
    near = [*near, *received]
    slab_far = line_far({k: after(s, near[0], far[0]) for k, s in slab_near.items()})
    far = [*far] + [core_swap(piece) for piece in received]

    def scatter(pieces):
        return [plane_shift(piece, g, y) for piece, (g, y) in zip(pieces[1:], offsets[1:])]

    def sum_up(own, pieces):
        return functools.reduce(lambda a, b: a + b.astype(f32), pieces, own)

    slabs = line_slabs(slab, slab_near, slab_far)
    pieces = project(near, far, shifts, slabs, side, place, pairs)
    key_pieces, value_pieces = pieces[: len(offsets)], pieces[len(offsets) :]
    value_parts = scatter(value_pieces)
    key_parts = scatter(key_pieces)
    values = sum_up(value_pieces[0], value_parts).astype(bf16)
    all_values = {k: line_shift(values, k) for k in near_shifts}
    key_parts = [after(k, all_values[1]) for k in key_parts]
    q_recv = plane_shift(after(q_send, all_values[1]), 0, 1)
    q_pair = jnp.where(
        side == 0,
        jnp.concatenate([q_own, q_recv], axis=0),
        jnp.concatenate([q_recv, q_own], axis=0),
    )
    q_heads = jnp.concatenate(
        [q_pair[:, h * HEAD_SIZE : (h + 1) * HEAD_SIZE] for h in range(heads)], axis=0
    )
    normed = norm(q_heads.astype(f32), query_norm_gain)
    keys = norm(sum_up(key_pieces[0], key_parts), key_norm_gain)
    all_keys = all_pairs(keys)
    if middle:
        all_values[middle] = line_shift(after(values, keys), middle)
    all_values = [values, *(all_values[k] for k in range(1, pairs))]
    weights, denominator = score(normed, all_keys, heads)
    attended = mix(weights, denominator, all_values, heads)
    passed = {0: plane_shift(attended, 0, 1)}
    arrived = {k: line_shift(attended, k) for k in range(1, pairs)}
    for k in near_shifts:
        passed[k] = plane_shift(after(arrived[k], passed[0]), 0, 1)
    totals = [
        own_output([attended, *(arrived[k] for k in near_shifts)], out_weight, side, "output_near")
    ]
    order = [0, *near_shifts]
    if middle:
        opposite = after(arrived[middle], totals[0], passed[near_shifts[0]])
        passed[middle] = plane_shift(opposite, 0, 1)
        totals.append(own_output([opposite], out_weight, side, "output_far"))
        order.append(middle)
    others = [passed[k] for k in range(pairs)]
    mine, send = other_output(others, out_weight, totals, order, 1 - side, place, core)
    mine = mine + core_swap(send).astype(f32)
    return (residual.astype(f32) + jnp.tanh(attn_gate[0]) * mine).astype(bf16)


def solution(mesh):
    in_specs = (
        P(("groups", "seq"), "head"),
        P(("groups", "seq"), None),
        P("seq", "head"),
        P("seq", "head"),
        P("head", "seq"),
        P(("groups", "head"), "seq"),
        P(),
        P(),
        P(),
    )
    out_specs = P(("groups", "head"), "seq")
    sizes = tuple(mesh.shape[axis] for axis in AXES)
    return jax.shard_map(
        functools.partial(body, sizes),
        mesh=mesh,
        in_specs=in_specs,
        out_specs=out_specs,
        check_vma=False,
    )
```

```python
import functools

import jax
import jax.numpy as jnp
from jax import lax
from jax.experimental import pallas as pl
from jax.experimental.pallas import tpu as pltpu
from jax.sharding import PartitionSpec as P

HEAD_SIZE = 128
epsilon = 1e-05
AXES = ("groups", "seq", "head")
VMEM_BYTES = 20 * 1024 * 1024
f32, bf16 = jnp.float32, jnp.bfloat16


def pack_kernel(groups, pairs, part, count, index_ref, rows_ref, *outs):
    for g in range(groups):
        for y in range(2):
            starts = [((2 * z + y) * groups + g) * part for z in range(pairs)]
            for k, out in enumerate(outs):

                @pl.when(index_ref[k] == g * 2 + y)
                def _():
                    out[...] = jnp.concatenate(
                        [rows_ref[:, s : s + part] for s in starts], axis=1
                    )


def pack(vision, index, core, groups, pairs, part, name):
    rows, width = vision.shape
    half = rows // 2
    block = 32
    steps = half // block
    count = len(index)
    depth = pairs * part
    scalars = jnp.stack([*index, core]).astype(jnp.int32)
    return pl.pallas_call(
        functools.partial(pack_kernel, groups, pairs, part, count),
        grid_spec=pltpu.PrefetchScalarGridSpec(
            num_scalar_prefetch=1,
            grid=(steps,),
            in_specs=[pl.BlockSpec((block, width), lambda i, s: (s[count] * steps + i, 0))],
            out_specs=[pl.BlockSpec((block, depth), lambda i, s: (i, 0))] * count,
        ),
        out_shape=[jax.ShapeDtypeStruct((half, depth), vision.dtype)] * count,
        compiler_params=pltpu.CompilerParams(vmem_limit_bytes=VMEM_BYTES),
        name=name,
    )(scalars, vision)


def project_kernel(groups, pairs, shifts, scalars, *refs):
    count = groups * 2
    near, far, slabs = refs[:count], refs[count : 2 * count], refs[2 * count : -2 * count - 3]
    outs, placed, held, arrived = refs[-2 * count - 3 : -3], *refs[-3:]
    copies = [
        pltpu.make_async_copy(ref, held.at[n], arrived.at[n]) for n, ref in enumerate(far)
    ]
    for copy in copies:
        copy.start()
    half = near[0].shape[0]
    side, place = scalars[0], scalars[1]
    for shift, slab in zip(shifts, slabs):
        if isinstance(shift, tuple):
            continue
        placed[lax.rem(place + pairs - shift, pairs)] = slab[...]
    for shift, slab in zip(shifts, slabs):
        if isinstance(shift, tuple):

            @pl.when(place >= pairs // 2)
            def _():
                placed[lax.rem(place + pairs - shift[0], pairs)] = slab[...]

    w = jnp.concatenate([placed[z] for z in range(pairs)], axis=0)
    for part in range(2):
        if part:
            for copy in copies:
                copy.wait()
        pieces = [held[n] for n in range(count)] if part else [ref[...] for ref in near]
        lhs = jnp.concatenate(pieces, axis=0)
        result = jnp.dot(lhs, w, preferred_element_type=f32)
        columns = [result[:, n * HEAD_SIZE : (n + 1) * HEAD_SIZE] for n in range(4)]
        for matrix in range(2):
            first, second = columns[2 * matrix : 2 * matrix + 2]
            heads = jnp.where(side == 0, first, second), jnp.where(side == 0, second, first)
            for source in range(count):
                by_group, by_side = source // 2, source % 2
                for to in range(2):
                    out = outs[matrix * count + (-by_group) % groups * 2 + to]
                    start = (0 if by_side == to else 2 * half) + part * half
                    out[start : start + half, :] = heads[to][
                        source * half : (source + 1) * half, :
                    ].astype(out.dtype)


def project(near, far, shifts, slabs, side, place, pairs):
    count = len(near)
    half = near[0].shape[0]
    vmem = pl.BlockSpec(memory_space=pltpu.VMEM)
    return pl.pallas_call(
        functools.partial(project_kernel, count // 2, pairs, shifts),
        in_specs=[pl.BlockSpec(memory_space=pltpu.SMEM)] + [vmem] * count
        + [pl.BlockSpec(memory_space=pl.ANY)] * count
        + [vmem] * len(slabs),
        out_specs=[vmem] * (2 * count),
        out_shape=[
            jax.ShapeDtypeStruct((4 * half, HEAD_SIZE), bf16 if k > count else f32)
            for k in range(2 * count)
        ],
        scratch_shapes=[
            pltpu.VMEM((pairs,) + slabs[0].shape, bf16),
            pltpu.VMEM((count,) + near[0].shape, bf16),
            pltpu.SemaphoreType.DMA((count,)),
        ],
        compiler_params=pltpu.CompilerParams(vmem_limit_bytes=VMEM_BYTES),
        name="project",
    )(jnp.stack([side, place]).astype(jnp.int32), *near, *far, *slabs)


def score_kernel(heads, q_ref, *refs):
    keys, weights_ref, denominator_ref = refs[:-2], refs[-2], refs[-1]
    block = keys[0].shape[0]
    text = q_ref.shape[0] // heads
    for h in range(heads):
        rows = slice(h * text, (h + 1) * text)
        scores = [
            lax.dot_general(
                q_ref[rows, :], k[...], (((1,), (1,)), ((), ())), preferred_element_type=f32
            )
            * HEAD_SIZE ** (-0.5)
            for k in keys
        ]
        top = functools.reduce(
            jnp.maximum, [jnp.max(s, axis=-1, keepdims=True) for s in scores]
        )
        total = jnp.zeros_like(top)
        for n, s in enumerate(scores):
            weights = jnp.exp(s - top)
            total = total + jnp.sum(weights, axis=-1, keepdims=True)
            weights_ref[rows, n * block : (n + 1) * block] = weights.astype(bf16)
        denominator_ref[rows, :] = jnp.broadcast_to(total, (text, HEAD_SIZE))


def score(normed, keys, heads):
    rows = normed.shape[0]
    return pl.pallas_call(
        functools.partial(score_kernel, heads),
        out_shape=[
            jax.ShapeDtypeStruct((rows, len(keys) * keys[0].shape[0]), bf16),
            jax.ShapeDtypeStruct((rows, HEAD_SIZE), f32),
        ],
        compiler_params=pltpu.CompilerParams(vmem_limit_bytes=VMEM_BYTES),
        name="score",
    )(normed, *keys)


def mix_kernel(weights_ref, denominator_ref, *refs):
    values, out_ref = refs[:-1], refs[-1]
    text = out_ref.shape[0]
    v = jnp.concatenate([ref[...] for ref in values], axis=0)
    numerator = jnp.dot(weights_ref[...], v, preferred_element_type=f32)
    attended = (numerator / denominator_ref[...]).astype(bf16)
    for h in range(out_ref.shape[1] // HEAD_SIZE):
        out_ref[:, h * HEAD_SIZE : (h + 1) * HEAD_SIZE] = attended[h * text : (h + 1) * text, :]


def mix(weights, denominator, values, heads):
    rows = weights.shape[0]
    return pl.pallas_call(
        mix_kernel,
        out_shape=jax.ShapeDtypeStruct((rows // heads, heads * HEAD_SIZE), bf16),
        compiler_params=pltpu.CompilerParams(vmem_limit_bytes=VMEM_BYTES),
        name="mix",
    )(weights, denominator, *values)


def own_kernel(scalars, *refs):
    pieces, weight, out = refs[:-2], refs[-2], refs[-1]
    depth = pieces[0].shape[1]
    rows = pl.ds(pl.multiple_of(scalars[0] * depth, depth), depth)
    lhs = jnp.concatenate([piece[...] for piece in pieces], axis=0)
    out[...] = jnp.dot(lhs, weight[rows, :], preferred_element_type=f32)


def own_output(pieces, out_weight, side, name):
    vmem = pl.BlockSpec(memory_space=pltpu.VMEM)
    rows = len(pieces) * pieces[0].shape[0]
    return pl.pallas_call(
        own_kernel,
        in_specs=[pl.BlockSpec(memory_space=pltpu.SMEM)] + [vmem] * (len(pieces) + 1),
        out_specs=vmem,
        out_shape=jax.ShapeDtypeStruct((rows, out_weight.shape[1]), f32),
        compiler_params=pltpu.CompilerParams(vmem_limit_bytes=VMEM_BYTES),
        name=name,
    )(jnp.stack([side]).astype(jnp.int32), *pieces, out_weight)


def other_kernel(shifts, scalars, *refs):
    pairs = len(shifts)
    pieces, weight, totals = refs[:pairs], refs[pairs], refs[pairs + 1 : -4]
    mine, send, placed, summed = refs[-4:]
    side, place, core = scalars[0], scalars[1], scalars[2]
    text, depth = pieces[0].shape
    for k, piece in enumerate(pieces):
        placed[lax.rem(place + pairs - k, pairs)] = piece[...]
    parts = [(ref, r) for ref in totals for r in range(0, ref.shape[0], text)]
    for k, (ref, r) in zip(shifts, parts):
        summed[lax.rem(place + pairs - k, pairs)] = ref[r : r + text, :]
    rows = pl.ds(pl.multiple_of(side * depth, depth), depth)
    half = pairs // 2
    for out, which in ((send, 1 - core), (mine, core)):
        base = which * half
        lhs = jnp.concatenate([placed[base + n] for n in range(half)], axis=0)
        own = jnp.concatenate([summed[base + n] for n in range(half)], axis=0)
        product = jnp.dot(lhs, weight[rows, :], preferred_element_type=f32)
        out[...] = (product + own).astype(out.dtype)


def other_output(pieces, out_weight, totals, shifts, side, place, core):
    vmem = pl.BlockSpec(memory_space=pltpu.VMEM)
    pairs = len(pieces)
    text, depth = pieces[0].shape
    width = out_weight.shape[1]
    rows = pairs * text // 2
    return pl.pallas_call(
        functools.partial(other_kernel, shifts),
        in_specs=[pl.BlockSpec(memory_space=pltpu.SMEM)] + [vmem] * (pairs + 1 + len(totals)),
        out_specs=[vmem] * 2,
        out_shape=[
            jax.ShapeDtypeStruct((rows, width), f32),
            jax.ShapeDtypeStruct((rows, width), bf16),
        ],
        scratch_shapes=[
            pltpu.VMEM((pairs, text, depth), bf16),
            pltpu.VMEM((pairs, text, width), f32),
        ],
        compiler_params=pltpu.CompilerParams(vmem_limit_bytes=VMEM_BYTES),
        name="output_other",
    )(jnp.stack([side, place, core]).astype(jnp.int32), *pieces, out_weight, *totals)


def after(array, *others):
    return lax.optimization_barrier((array, others))[0]


def norm(array, gain):
    mean = jnp.mean(array * array, axis=-1, keepdims=True)
    return (array * lax.rsqrt(mean + epsilon) * gain).astype(bf16)


def body(
    sizes,
    queries,
    vision,
    key_matrix,
    value_matrix,
    out_weight,
    residual,
    query_norm_gain,
    key_norm_gain,
    attn_gate,
):
    groups, seq, cores = sizes
    pairs = seq // 2
    group = lax.axis_index("groups")
    side = lax.axis_index("seq") % 2
    place = lax.axis_index("seq") // 2
    core = lax.axis_index("head")

    def permute(array, target):
        perm = []
        for g in range(groups):
            for z in range(pairs):
                for y in range(2):
                    for c in range(cores):
                        to = target(g, z, y, c)
                        if to is not None:
                            tg, tz, ty, tc = to
                            perm.append(
                                (
                                    (g * seq + z * 2 + y) * cores + c,
                                    (tg % groups * seq + tz % pairs * 2 + ty % 2) * cores
                                    + tc % cores,
                                )
                            )
        return lax.ppermute(array, AXES, perm)

    def plane_shift(array, by_group, by_side):
        return permute(array, lambda g, z, y, c: (g + by_group, z, y + by_side, c))

    def line_shift(array, by):
        return permute(array, lambda g, z, y, c: (g, z + by, y, c))

    def core_swap(array):
        return permute(array, lambda g, z, y, c: (g, z, y, c + 1))

    middle = pairs // 2 if pairs % 2 == 0 and pairs > 2 else 0

    def line_near(array):
        return {k: line_shift(array, k) for k in range(1, pairs) if k != middle}

    def line_far(pieces):
        if not middle:
            return []
        up = permute(
            pieces[middle - 1],
            lambda g, z, y, c: (g, z + 1, y, c) if middle <= z + 1 < pairs else None,
        )
        down = permute(
            pieces[middle + 1],
            lambda g, z, y, c: (g, z - 1, y, c) if 0 <= z - 1 < middle else None,
        )
        return [up, down]

    near_shifts = [k for k in range(1, pairs) if k != middle]
    shifts = [0] + near_shifts + ([middle, (middle,)] if middle else [])

    def line_slabs(own, pieces, far):
        return [own] + [pieces[k] for k in near_shifts] + far[::-1]

    def all_pairs(array):
        return [array] + [line_shift(array, k) for k in range(1, pairs)]

    offsets = [(g, y) for g in range(groups) for y in range(2)]

    part = key_matrix.shape[0] // groups

    def own_part(matrix):
        return lax.dynamic_slice_in_dim(matrix, group * part, part, axis=0)

    slab = jnp.concatenate([own_part(key_matrix), own_part(value_matrix)], axis=1)
    slab_near = line_near(slab)

    index = [(group + g) % groups * 2 + (side + y) % 2 for g, y in offsets]
    sends = pack(vision, index[1:], core, groups, pairs, part, "pack_sends")
    received = [plane_shift(send, g, y) for send, (g, y) in zip(sends, offsets[1:])]
    vision = after(vision, *sends)
    near = pack(vision, index[:1], core, groups, pairs, part, "pack_near")
    far = pack(vision, index[:1], 1 - core, groups, pairs, part, "pack_far")

    rows_q = queries.shape[0]
    half_q = queries.shape[1] // 2
    heads = half_q // HEAD_SIZE
    queries = after(queries, far[0])
    q_own = lax.dynamic_slice_in_dim(queries, side * half_q, half_q, axis=1)
    q_send = lax.dynamic_slice_in_dim(queries, (1 - side) * half_q, half_q, axis=1)

    received = [after(piece, near[0], far[0]) for piece in received]
    near = [*near, *received]
    slab_far = line_far({k: after(s, near[0], far[0]) for k, s in slab_near.items()})
    far = [*far] + [core_swap(piece) for piece in received]

    def scatter(pieces):
        return [plane_shift(piece, g, y) for piece, (g, y) in zip(pieces[1:], offsets[1:])]

    def sum_up(own, pieces):
        return functools.reduce(lambda a, b: a + b.astype(f32), pieces, own)

    slabs = line_slabs(slab, slab_near, slab_far)
    pieces = project(near, far, shifts, slabs, side, place, pairs)
    key_pieces, value_pieces = pieces[: len(offsets)], pieces[len(offsets) :]
    value_parts = scatter(value_pieces)
    key_parts = scatter(key_pieces)
    values = sum_up(value_pieces[0], value_parts).astype(bf16)
    all_values = all_pairs(values)
    key_parts = [after(k, all_values[1]) for k in key_parts]
    q_recv = plane_shift(after(q_send, all_values[1]), 0, 1)
    q_pair = jnp.where(
        side == 0,
        jnp.concatenate([q_own, q_recv], axis=0),
        jnp.concatenate([q_recv, q_own], axis=0),
    )
    q_heads = jnp.concatenate(
        [q_pair[:, h * HEAD_SIZE : (h + 1) * HEAD_SIZE] for h in range(heads)], axis=0
    )
    normed = norm(q_heads.astype(f32), query_norm_gain)
    keys = norm(sum_up(key_pieces[0], key_parts), key_norm_gain)
    all_keys = all_pairs(keys)
    weights, denominator = score(normed, all_keys, heads)
    attended = mix(weights, denominator, all_values, heads)
    passed = {0: plane_shift(attended, 0, 1)}
    arrived = {k: line_shift(attended, k) for k in range(1, pairs)}
    for k in near_shifts:
        passed[k] = plane_shift(after(arrived[k], passed[0]), 0, 1)
    totals = [
        own_output([attended, *(arrived[k] for k in near_shifts)], out_weight, side, "output_near")
    ]
    order = [0, *near_shifts]
    if middle:
        opposite = after(arrived[middle], totals[0], passed[near_shifts[0]])
        passed[middle] = plane_shift(opposite, 0, 1)
        totals.append(own_output([opposite], out_weight, side, "output_far"))
        order.append(middle)
    others = [passed[k] for k in range(pairs)]
    mine, send = other_output(others, out_weight, totals, order, 1 - side, place, core)
    mine = mine + core_swap(send).astype(f32)
    return (residual.astype(f32) + jnp.tanh(attn_gate[0]) * mine).astype(bf16)


def solution(mesh):
    in_specs = (
        P(("groups", "seq"), "head"),
        P(("groups", "seq"), None),
        P("seq", "head"),
        P("seq", "head"),
        P("head", "seq"),
        P(("groups", "head"), "seq"),
        P(),
        P(),
        P(),
    )
    out_specs = P(("groups", "head"), "seq")
    sizes = tuple(mesh.shape[axis] for axis in AXES)
    return jax.shard_map(
        functools.partial(body, sizes),
        mesh=mesh,
        in_specs=in_specs,
        out_specs=out_specs,
        check_vma=False,
    )
```

```python
import functools

import jax
import jax.numpy as jnp
from jax import lax
from jax.experimental import pallas as pl
from jax.experimental.pallas import tpu as pltpu
from jax.sharding import PartitionSpec as P

HEAD_SIZE = 128
epsilon = 1e-05
AXES = ("groups", "seq", "head")
VMEM_BYTES = 20 * 1024 * 1024
f32, bf16 = jnp.float32, jnp.bfloat16


def pack_kernel(groups, pairs, part, count, index_ref, rows_ref, *outs):
    for g in range(groups):
        for y in range(2):
            starts = [((2 * z + y) * groups + g) * part for z in range(pairs)]
            for k, out in enumerate(outs):

                @pl.when(index_ref[k] == g * 2 + y)
                def _():
                    out[...] = jnp.concatenate(
                        [rows_ref[:, s : s + part] for s in starts], axis=1
                    )


def pack(vision, index, core, groups, pairs, part, name):
    rows, width = vision.shape
    half = rows // 2
    block = 32
    steps = half // block
    count = len(index)
    depth = pairs * part
    scalars = jnp.stack([*index, core]).astype(jnp.int32)
    return pl.pallas_call(
        functools.partial(pack_kernel, groups, pairs, part, count),
        grid_spec=pltpu.PrefetchScalarGridSpec(
            num_scalar_prefetch=1,
            grid=(steps,),
            in_specs=[pl.BlockSpec((block, width), lambda i, s: (s[count] * steps + i, 0))],
            out_specs=[pl.BlockSpec((block, depth), lambda i, s: (i, 0))] * count,
        ),
        out_shape=[jax.ShapeDtypeStruct((half, depth), vision.dtype)] * count,
        compiler_params=pltpu.CompilerParams(vmem_limit_bytes=VMEM_BYTES),
        name=name,
    )(scalars, vision)


def project_kernel(groups, pairs, shifts, scalars, *refs):
    count = groups * 2
    near, far, slabs = refs[:count], refs[count : 2 * count], refs[2 * count : -2 * count - 1]
    outs, placed = refs[-2 * count - 1 : -1], refs[-1]
    half = near[0].shape[0]
    side, place = scalars[0], scalars[1]
    for shift, slab in zip(shifts, slabs):
        if isinstance(shift, tuple):
            continue
        placed[lax.rem(place + pairs - shift, pairs)] = slab[...]
    for shift, slab in zip(shifts, slabs):
        if isinstance(shift, tuple):

            @pl.when(place >= pairs // 2)
            def _():
                placed[lax.rem(place + pairs - shift[0], pairs)] = slab[...]

    w = jnp.concatenate([placed[z] for z in range(pairs)], axis=0)
    for part, pieces in enumerate((near, far)):
        lhs = jnp.concatenate([ref[...] for ref in pieces], axis=0)
        result = jnp.dot(lhs, w, preferred_element_type=f32)
        columns = [result[:, n * HEAD_SIZE : (n + 1) * HEAD_SIZE] for n in range(4)]
        for matrix in range(2):
            first, second = columns[2 * matrix : 2 * matrix + 2]
            heads = jnp.where(side == 0, first, second), jnp.where(side == 0, second, first)
            for source in range(count):
                by_group, by_side = source // 2, source % 2
                for to in range(2):
                    out = outs[matrix * count + (-by_group) % groups * 2 + to]
                    start = (0 if by_side == to else 2 * half) + part * half
                    out[start : start + half, :] = heads[to][
                        source * half : (source + 1) * half, :
                    ].astype(out.dtype)


def project(near, far, shifts, slabs, side, place, pairs):
    count = len(near)
    half = near[0].shape[0]
    vmem = pl.BlockSpec(memory_space=pltpu.VMEM)
    return pl.pallas_call(
        functools.partial(project_kernel, count // 2, pairs, shifts),
        in_specs=[pl.BlockSpec(memory_space=pltpu.SMEM)] + [vmem] * (2 * count + len(slabs)),
        out_specs=[vmem] * (2 * count),
        out_shape=[
            jax.ShapeDtypeStruct((4 * half, HEAD_SIZE), bf16 if k > count else f32)
            for k in range(2 * count)
        ],
        scratch_shapes=[pltpu.VMEM((pairs,) + slabs[0].shape, bf16)],
        compiler_params=pltpu.CompilerParams(vmem_limit_bytes=VMEM_BYTES),
        name="project",
    )(jnp.stack([side, place]).astype(jnp.int32), *near, *far, *slabs)


def score_kernel(heads, q_ref, *refs):
    keys, weights_ref, denominator_ref = refs[:-2], refs[-2], refs[-1]
    block = keys[0].shape[0]
    text = q_ref.shape[0] // heads
    for h in range(heads):
        rows = slice(h * text, (h + 1) * text)
        scores = [
            lax.dot_general(
                q_ref[rows, :], k[...], (((1,), (1,)), ((), ())), preferred_element_type=f32
            )
            * HEAD_SIZE ** (-0.5)
            for k in keys
        ]
        top = functools.reduce(
            jnp.maximum, [jnp.max(s, axis=-1, keepdims=True) for s in scores]
        )
        total = jnp.zeros_like(top)
        for n, s in enumerate(scores):
            weights = jnp.exp(s - top)
            total = total + jnp.sum(weights, axis=-1, keepdims=True)
            weights_ref[rows, n * block : (n + 1) * block] = weights.astype(bf16)
        denominator_ref[rows, :] = jnp.broadcast_to(total, (text, HEAD_SIZE))


def score(normed, keys, heads):
    rows = normed.shape[0]
    return pl.pallas_call(
        functools.partial(score_kernel, heads),
        out_shape=[
            jax.ShapeDtypeStruct((rows, len(keys) * keys[0].shape[0]), bf16),
            jax.ShapeDtypeStruct((rows, HEAD_SIZE), f32),
        ],
        compiler_params=pltpu.CompilerParams(vmem_limit_bytes=VMEM_BYTES),
        name="score",
    )(normed, *keys)


def mix_kernel(weights_ref, denominator_ref, *refs):
    values, out_ref = refs[:-1], refs[-1]
    text = out_ref.shape[0]
    v = jnp.concatenate([ref[...] for ref in values], axis=0)
    numerator = jnp.dot(weights_ref[...], v, preferred_element_type=f32)
    attended = (numerator / denominator_ref[...]).astype(bf16)
    for h in range(out_ref.shape[1] // HEAD_SIZE):
        out_ref[:, h * HEAD_SIZE : (h + 1) * HEAD_SIZE] = attended[h * text : (h + 1) * text, :]


def mix(weights, denominator, values, heads):
    rows = weights.shape[0]
    return pl.pallas_call(
        mix_kernel,
        out_shape=jax.ShapeDtypeStruct((rows // heads, heads * HEAD_SIZE), bf16),
        compiler_params=pltpu.CompilerParams(vmem_limit_bytes=VMEM_BYTES),
        name="mix",
    )(weights, denominator, *values)


def own_kernel(scalars, *refs):
    pieces, weight, out = refs[:-2], refs[-2], refs[-1]
    depth = pieces[0].shape[1]
    rows = pl.ds(pl.multiple_of(scalars[0] * depth, depth), depth)
    lhs = jnp.concatenate([piece[...] for piece in pieces], axis=0)
    out[...] = jnp.dot(lhs, weight[rows, :], preferred_element_type=f32)


def own_output(pieces, out_weight, side, name):
    vmem = pl.BlockSpec(memory_space=pltpu.VMEM)
    rows = len(pieces) * pieces[0].shape[0]
    return pl.pallas_call(
        own_kernel,
        in_specs=[pl.BlockSpec(memory_space=pltpu.SMEM)] + [vmem] * (len(pieces) + 1),
        out_specs=vmem,
        out_shape=jax.ShapeDtypeStruct((rows, out_weight.shape[1]), f32),
        compiler_params=pltpu.CompilerParams(vmem_limit_bytes=VMEM_BYTES),
        name=name,
    )(jnp.stack([side]).astype(jnp.int32), *pieces, out_weight)


def other_kernel(shifts, scalars, *refs):
    pairs = len(shifts)
    pieces, weight, totals = refs[:pairs], refs[pairs], refs[pairs + 1 : -4]
    mine, send, placed, summed = refs[-4:]
    side, place, core = scalars[0], scalars[1], scalars[2]
    text, depth = pieces[0].shape
    for k, piece in enumerate(pieces):
        placed[lax.rem(place + pairs - k, pairs)] = piece[...]
    parts = [(ref, r) for ref in totals for r in range(0, ref.shape[0], text)]
    for k, (ref, r) in zip(shifts, parts):
        summed[lax.rem(place + pairs - k, pairs)] = ref[r : r + text, :]
    rows = pl.ds(pl.multiple_of(side * depth, depth), depth)
    half = pairs // 2
    for out, which in ((send, 1 - core), (mine, core)):
        base = which * half
        lhs = jnp.concatenate([placed[base + n] for n in range(half)], axis=0)
        own = jnp.concatenate([summed[base + n] for n in range(half)], axis=0)
        product = jnp.dot(lhs, weight[rows, :], preferred_element_type=f32)
        out[...] = (product + own).astype(out.dtype)


def other_output(pieces, out_weight, totals, shifts, side, place, core):
    vmem = pl.BlockSpec(memory_space=pltpu.VMEM)
    pairs = len(pieces)
    text, depth = pieces[0].shape
    width = out_weight.shape[1]
    rows = pairs * text // 2
    return pl.pallas_call(
        functools.partial(other_kernel, shifts),
        in_specs=[pl.BlockSpec(memory_space=pltpu.SMEM)] + [vmem] * (pairs + 1 + len(totals)),
        out_specs=[vmem] * 2,
        out_shape=[
            jax.ShapeDtypeStruct((rows, width), f32),
            jax.ShapeDtypeStruct((rows, width), bf16),
        ],
        scratch_shapes=[
            pltpu.VMEM((pairs, text, depth), bf16),
            pltpu.VMEM((pairs, text, width), f32),
        ],
        compiler_params=pltpu.CompilerParams(vmem_limit_bytes=VMEM_BYTES),
        name="output_other",
    )(jnp.stack([side, place, core]).astype(jnp.int32), *pieces, out_weight, *totals)


def after(array, *others):
    return lax.optimization_barrier((array, others))[0]


def norm(array, gain):
    mean = jnp.mean(array * array, axis=-1, keepdims=True)
    return (array * lax.rsqrt(mean + epsilon) * gain).astype(bf16)


def body(
    sizes,
    queries,
    vision,
    key_matrix,
    value_matrix,
    out_weight,
    residual,
    query_norm_gain,
    key_norm_gain,
    attn_gate,
):
    groups, seq, cores = sizes
    pairs = seq // 2
    group = lax.axis_index("groups")
    side = lax.axis_index("seq") % 2
    place = lax.axis_index("seq") // 2
    core = lax.axis_index("head")

    def permute(array, target):
        perm = []
        for g in range(groups):
            for z in range(pairs):
                for y in range(2):
                    for c in range(cores):
                        to = target(g, z, y, c)
                        if to is not None:
                            tg, tz, ty, tc = to
                            perm.append(
                                (
                                    (g * seq + z * 2 + y) * cores + c,
                                    (tg % groups * seq + tz % pairs * 2 + ty % 2) * cores
                                    + tc % cores,
                                )
                            )
        return lax.ppermute(array, AXES, perm)

    def plane_shift(array, by_group, by_side):
        return permute(array, lambda g, z, y, c: (g + by_group, z, y + by_side, c))

    def line_shift(array, by):
        return permute(array, lambda g, z, y, c: (g, z + by, y, c))

    def core_swap(array):
        return permute(array, lambda g, z, y, c: (g, z, y, c + 1))

    middle = pairs // 2 if pairs % 2 == 0 and pairs > 2 else 0

    def line_near(array):
        return {k: line_shift(array, k) for k in range(1, pairs) if k != middle}

    def line_far(pieces):
        if not middle:
            return []
        up = permute(
            pieces[middle - 1],
            lambda g, z, y, c: (g, z + 1, y, c) if middle <= z + 1 < pairs else None,
        )
        down = permute(
            pieces[middle + 1],
            lambda g, z, y, c: (g, z - 1, y, c) if 0 <= z - 1 < middle else None,
        )
        return [up, down]

    near_shifts = [k for k in range(1, pairs) if k != middle]
    shifts = [0] + near_shifts + ([middle, (middle,)] if middle else [])

    def line_slabs(own, pieces, far):
        return [own] + [pieces[k] for k in near_shifts] + far[::-1]

    def all_pairs(array):
        return [array] + [line_shift(array, k) for k in range(1, pairs)]

    offsets = [(g, y) for g in range(groups) for y in range(2)]

    part = key_matrix.shape[0] // groups

    def own_part(matrix):
        return lax.dynamic_slice_in_dim(matrix, group * part, part, axis=0)

    slab = jnp.concatenate([own_part(key_matrix), own_part(value_matrix)], axis=1)
    slab_near = line_near(slab)

    index = [(group + g) % groups * 2 + (side + y) % 2 for g, y in offsets]
    sends = pack(vision, index[1:], core, groups, pairs, part, "pack_sends")
    received = [plane_shift(send, g, y) for send, (g, y) in zip(sends, offsets[1:])]
    vision = after(vision, *sends)
    near = pack(vision, index[:1], core, groups, pairs, part, "pack_near")
    far = pack(vision, index[:1], 1 - core, groups, pairs, part, "pack_far")

    rows_q = queries.shape[0]
    half_q = queries.shape[1] // 2
    heads = half_q // HEAD_SIZE
    queries = after(queries, far[0])
    q_own = lax.dynamic_slice_in_dim(queries, side * half_q, half_q, axis=1)
    q_send = lax.dynamic_slice_in_dim(queries, (1 - side) * half_q, half_q, axis=1)

    received = [after(piece, near[0], far[0]) for piece in received]
    near = [*near, *received]
    slab_far = line_far({k: after(s, near[0], far[0]) for k, s in slab_near.items()})
    far = [*far] + [core_swap(piece) for piece in received]

    def scatter(pieces):
        return [plane_shift(piece, g, y) for piece, (g, y) in zip(pieces[1:], offsets[1:])]

    def sum_up(own, pieces):
        return functools.reduce(lambda a, b: a + b.astype(f32), pieces, own)

    slabs = line_slabs(slab, slab_near, slab_far)
    pieces = project(near, far, shifts, slabs, side, place, pairs)
    key_pieces, value_pieces = pieces[: len(offsets)], pieces[len(offsets) :]
    value_parts = scatter(value_pieces)
    key_parts = scatter(key_pieces)
    values = sum_up(value_pieces[0], value_parts).astype(bf16)
    all_values = all_pairs(values)
    key_parts = [after(k, all_values[1], all_values[-1]) for k in key_parts]
    q_recv = plane_shift(after(q_send, all_values[1]), 0, 1)
    q_pair = jnp.where(
        side == 0,
        jnp.concatenate([q_own, q_recv], axis=0),
        jnp.concatenate([q_recv, q_own], axis=0),
    )
    q_heads = jnp.concatenate(
        [q_pair[:, h * HEAD_SIZE : (h + 1) * HEAD_SIZE] for h in range(heads)], axis=0
    )
    normed = norm(q_heads.astype(f32), query_norm_gain)
    keys = norm(sum_up(key_pieces[0], key_parts), key_norm_gain)
    all_keys = all_pairs(keys)
    weights, denominator = score(normed, all_keys, heads)
    attended = mix(weights, denominator, all_values, heads)
    passed = {0: plane_shift(attended, 0, 1)}
    arrived = {k: line_shift(attended, k) for k in range(1, pairs)}
    for k in near_shifts:
        passed[k] = plane_shift(after(arrived[k], passed[0]), 0, 1)
    totals = [
        own_output([attended, *(arrived[k] for k in near_shifts)], out_weight, side, "output_near")
    ]
    order = [0, *near_shifts]
    if middle:
        opposite = after(arrived[middle], totals[0], passed[near_shifts[0]])
        passed[middle] = plane_shift(opposite, 0, 1)
        totals.append(own_output([opposite], out_weight, side, "output_far"))
        order.append(middle)
    others = [passed[k] for k in range(pairs)]
    mine, send = other_output(others, out_weight, totals, order, 1 - side, place, core)
    mine = mine + core_swap(send).astype(f32)
    return (residual.astype(f32) + jnp.tanh(attn_gate[0]) * mine).astype(bf16)


def solution(mesh):
    in_specs = (
        P(("groups", "seq"), "head"),
        P(("groups", "seq"), None),
        P("seq", "head"),
        P("seq", "head"),
        P("head", "seq"),
        P(("groups", "head"), "seq"),
        P(),
        P(),
        P(),
    )
    out_specs = P(("groups", "head"), "seq")
    sizes = tuple(mesh.shape[axis] for axis in AXES)
    return jax.shard_map(
        functools.partial(body, sizes),
        mesh=mesh,
        in_specs=in_specs,
        out_specs=out_specs,
        check_vma=False,
    )
```

```python
import functools

import jax
import jax.numpy as jnp
from jax import lax
from jax.experimental import pallas as pl
from jax.experimental.pallas import tpu as pltpu
from jax.sharding import PartitionSpec as P

HEAD_SIZE = 128
epsilon = 1e-05
AXES = ("groups", "seq", "head")
VMEM_BYTES = 20 * 1024 * 1024
f32, bf16 = jnp.float32, jnp.bfloat16


def pack_kernel(groups, pairs, part, count, index_ref, rows_ref, *outs):
    for g in range(groups):
        for y in range(2):
            starts = [((2 * z + y) * groups + g) * part for z in range(pairs)]
            for k, out in enumerate(outs):

                @pl.when(index_ref[k] == g * 2 + y)
                def _():
                    out[...] = jnp.concatenate(
                        [rows_ref[:, s : s + part] for s in starts], axis=1
                    )


def pack(vision, index, core, groups, pairs, part, name):
    rows, width = vision.shape
    half = rows // 2
    block = 32
    steps = half // block
    count = len(index)
    depth = pairs * part
    scalars = jnp.stack([*index, core]).astype(jnp.int32)
    return pl.pallas_call(
        functools.partial(pack_kernel, groups, pairs, part, count),
        grid_spec=pltpu.PrefetchScalarGridSpec(
            num_scalar_prefetch=1,
            grid=(steps,),
            in_specs=[pl.BlockSpec((block, width), lambda i, s: (s[count] * steps + i, 0))],
            out_specs=[pl.BlockSpec((block, depth), lambda i, s: (i, 0))] * count,
        ),
        out_shape=[jax.ShapeDtypeStruct((half, depth), vision.dtype)] * count,
        compiler_params=pltpu.CompilerParams(vmem_limit_bytes=VMEM_BYTES),
        name=name,
    )(scalars, vision)


def project_kernel(groups, pairs, shifts, scalars, *refs):
    count = groups * 2
    slabs, near, far = refs[: -4 * count - 1], refs[-4 * count - 1 : -3 * count - 1], refs[-3 * count - 1 : -2 * count - 1]
    outs, placed = refs[-2 * count - 1 : -1], refs[-1]
    half = near[0].shape[0]
    side, place = scalars[0], scalars[1]
    for shift, slab in zip(shifts, slabs):
        if isinstance(shift, tuple):
            continue
        placed[lax.rem(place + pairs - shift, pairs)] = slab[...]
    for shift, slab in zip(shifts, slabs):
        if isinstance(shift, tuple):

            @pl.when(place >= pairs // 2)
            def _():
                placed[lax.rem(place + pairs - shift[0], pairs)] = slab[...]

    w = jnp.concatenate([placed[z] for z in range(pairs)], axis=0)
    for part, pieces in enumerate((near, far)):
        lhs = jnp.concatenate([ref[...] for ref in pieces], axis=0)
        result = jnp.dot(lhs, w, preferred_element_type=f32)
        columns = [result[:, n * HEAD_SIZE : (n + 1) * HEAD_SIZE] for n in range(4)]
        for matrix in range(2):
            first, second = columns[2 * matrix : 2 * matrix + 2]
            heads = jnp.where(side == 0, first, second), jnp.where(side == 0, second, first)
            for source in range(count):
                by_group, by_side = source // 2, source % 2
                for to in range(2):
                    out = outs[matrix * count + (-by_group) % groups * 2 + to]
                    start = (0 if by_side == to else 2 * half) + part * half
                    out[start : start + half, :] = heads[to][
                        source * half : (source + 1) * half, :
                    ].astype(out.dtype)


def project(near, far, shifts, slabs, side, place, pairs):
    count = len(near)
    half = near[0].shape[0]
    vmem = pl.BlockSpec(memory_space=pltpu.VMEM)
    return pl.pallas_call(
        functools.partial(project_kernel, count // 2, pairs, shifts),
        in_specs=[pl.BlockSpec(memory_space=pltpu.SMEM)] + [vmem] * (2 * count + len(slabs)),
        out_specs=[vmem] * (2 * count),
        out_shape=[
            jax.ShapeDtypeStruct((4 * half, HEAD_SIZE), bf16 if k > count else f32)
            for k in range(2 * count)
        ],
        scratch_shapes=[pltpu.VMEM((pairs,) + slabs[0].shape, bf16)],
        compiler_params=pltpu.CompilerParams(vmem_limit_bytes=VMEM_BYTES),
        name="project",
    )(jnp.stack([side, place]).astype(jnp.int32), *slabs, *near, *far)


def score_kernel(heads, q_ref, *refs):
    keys, weights_ref, denominator_ref = refs[:-2], refs[-2], refs[-1]
    block = keys[0].shape[0]
    text = q_ref.shape[0] // heads
    for h in range(heads):
        rows = slice(h * text, (h + 1) * text)
        scores = [
            lax.dot_general(
                q_ref[rows, :], k[...], (((1,), (1,)), ((), ())), preferred_element_type=f32
            )
            * HEAD_SIZE ** (-0.5)
            for k in keys
        ]
        top = functools.reduce(
            jnp.maximum, [jnp.max(s, axis=-1, keepdims=True) for s in scores]
        )
        total = jnp.zeros_like(top)
        for n, s in enumerate(scores):
            weights = jnp.exp(s - top)
            total = total + jnp.sum(weights, axis=-1, keepdims=True)
            weights_ref[rows, n * block : (n + 1) * block] = weights.astype(bf16)
        denominator_ref[rows, :] = jnp.broadcast_to(total, (text, HEAD_SIZE))


def score(normed, keys, heads):
    rows = normed.shape[0]
    return pl.pallas_call(
        functools.partial(score_kernel, heads),
        out_shape=[
            jax.ShapeDtypeStruct((rows, len(keys) * keys[0].shape[0]), bf16),
            jax.ShapeDtypeStruct((rows, HEAD_SIZE), f32),
        ],
        compiler_params=pltpu.CompilerParams(vmem_limit_bytes=VMEM_BYTES),
        name="score",
    )(normed, *keys)


def mix_kernel(weights_ref, denominator_ref, *refs):
    values, out_ref = refs[:-1], refs[-1]
    text = out_ref.shape[0]
    v = jnp.concatenate([ref[...] for ref in values], axis=0)
    numerator = jnp.dot(weights_ref[...], v, preferred_element_type=f32)
    attended = (numerator / denominator_ref[...]).astype(bf16)
    for h in range(out_ref.shape[1] // HEAD_SIZE):
        out_ref[:, h * HEAD_SIZE : (h + 1) * HEAD_SIZE] = attended[h * text : (h + 1) * text, :]


def mix(weights, denominator, values, heads):
    rows = weights.shape[0]
    return pl.pallas_call(
        mix_kernel,
        out_shape=jax.ShapeDtypeStruct((rows // heads, heads * HEAD_SIZE), bf16),
        compiler_params=pltpu.CompilerParams(vmem_limit_bytes=VMEM_BYTES),
        name="mix",
    )(weights, denominator, *values)


def own_kernel(scalars, *refs):
    pieces, weight, out = refs[:-2], refs[-2], refs[-1]
    depth = pieces[0].shape[1]
    rows = pl.ds(pl.multiple_of(scalars[0] * depth, depth), depth)
    lhs = jnp.concatenate([piece[...] for piece in pieces], axis=0)
    out[...] = jnp.dot(lhs, weight[rows, :], preferred_element_type=f32)


def own_output(pieces, out_weight, side, name):
    vmem = pl.BlockSpec(memory_space=pltpu.VMEM)
    rows = len(pieces) * pieces[0].shape[0]
    return pl.pallas_call(
        own_kernel,
        in_specs=[pl.BlockSpec(memory_space=pltpu.SMEM)] + [vmem] * (len(pieces) + 1),
        out_specs=vmem,
        out_shape=jax.ShapeDtypeStruct((rows, out_weight.shape[1]), f32),
        compiler_params=pltpu.CompilerParams(vmem_limit_bytes=VMEM_BYTES),
        name=name,
    )(jnp.stack([side]).astype(jnp.int32), *pieces, out_weight)


def other_kernel(shifts, scalars, *refs):
    pairs = len(shifts)
    pieces, weight, totals = refs[:pairs], refs[pairs], refs[pairs + 1 : -4]
    mine, send, placed, summed = refs[-4:]
    side, place, core = scalars[0], scalars[1], scalars[2]
    text, depth = pieces[0].shape
    for k, piece in enumerate(pieces):
        placed[lax.rem(place + pairs - k, pairs)] = piece[...]
    parts = [(ref, r) for ref in totals for r in range(0, ref.shape[0], text)]
    for k, (ref, r) in zip(shifts, parts):
        summed[lax.rem(place + pairs - k, pairs)] = ref[r : r + text, :]
    rows = pl.ds(pl.multiple_of(side * depth, depth), depth)
    half = pairs // 2
    for out, which in ((send, 1 - core), (mine, core)):
        base = which * half
        lhs = jnp.concatenate([placed[base + n] for n in range(half)], axis=0)
        own = jnp.concatenate([summed[base + n] for n in range(half)], axis=0)
        product = jnp.dot(lhs, weight[rows, :], preferred_element_type=f32)
        out[...] = (product + own).astype(out.dtype)


def other_output(pieces, out_weight, totals, shifts, side, place, core):
    vmem = pl.BlockSpec(memory_space=pltpu.VMEM)
    pairs = len(pieces)
    text, depth = pieces[0].shape
    width = out_weight.shape[1]
    rows = pairs * text // 2
    return pl.pallas_call(
        functools.partial(other_kernel, shifts),
        in_specs=[pl.BlockSpec(memory_space=pltpu.SMEM)] + [vmem] * (pairs + 1 + len(totals)),
        out_specs=[vmem] * 2,
        out_shape=[
            jax.ShapeDtypeStruct((rows, width), f32),
            jax.ShapeDtypeStruct((rows, width), bf16),
        ],
        scratch_shapes=[
            pltpu.VMEM((pairs, text, depth), bf16),
            pltpu.VMEM((pairs, text, width), f32),
        ],
        compiler_params=pltpu.CompilerParams(vmem_limit_bytes=VMEM_BYTES),
        name="output_other",
    )(jnp.stack([side, place, core]).astype(jnp.int32), *pieces, out_weight, *totals)


def after(array, *others):
    return lax.optimization_barrier((array, others))[0]


def norm(array, gain):
    mean = jnp.mean(array * array, axis=-1, keepdims=True)
    return (array * lax.rsqrt(mean + epsilon) * gain).astype(bf16)


def body(
    sizes,
    queries,
    vision,
    key_matrix,
    value_matrix,
    out_weight,
    residual,
    query_norm_gain,
    key_norm_gain,
    attn_gate,
):
    groups, seq, cores = sizes
    pairs = seq // 2
    group = lax.axis_index("groups")
    side = lax.axis_index("seq") % 2
    place = lax.axis_index("seq") // 2
    core = lax.axis_index("head")

    def permute(array, target):
        perm = []
        for g in range(groups):
            for z in range(pairs):
                for y in range(2):
                    for c in range(cores):
                        to = target(g, z, y, c)
                        if to is not None:
                            tg, tz, ty, tc = to
                            perm.append(
                                (
                                    (g * seq + z * 2 + y) * cores + c,
                                    (tg % groups * seq + tz % pairs * 2 + ty % 2) * cores
                                    + tc % cores,
                                )
                            )
        return lax.ppermute(array, AXES, perm)

    def plane_shift(array, by_group, by_side):
        return permute(array, lambda g, z, y, c: (g + by_group, z, y + by_side, c))

    def line_shift(array, by):
        return permute(array, lambda g, z, y, c: (g, z + by, y, c))

    def core_swap(array):
        return permute(array, lambda g, z, y, c: (g, z, y, c + 1))

    middle = pairs // 2 if pairs % 2 == 0 and pairs > 2 else 0

    def line_near(array):
        return {k: line_shift(array, k) for k in range(1, pairs) if k != middle}

    def line_far(pieces):
        if not middle:
            return []
        up = permute(
            pieces[middle - 1],
            lambda g, z, y, c: (g, z + 1, y, c) if middle <= z + 1 < pairs else None,
        )
        down = permute(
            pieces[middle + 1],
            lambda g, z, y, c: (g, z - 1, y, c) if 0 <= z - 1 < middle else None,
        )
        return [up, down]

    near_shifts = [k for k in range(1, pairs) if k != middle]
    shifts = [0] + near_shifts + ([(middle,), middle] if middle else [])

    def line_slabs(own, pieces, far):
        return [own] + [pieces[k] for k in near_shifts] + far

    def all_pairs(array):
        return [array] + [line_shift(array, k) for k in range(1, pairs)]

    offsets = [(g, y) for g in range(groups) for y in range(2)]

    part = key_matrix.shape[0] // groups

    def own_part(matrix):
        return lax.dynamic_slice_in_dim(matrix, group * part, part, axis=0)

    slab = jnp.concatenate([own_part(key_matrix), own_part(value_matrix)], axis=1)
    slab_near = line_near(slab)

    index = [(group + g) % groups * 2 + (side + y) % 2 for g, y in offsets]
    sends = pack(vision, index[1:], core, groups, pairs, part, "pack_sends")
    received = [plane_shift(send, g, y) for send, (g, y) in zip(sends, offsets[1:])]
    vision = after(vision, *sends)
    near = pack(vision, index[:1], core, groups, pairs, part, "pack_near")
    far = pack(vision, index[:1], 1 - core, groups, pairs, part, "pack_far")

    rows_q = queries.shape[0]
    half_q = queries.shape[1] // 2
    heads = half_q // HEAD_SIZE
    queries = after(queries, far[0])
    q_own = lax.dynamic_slice_in_dim(queries, side * half_q, half_q, axis=1)
    q_send = lax.dynamic_slice_in_dim(queries, (1 - side) * half_q, half_q, axis=1)

    received = [after(piece, near[0], far[0]) for piece in received]
    near = [*near, *received]
    slab_far = line_far({k: after(s, near[0], far[0], q_own, q_send) for k, s in slab_near.items()})
    far = [*far] + [core_swap(piece) for piece in received]

    def scatter(pieces):
        return [plane_shift(piece, g, y) for piece, (g, y) in zip(pieces[1:], offsets[1:])]

    def sum_up(own, pieces):
        return functools.reduce(lambda a, b: a + b.astype(f32), pieces, own)

    slabs = line_slabs(slab, slab_near, slab_far)
    pieces = project(near, far, shifts, slabs, side, place, pairs)
    key_pieces, value_pieces = pieces[: len(offsets)], pieces[len(offsets) :]
    value_parts = scatter(value_pieces)
    key_parts = scatter(key_pieces)
    values = sum_up(value_pieces[0], value_parts).astype(bf16)
    all_values = all_pairs(values)
    key_parts = [after(k, all_values[1]) for k in key_parts]
    q_recv = plane_shift(after(q_send, all_values[1]), 0, 1)
    q_pair = jnp.where(
        side == 0,
        jnp.concatenate([q_own, q_recv], axis=0),
        jnp.concatenate([q_recv, q_own], axis=0),
    )
    q_heads = jnp.concatenate(
        [q_pair[:, h * HEAD_SIZE : (h + 1) * HEAD_SIZE] for h in range(heads)], axis=0
    )
    normed = norm(q_heads.astype(f32), query_norm_gain)
    keys = norm(sum_up(key_pieces[0], key_parts), key_norm_gain)
    all_keys = all_pairs(keys)
    weights, denominator = score(normed, all_keys, heads)
    attended = mix(weights, denominator, all_values, heads)
    passed = {0: plane_shift(attended, 0, 1)}
    arrived = {k: line_shift(attended, k) for k in range(1, pairs)}
    for k in near_shifts:
        passed[k] = plane_shift(after(arrived[k], passed[0]), 0, 1)
    totals = [
        own_output([attended, *(arrived[k] for k in near_shifts)], out_weight, side, "output_near")
    ]
    order = [0, *near_shifts]
    if middle:
        opposite = after(arrived[middle], totals[0], passed[near_shifts[0]])
        passed[middle] = plane_shift(opposite, 0, 1)
        totals.append(own_output([opposite], out_weight, side, "output_far"))
        order.append(middle)
    others = [passed[k] for k in range(pairs)]
    mine, send = other_output(others, out_weight, totals, order, 1 - side, place, core)
    mine = mine + core_swap(send).astype(f32)
    return (residual.astype(f32) + jnp.tanh(attn_gate[0]) * mine).astype(bf16)


def solution(mesh):
    in_specs = (
        P(("groups", "seq"), "head"),
        P(("groups", "seq"), None),
        P("seq", "head"),
        P("seq", "head"),
        P("head", "seq"),
        P(("groups", "head"), "seq"),
        P(),
        P(),
        P(),
    )
    out_specs = P(("groups", "head"), "seq")
    sizes = tuple(mesh.shape[axis] for axis in AXES)
    return jax.shard_map(
        functools.partial(body, sizes),
        mesh=mesh,
        in_specs=in_specs,
        out_specs=out_specs,
        check_vma=False,
    )
```

```python
import functools

import jax
import jax.numpy as jnp
from jax import lax
from jax.experimental import pallas as pl
from jax.experimental.pallas import tpu as pltpu
from jax.sharding import PartitionSpec as P

HEAD_SIZE = 128
epsilon = 1e-05
AXES = ("groups", "seq", "head")
VMEM_BYTES = 20 * 1024 * 1024
f32, bf16 = jnp.float32, jnp.bfloat16


def pack_kernel(groups, pairs, part, count, index_ref, rows_ref, *outs):
    for g in range(groups):
        for y in range(2):
            starts = [((2 * z + y) * groups + g) * part for z in range(pairs)]
            for k, out in enumerate(outs):

                @pl.when(index_ref[k] == g * 2 + y)
                def _():
                    out[...] = jnp.concatenate(
                        [rows_ref[:, s : s + part] for s in starts], axis=1
                    )


def pack(vision, index, core, groups, pairs, part, name):
    rows, width = vision.shape
    half = rows // 2
    block = min(64, half)
    steps = half // block
    count = len(index)
    depth = pairs * part
    scalars = jnp.stack([*index, core]).astype(jnp.int32)
    return pl.pallas_call(
        functools.partial(pack_kernel, groups, pairs, part, count),
        grid_spec=pltpu.PrefetchScalarGridSpec(
            num_scalar_prefetch=1,
            grid=(steps,),
            in_specs=[pl.BlockSpec((block, width), lambda i, s: (s[count] * steps + i, 0))],
            out_specs=[pl.BlockSpec((block, depth), lambda i, s: (i, 0))] * count,
        ),
        out_shape=[jax.ShapeDtypeStruct((half, depth), vision.dtype)] * count,
        compiler_params=pltpu.CompilerParams(vmem_limit_bytes=VMEM_BYTES),
        name=name,
    )(scalars, vision)


def project_kernel(groups, pairs, shifts, scalars, *refs):
    count = groups * 2
    near, far, slabs = refs[:count], refs[count : 2 * count], refs[2 * count : -2 * count - 1]
    outs, placed = refs[-2 * count - 1 : -1], refs[-1]
    half = near[0].shape[0]
    side, place = scalars[0], scalars[1]
    for shift, slab in zip(shifts, slabs):
        if isinstance(shift, tuple):
            continue
        placed[lax.rem(place + pairs - shift, pairs)] = slab[...]
    for shift, slab in zip(shifts, slabs):
        if isinstance(shift, tuple):

            @pl.when(place >= pairs // 2)
            def _():
                placed[lax.rem(place + pairs - shift[0], pairs)] = slab[...]

    w = jnp.concatenate([placed[z] for z in range(pairs)], axis=0)
    for part, pieces in enumerate((near, far)):
        lhs = jnp.concatenate([ref[...] for ref in pieces], axis=0)
        result = jnp.dot(lhs, w, preferred_element_type=f32)
        columns = [result[:, n * HEAD_SIZE : (n + 1) * HEAD_SIZE] for n in range(4)]
        for matrix in range(2):
            first, second = columns[2 * matrix : 2 * matrix + 2]
            heads = jnp.where(side == 0, first, second), jnp.where(side == 0, second, first)
            for source in range(count):
                by_group, by_side = source // 2, source % 2
                for to in range(2):
                    out = outs[matrix * count + (-by_group) % groups * 2 + to]
                    start = (0 if by_side == to else 2 * half) + part * half
                    out[start : start + half, :] = heads[to][
                        source * half : (source + 1) * half, :
                    ].astype(out.dtype)


def project(near, far, shifts, slabs, side, place, pairs):
    count = len(near)
    half = near[0].shape[0]
    vmem = pl.BlockSpec(memory_space=pltpu.VMEM)
    return pl.pallas_call(
        functools.partial(project_kernel, count // 2, pairs, shifts),
        in_specs=[pl.BlockSpec(memory_space=pltpu.SMEM)] + [vmem] * (2 * count + len(slabs)),
        out_specs=[vmem] * (2 * count),
        out_shape=[
            jax.ShapeDtypeStruct((4 * half, HEAD_SIZE), bf16 if k > count else f32)
            for k in range(2 * count)
        ],
        scratch_shapes=[pltpu.VMEM((pairs,) + slabs[0].shape, bf16)],
        compiler_params=pltpu.CompilerParams(vmem_limit_bytes=VMEM_BYTES),
        name="project",
    )(jnp.stack([side, place]).astype(jnp.int32), *near, *far, *slabs)


def score_kernel(heads, q_ref, *refs):
    keys, weights_ref, denominator_ref = refs[:-2], refs[-2], refs[-1]
    block = keys[0].shape[0]
    text = q_ref.shape[0] // heads
    for h in range(heads):
        rows = slice(h * text, (h + 1) * text)
        scores = [
            lax.dot_general(
                q_ref[rows, :], k[...], (((1,), (1,)), ((), ())), preferred_element_type=f32
            )
            * HEAD_SIZE ** (-0.5)
            for k in keys
        ]
        top = functools.reduce(
            jnp.maximum, [jnp.max(s, axis=-1, keepdims=True) for s in scores]
        )
        total = jnp.zeros_like(top)
        for n, s in enumerate(scores):
            weights = jnp.exp(s - top)
            total = total + jnp.sum(weights, axis=-1, keepdims=True)
            weights_ref[rows, n * block : (n + 1) * block] = weights.astype(bf16)
        denominator_ref[rows, :] = jnp.broadcast_to(total, (text, HEAD_SIZE))


def score(normed, keys, heads):
    rows = normed.shape[0]
    return pl.pallas_call(
        functools.partial(score_kernel, heads),
        out_shape=[
            jax.ShapeDtypeStruct((rows, len(keys) * keys[0].shape[0]), bf16),
            jax.ShapeDtypeStruct((rows, HEAD_SIZE), f32),
        ],
        compiler_params=pltpu.CompilerParams(vmem_limit_bytes=VMEM_BYTES),
        name="score",
    )(normed, *keys)


def mix_kernel(weights_ref, denominator_ref, *refs):
    values, out_ref = refs[:-1], refs[-1]
    text = out_ref.shape[0]
    v = jnp.concatenate([ref[...] for ref in values], axis=0)
    numerator = jnp.dot(weights_ref[...], v, preferred_element_type=f32)
    attended = (numerator / denominator_ref[...]).astype(bf16)
    for h in range(out_ref.shape[1] // HEAD_SIZE):
        out_ref[:, h * HEAD_SIZE : (h + 1) * HEAD_SIZE] = attended[h * text : (h + 1) * text, :]


def mix(weights, denominator, values, heads):
    rows = weights.shape[0]
    return pl.pallas_call(
        mix_kernel,
        out_shape=jax.ShapeDtypeStruct((rows // heads, heads * HEAD_SIZE), bf16),
        compiler_params=pltpu.CompilerParams(vmem_limit_bytes=VMEM_BYTES),
        name="mix",
    )(weights, denominator, *values)


def own_kernel(scalars, *refs):
    pieces, weight, out = refs[:-2], refs[-2], refs[-1]
    depth = pieces[0].shape[1]
    rows = pl.ds(pl.multiple_of(scalars[0] * depth, depth), depth)
    lhs = jnp.concatenate([piece[...] for piece in pieces], axis=0)
    out[...] = jnp.dot(lhs, weight[rows, :], preferred_element_type=f32)


def own_output(pieces, out_weight, side, name):
    vmem = pl.BlockSpec(memory_space=pltpu.VMEM)
    rows = len(pieces) * pieces[0].shape[0]
    return pl.pallas_call(
        own_kernel,
        in_specs=[pl.BlockSpec(memory_space=pltpu.SMEM)] + [vmem] * (len(pieces) + 1),
        out_specs=vmem,
        out_shape=jax.ShapeDtypeStruct((rows, out_weight.shape[1]), f32),
        compiler_params=pltpu.CompilerParams(vmem_limit_bytes=VMEM_BYTES),
        name=name,
    )(jnp.stack([side]).astype(jnp.int32), *pieces, out_weight)


def other_kernel(shifts, scalars, *refs):
    pairs = len(shifts)
    pieces, weight, totals = refs[:pairs], refs[pairs], refs[pairs + 1 : -4]
    mine, send, placed, summed = refs[-4:]
    side, place, core = scalars[0], scalars[1], scalars[2]
    text, depth = pieces[0].shape
    for k, piece in enumerate(pieces):
        placed[lax.rem(place + pairs - k, pairs)] = piece[...]
    parts = [(ref, r) for ref in totals for r in range(0, ref.shape[0], text)]
    for k, (ref, r) in zip(shifts, parts):
        summed[lax.rem(place + pairs - k, pairs)] = ref[r : r + text, :]
    rows = pl.ds(pl.multiple_of(side * depth, depth), depth)
    half = pairs // 2
    for out, which in ((send, 1 - core), (mine, core)):
        base = which * half
        lhs = jnp.concatenate([placed[base + n] for n in range(half)], axis=0)
        own = jnp.concatenate([summed[base + n] for n in range(half)], axis=0)
        product = jnp.dot(lhs, weight[rows, :], preferred_element_type=f32)
        out[...] = (product + own).astype(out.dtype)


def other_output(pieces, out_weight, totals, shifts, side, place, core):
    vmem = pl.BlockSpec(memory_space=pltpu.VMEM)
    pairs = len(pieces)
    text, depth = pieces[0].shape
    width = out_weight.shape[1]
    rows = pairs * text // 2
    return pl.pallas_call(
        functools.partial(other_kernel, shifts),
        in_specs=[pl.BlockSpec(memory_space=pltpu.SMEM)] + [vmem] * (pairs + 1 + len(totals)),
        out_specs=[vmem] * 2,
        out_shape=[
            jax.ShapeDtypeStruct((rows, width), f32),
            jax.ShapeDtypeStruct((rows, width), bf16),
        ],
        scratch_shapes=[
            pltpu.VMEM((pairs, text, depth), bf16),
            pltpu.VMEM((pairs, text, width), f32),
        ],
        compiler_params=pltpu.CompilerParams(vmem_limit_bytes=VMEM_BYTES),
        name="output_other",
    )(jnp.stack([side, place, core]).astype(jnp.int32), *pieces, out_weight, *totals)


def after(array, *others):
    return lax.optimization_barrier((array, others))[0]


def norm(array, gain):
    mean = jnp.mean(array * array, axis=-1, keepdims=True)
    return (array * lax.rsqrt(mean + epsilon) * gain).astype(bf16)


def body(
    sizes,
    queries,
    vision,
    key_matrix,
    value_matrix,
    out_weight,
    residual,
    query_norm_gain,
    key_norm_gain,
    attn_gate,
):
    groups, seq, cores = sizes
    pairs = seq // 2
    group = lax.axis_index("groups")
    side = lax.axis_index("seq") % 2
    place = lax.axis_index("seq") // 2
    core = lax.axis_index("head")

    def permute(array, target):
        perm = []
        for g in range(groups):
            for z in range(pairs):
                for y in range(2):
                    for c in range(cores):
                        to = target(g, z, y, c)
                        if to is not None:
                            tg, tz, ty, tc = to
                            perm.append(
                                (
                                    (g * seq + z * 2 + y) * cores + c,
                                    (tg % groups * seq + tz % pairs * 2 + ty % 2) * cores
                                    + tc % cores,
                                )
                            )
        return lax.ppermute(array, AXES, perm)

    def plane_shift(array, by_group, by_side):
        return permute(array, lambda g, z, y, c: (g + by_group, z, y + by_side, c))

    def line_shift(array, by):
        return permute(array, lambda g, z, y, c: (g, z + by, y, c))

    def core_swap(array):
        return permute(array, lambda g, z, y, c: (g, z, y, c + 1))

    middle = pairs // 2 if pairs % 2 == 0 and pairs > 2 else 0

    def line_near(array):
        return {k: line_shift(array, k) for k in range(1, pairs) if k != middle}

    def line_far(pieces):
        if not middle:
            return []
        up = permute(
            pieces[middle - 1],
            lambda g, z, y, c: (g, z + 1, y, c) if middle <= z + 1 < pairs else None,
        )
        down = permute(
            pieces[middle + 1],
            lambda g, z, y, c: (g, z - 1, y, c) if 0 <= z - 1 < middle else None,
        )
        return [up, down]

    near_shifts = [k for k in range(1, pairs) if k != middle]
    shifts = [0] + near_shifts + ([middle, (middle,)] if middle else [])

    def line_slabs(own, pieces, far):
        return [own] + [pieces[k] for k in near_shifts] + far[::-1]

    def all_pairs(array):
        return [array] + [line_shift(array, k) for k in range(1, pairs)]

    offsets = [(g, y) for g in range(groups) for y in range(2)]

    part = key_matrix.shape[0] // groups

    def own_part(matrix):
        return lax.dynamic_slice_in_dim(matrix, group * part, part, axis=0)

    slab = jnp.concatenate([own_part(key_matrix), own_part(value_matrix)], axis=1)
    slab_near = line_near(slab)

    index = [(group + g) % groups * 2 + (side + y) % 2 for g, y in offsets]
    sends = pack(vision, index[1:], core, groups, pairs, part, "pack_sends")
    received = [plane_shift(send, g, y) for send, (g, y) in zip(sends, offsets[1:])]
    vision = after(vision, *sends)
    near = pack(vision, index[:1], core, groups, pairs, part, "pack_near")
    far = pack(vision, index[:1], 1 - core, groups, pairs, part, "pack_far")

    rows_q = queries.shape[0]
    half_q = queries.shape[1] // 2
    heads = half_q // HEAD_SIZE
    queries = after(queries, far[0])
    q_own = lax.dynamic_slice_in_dim(queries, side * half_q, half_q, axis=1)
    q_send = lax.dynamic_slice_in_dim(queries, (1 - side) * half_q, half_q, axis=1)

    received = [after(piece, near[0], far[0]) for piece in received]
    near = [*near, *received]
    slab_far = line_far({k: after(s, near[0], far[0]) for k, s in slab_near.items()})
    far = [*far] + [core_swap(piece) for piece in received]

    def scatter(pieces):
        return [plane_shift(piece, g, y) for piece, (g, y) in zip(pieces[1:], offsets[1:])]

    def sum_up(own, pieces):
        return functools.reduce(lambda a, b: a + b.astype(f32), pieces, own)

    slabs = line_slabs(slab, slab_near, slab_far)
    pieces = project(near, far, shifts, slabs, side, place, pairs)
    key_pieces, value_pieces = pieces[: len(offsets)], pieces[len(offsets) :]
    value_parts = scatter(value_pieces)
    key_parts = scatter(key_pieces)
    values = sum_up(value_pieces[0], value_parts).astype(bf16)
    all_values = all_pairs(values)
    key_parts = [after(k, all_values[1]) for k in key_parts]
    q_recv = plane_shift(after(q_send, all_values[1]), 0, 1)
    q_pair = jnp.where(
        side == 0,
        jnp.concatenate([q_own, q_recv], axis=0),
        jnp.concatenate([q_recv, q_own], axis=0),
    )
    q_heads = jnp.concatenate(
        [q_pair[:, h * HEAD_SIZE : (h + 1) * HEAD_SIZE] for h in range(heads)], axis=0
    )
    normed = norm(q_heads.astype(f32), query_norm_gain)
    keys = norm(sum_up(key_pieces[0], key_parts), key_norm_gain)
    all_keys = all_pairs(keys)
    weights, denominator = score(normed, all_keys, heads)
    attended = mix(weights, denominator, all_values, heads)
    passed = {0: plane_shift(attended, 0, 1)}
    arrived = {k: line_shift(attended, k) for k in range(1, pairs)}
    for k in near_shifts:
        passed[k] = plane_shift(after(arrived[k], passed[0]), 0, 1)
    totals = [
        own_output([attended, *(arrived[k] for k in near_shifts)], out_weight, side, "output_near")
    ]
    order = [0, *near_shifts]
    if middle:
        opposite = after(arrived[middle], totals[0], passed[near_shifts[0]])
        passed[middle] = plane_shift(opposite, 0, 1)
        totals.append(own_output([opposite], out_weight, side, "output_far"))
        order.append(middle)
    others = [passed[k] for k in range(pairs)]
    mine, send = other_output(others, out_weight, totals, order, 1 - side, place, core)
    mine = mine + core_swap(send).astype(f32)
    return (residual.astype(f32) + jnp.tanh(attn_gate[0]) * mine).astype(bf16)


def solution(mesh):
    in_specs = (
        P(("groups", "seq"), "head"),
        P(("groups", "seq"), None),
        P("seq", "head"),
        P("seq", "head"),
        P("head", "seq"),
        P(("groups", "head"), "seq"),
        P(),
        P(),
        P(),
    )
    out_specs = P(("groups", "head"), "seq")
    sizes = tuple(mesh.shape[axis] for axis in AXES)
    return jax.shard_map(
        functools.partial(body, sizes),
        mesh=mesh,
        in_specs=in_specs,
        out_specs=out_specs,
        check_vma=False,
    )
```
